32 devices in a mesh: dp: 8 (over y, x, core), seq: 4 (over z).
Axes of the slice: x: 2, y: 2, z: 4, core: 2. Of those that a mesh axis runs over, the one named last changes fastest.
Arguments:
- hidden: bfloat16 [32, 272, 1152], P(('dp', 'seq')), may hold values from -6 to 6
- skipped: bfloat16 [32, 272, 1152], P(('dp', 'seq')), may hold values from -6 to 6
- row_mask: int32 [32, 272], P('dp'), may hold values from 0 to 1, as said below
- cotangent: bfloat16 [32, 272, 1152], P(('dp', 'seq')), may hold values from -6 to 6
- merge_weight: bfloat16 [2304, 1152], P('seq'), may hold values from -0.125 to 0.125
- merge_bias: bfloat16 [1152], replicated, may hold values from -1.75 to 1.75
- first_gain: bfloat16 [1152], replicated, may hold values from 0.099609375 to 1.8984375
- first_shift: bfloat16 [1152], replicated, may hold values from -1.75 to 1.75
- triple_weight: bfloat16 [1152, 3456], P('seq'), may hold values from -0.1875 to 0.1875
- output_weight: bfloat16 [1152, 1152], P('seq'), may hold values from -1 to 1
- output_bias: bfloat16 [1152], replicated, may hold values from -1.75 to 1.75
- second_gain: bfloat16 [1152], replicated, may hold values from 0.099609375 to 1.8984375
- second_shift: bfloat16 [1152], replicated, may hold values from -1.75 to 1.75
- expand_weight: bfloat16 [1152, 4608], P('seq'), may hold values from -0.1875 to 0.1875
- expand_bias: bfloat16 [4608], replicated, may hold values from -1.75 to 1.75
- reduce_weight: bfloat16 [4608, 1152], P('seq'), may hold values from -0.09375 to 0.09375
- reduce_bias: bfloat16 [1152], replicated, may hold values from -1.75 to 1.75
Outputs:
- result: bfloat16 [32, 272, 1152], P(('dp', 'seq'))
- hidden_grad: bfloat16 [32, 272, 1152], P(('dp', 'seq'))
- skipped_grad: bfloat16 [32, 272, 1152], P(('dp', 'seq'))
- merge_weight_grad: float32 [2304, 1152], P('seq')
- merge_bias_grad: float32 [1152], replicated
- first_gain_grad: float32 [1152], replicated
- first_shift_grad: float32 [1152], replicated
- triple_weight_grad: float32 [1152, 3456], P('seq')
- output_weight_grad: float32 [1152, 1152], P('seq')
- output_bias_grad: float32 [1152], replicated
- second_gain_grad: float32 [1152], replicated
- second_shift_grad: float32 [1152], replicated
- expand_weight_grad: float32 [1152, 4608], P('seq')
- expand_bias_grad: float32 [4608], replicated
- reduce_weight_grad: float32 [4608, 1152], P('seq')
- reduce_bias_grad: float32 [1152], replicated
The draws below stay inside these ranges and needn't reach their ends.
Inputs may be any that keep to these rules, and one draw needn't show every extreme that they name: `row_mask`: in each image exactly 258 of the 272 rows are 1; which ones is drawn from the seed.
All inputs are finite; a program needn't handle non-finite values.
Results may differ from the reference program's by a relative error of at most 0.02.
Values may be sent and summed in bfloat16 or wider, within the bound.
A program may use at most 256 MiB of HBM per device.

```python
import jax
import jax.numpy as jnp
from jax import lax

D = 1152
HEADS = 16
FF = 4608
L = 272
VALID = 258
IMAGES = 32


def draw_row_mask(key, part):
    key = jax.random.fold_in(key, 7)
    keys = jax.random.split(key, IMAGES)
    orders = jax.vmap(lambda single: jax.random.permutation(single, L))(keys)
    return (orders < VALID).astype(jnp.int32)


def block_scale(rng, extent, cuts, least, largest):
    level = 1.0
    for dim, shards_of in cuts:
        heights = jax.random.uniform(jax.random.fold_in(jax.random.fold_in(rng, 6), dim), (shards_of,), jnp.float32, least / len(cuts), largest / len(cuts))
        level = level * jnp.repeat(jnp.exp(heights), extent[dim] // shards_of).reshape((-1,) + (1,) * (len(extent) - 1 - dim))
    return level


def gaussian(stream_key, dims, scale, limit, pieces=(), held_as=jnp.bfloat16):
    entries = scale * jax.random.normal(stream_key, dims, jnp.float32)
    if pieces:
        entries = entries * block_scale(stream_key, dims, pieces, -0.22, 0.18)
    return jnp.clip(entries, -limit, limit).astype(held_as)


def setup_inputs(seed: int = 0) -> dict:
    seeds = jax.random.split(jax.random.key(seed), 18)
    hidden = gaussian(seeds[0], (IMAGES, L, D), 1.0, 6.0, ((0, 32),))
    skipped = gaussian(seeds[1], (IMAGES, L, D), 1.0, 6.0, ((0, 32),))
    row_mask = draw_row_mask(jax.random.fold_in(seeds[17], 71), 0)
    cotangent = gaussian(seeds[3], (IMAGES, L, D), 1.0, 6.0, ((0, 32),))
    merge_weight = gaussian(seeds[4], (2 * D, D), (2 * D) ** -0.5, 0.125, ((0, 4),))
    merge_bias = gaussian(seeds[5], (D,), 0.3, 1.75)
    first_gain = jnp.clip(1.0 + 0.18 * jax.random.normal(seeds[6], (D,), jnp.float32), 0.099609375, 1.8984375).astype(jnp.bfloat16)
    first_shift = gaussian(seeds[7], (D,), 0.3, 1.75)
    triple_weight = gaussian(seeds[8], (D, 3 * D), D ** -0.5, 0.1875, ((0, 4),))
    output_weight = gaussian(seeds[9], (D, D), (D // 32) ** -0.5, 1.0, ((0, 4),))
    output_bias = gaussian(seeds[10], (D,), 0.3, 1.75)
    second_gain = jnp.clip(1.0 + 0.18 * jax.random.normal(seeds[11], (D,), jnp.float32), 0.099609375, 1.8984375).astype(jnp.bfloat16)
    second_shift = gaussian(seeds[12], (D,), 0.3, 1.75)
    expand_weight = gaussian(seeds[13], (D, FF), D ** -0.5, 0.1875, ((0, 4),))
    expand_bias = gaussian(seeds[14], (FF,), 0.3, 1.75)
    reduce_weight = gaussian(seeds[15], (FF, D), FF ** -0.5, 0.09375, ((0, 4),))
    reduce_bias = gaussian(seeds[16], (D,), 0.3, 1.75)
    return {"hidden": hidden, "skipped": skipped, "row_mask": row_mask, "cotangent": cotangent, "merge_weight": merge_weight, "merge_bias": merge_bias, "first_gain": first_gain, "first_shift": first_shift, "triple_weight": triple_weight, "output_weight": output_weight, "output_bias": output_bias, "second_gain": second_gain, "second_shift": second_shift, "expand_weight": expand_weight, "expand_bias": expand_bias, "reduce_weight": reduce_weight, "reduce_bias": reduce_bias}


@jax.custom_vjp
def low(v):
    return lax.optimization_barrier(v.astype(jnp.bfloat16)).astype(jnp.float32)

@jax.custom_vjp
def low_back(v):
    return v

def low_keep(v):
    return (low(v), None)

def low_pass(kept, grad):
    return (grad,)

def back_keep(v):
    return (v, None)

def back_low(kept, grad):
    return (low(grad),)
low.defvjp(low_keep, low_pass)
low_back.defvjp(back_keep, back_low)
EPS = 1e-05
NEGATIVE = -1e+30
HIGH = lax.Precision.HIGHEST

def layer_norm(values, gain, shift):
    center = lax.optimization_barrier(jnp.mean(values, axis=-1, keepdims=True))
    centred = values - center
    spread = lax.optimization_barrier(jnp.mean(centred * centred, axis=-1, keepdims=True))
    return centred * lax.rsqrt(spread + EPS) * gain + shift

def forward(params, hidden, skipped, valid):
    merge_w, merge_b, gain_a, shift_a, triple_w, out_w, out_b, gain_b, shift_b, expand_w, expand_b, reduce_w, reduce_b = params
    count, length, width = hidden.shape
    head_size = width // HEADS
    joined = jnp.concatenate([hidden, skipped], axis=-1)
    merged = low_back(jnp.einsum('bld,de->ble', joined, merge_w, precision=HIGH) + merge_b)
    normed = low(layer_norm(merged, gain_a, shift_a))
    triple = low_back(low(jnp.einsum('bld,de->ble', normed, triple_w, precision=HIGH)))
    queries = triple[..., :width].reshape(count, length, HEADS, head_size)
    key_heads = triple[..., width:2 * width].reshape(count, length, HEADS, head_size)
    value_heads = triple[..., 2 * width:].reshape(count, length, HEADS, head_size)
    scores = jnp.einsum('bqhd,bkhd->bhqk', queries, key_heads, precision=HIGH) * head_size ** (-0.5)
    scores = low_back(scores)
    scores = jnp.where(valid[:, None, None, :] > 0, scores, NEGATIVE)
    log_total = jax.scipy.special.logsumexp(scores, axis=-1, keepdims=True)
    probs = low(jnp.exp(scores - log_total))
    attended = jnp.einsum('bhqk,bkhd->bqhd', probs, value_heads, precision=HIGH)
    attended = low_back(low(attended)).reshape(count, length, width)
    branch = low_back(jnp.einsum('bld,de->ble', attended, out_w, precision=HIGH) + out_b)
    middle = merged + branch
    normed_two = low(layer_norm(middle, gain_b, shift_b))
    expanded = low_back(jnp.einsum('bld,de->ble', normed_two, expand_w, precision=HIGH) + expand_b)
    activated = low(jax.nn.gelu(expanded, approximate=False))
    return middle + jnp.einsum('bld,de->ble', activated, reduce_w, precision=HIGH) + reduce_b

def reference(hidden, skipped, row_mask, cotangent, merge_weight, merge_bias, first_gain, first_shift, triple_weight, output_weight, output_bias, second_gain, second_shift, expand_weight, expand_bias, reduce_weight, reduce_bias):
    params = tuple((weight.astype(jnp.float32) for weight in (merge_weight, merge_bias, first_gain, first_shift, triple_weight, output_weight, output_bias, second_gain, second_shift, expand_weight, expand_bias, reduce_weight, reduce_bias)))
    images = hidden.shape[0]
    group = max((candidate for candidate in range(1, images + 1) if images % candidate == 0 and candidate * L <= 4096))
    blocks = images // group

    def regroup(array):
        return array.reshape((blocks, group) + array.shape[1:])

    def step(totals, block):
        first_in, second_in, valid, upstream = block

        def apply(weights, first_part, second_part):
            return forward(weights, first_part, second_part, valid)
        output, backward = jax.vjp(apply, params, first_in.astype(jnp.float32), second_in.astype(jnp.float32))
        weight_grads, first_grad, second_grad = backward(upstream.astype(jnp.float32))
        totals = jax.tree.map(lambda total, extra: total + extra, totals, weight_grads)
        return (totals, (output.astype(jnp.bfloat16), first_grad.astype(jnp.bfloat16), second_grad.astype(jnp.bfloat16)))
    zeros = jax.tree.map(jnp.zeros_like, params)
    totals, (output, first_grad, second_grad) = lax.scan(step, zeros, (regroup(hidden), regroup(skipped), regroup(row_mask), regroup(cotangent)))
    shape = hidden.shape
    return (output.reshape(shape), first_grad.reshape(shape), second_grad.reshape(shape), totals[0], totals[1], totals[2], totals[3], totals[4], totals[5], totals[6], totals[7], totals[8], totals[9], totals[10], totals[11], totals[12])
```

```python
import functools

import jax
import jax.numpy as jnp
from jax import lax
from jax.experimental import pallas as pl
from jax.experimental.pallas import tpu as pltpu
from jax.sharding import PartitionSpec as P

MESH = pl.DeviceIdType.MESH
HEADS = 16
EPS = 1e-05
NEGATIVE = -1e30
NB = 14
NP, SUB = 7, 3
Q = NP * SUB
AHEAD = 2
RING = 8
SLOTS = 3
VR = 16
READY = 5
LEAD = READY + 11
f32, bf16 = jnp.float32, jnp.bfloat16


def block_slices(refs):
    merge, triple, output, expand, reduce = refs
    R, C = output.shape
    out = []
    for j in range(merge.shape[0] // R): out.append(merge.at[pl.ds(j * R, R), :])
    for j in range(triple.shape[1] // C): out.append(triple.at[:, pl.ds(j * C, C)])
    out.append(output.at[:, :])
    for j in range(expand.shape[1] // C): out.append(expand.at[:, pl.ds(j * C, C)])
    for j in range(reduce.shape[0] // R): out.append(reduce.at[pl.ds(j * R, R), :])
    return out


def nn(a, b):
    return jnp.dot(a, b, preferred_element_type=f32)


def nt(a, b):
    return lax.dot_general(a, b, (((1,), (1,)), ((), ())), preferred_element_type=f32)


def tn(a, b):
    return lax.dot_general(a, b, (((0,), (0,)), ((), ())), preferred_element_type=f32)


HID, SKP, COT, NORMED, ATT, TWO, ACT, TRI, BR, TG, GR, EXP, PX, ATTG, OUT, PLACES = 0, 2, 4, 6, 8, 10, 12, 20, 23, 25, 31, 33, 37, 39, 40, 42
NN, NT, EXTRA, CAST, FETCH, NORM, NORM_BACK, GELU, GELU_BACK, ATTEND, ATTEND_BACK, ROWS, FULL = range(1, 14)


def op(mode, a=0, w=0, acc=0, e=0, wait=1, pre=None, post=None):
    pre, post = (0 if v is None else v + 1 for v in (pre, post))
    return mode + 16 * (a + 64 * (w + 32 * (acc + 2 * (e + 2 * (wait + 2 * (pre + 32 * post))))))


def plan():
    B = READY
    ops = [(0, op(EXTRA, 0)), (1, op(EXTRA, 1))]
    ops += [(B + 1, o) for o in (op(FETCH, 0), op(NN, HID, 0, pre=1), op(NN, SKP, 1, acc=1), op(NORM, 0))]
    for j in range(3):
        ops += [(B + 2 + j, o) for o in (op(NN, NORMED, 2 + j, pre=2 + j), op(CAST, TRI + j))]
    ops += [(B + 4, op(ATTEND, 0)), (B + 4, op(ATTEND, 1)), (B + 5, op(ATTEND, 2)), (B + 5, op(ATTEND, 3)), (B + 5, op(EXTRA, 2))]
    ops += [(B + 5, op(NN, ATT, 5, pre=5)), (B + 5, op(NORM, 1))]
    for i in range(4):
        ops += [(B + 6 + i, op(NN, TWO, 6 + i, pre=6 + i)), (B + 6 + i, op(GELU, i))]
    ops += [(B + 9, op(EXTRA, 3)), (B + 9, op(ROWS, 0)), (B + 10, op(ROWS, 1))]
    ops += [(B + 13, op(FETCH, 10 + i)) for i in range(3)]
    for i in range(4):
        ops += [(B + 13 + i // 2, o) for o in (
            op(NN, ACT + 2 * i, 10 + i, acc=int(i > 0)), op(NT, COT, 10 + i, e=1, wait=0, post=13 + i), op(GELU_BACK, i))]
    ops += [(B + 14, op(EXTRA, 4)), (B + 15, op(EXTRA, 5)), (B + 15, op(FULL, 0)), (B + 16, op(FULL, 1))]
    for i in range(4):
        ops += [(B + 16 + (i > 0), op(NT, EXP + i, 14 + i, acc=int(i > 0), post=17 + i))]
    ops += [(B + 17, op(NORM_BACK, 1)), (B + 18, op(NT, BR, 18, post=21)), (B + 18, op(CAST, ATTG))]
    ops += [(B + 18 + g // 2, op(ATTEND_BACK, g)) for g in range(4)]
    ops += [(B + 19, op(EXTRA, 6)), (B + 20, op(EXTRA, 7)), (B + 20, op(FULL, 2)), (B + 21, op(FULL, 3))]
    for j in range(3):
        ops += [(B + 22, op(NT, TG + 2 * j, 19 + j, acc=int(j > 0), post=22 + j if j < 2 else None))]
    ops += [(B + 23, op(NORM_BACK, 0)), (B + 24, op(EXTRA, 8)), (B + 24, op(ROWS, 2)), (B + 25, op(EXTRA, 9))]
    for i in range(2):
        ops += [(B + 25, op(NT, GR, 22 + i)), (B + 25, op(CAST, OUT + i))]
    ops += [(B + 25, op(EXTRA, 10))]
    ops += [(B + t, op(EXTRA, 11 + i)) for i, t in enumerate((26, 27, 28, 29, 32))]
    return ops


OPS = plan()
STARTS = [sum(t < tick for t, _ in OPS) for tick in range(LEAD + AHEAD + Q + 10)]
UNITS = [2, 6] + [4 * j for j in range(2, 10)] + [1 + 4 * s for s in range(4)] + [4 * j for j in (6, 7, 8, 9, 5, 2, 3, 4)] + [2, 6]


def lookup(values, i):
    total = jnp.int32(values[0])
    for k in range(1, len(values)):
        if values[k] != values[k - 1]:
            total = total + jnp.where(i >= k, values[k] - values[k - 1], 0)
    return total


def block_kernel(hid, skp, cot_in, mask_in, vec_in, wm, wt, wo, we, wr,
                 res, hgrad, sgrad, F, WV, G, D,
                 W, X, PR, XH, MID, E, INV, MASK, VEC, DB,
                 K, R1, R2, R3, O, VB,
                 loc, loc2, zs, zr, xs, xr, ys, yr, cs, cr, fsem, insem, es, er, dsem, osem,
                 ld, s1, r1, s2, r2, s3, r3, st, sf, rf, sc, rcv, vl, vs, vr, *, nz):
    dp = lax.axis_index("dp"); z = lax.axis_index("seq")
    c = dp % 2; x = (dp // 2) % 2; y = dp // 4
    xn = dp + 2 - 4 * x; yn = dp + 4 - 8 * y; cn = dp + 1 - 2 * c; co = 1 - c
    L, C = X.shape[1:]
    R = G.shape[2]
    scale = (C // HEADS) ** -0.5
    bar = pltpu.get_barrier_semaphore()
    for tgt in (xn, yn, cn):
        pl.semaphore_signal(bar, inc=1, device_id=(tgt, z), device_id_type=MESH)
    for d in range(1, nz):
        pl.semaphore_signal(bar, inc=1, device_id=(dp, (z + d) % nz), device_id_type=MESH)

    def rc(src, dst, ss, rs, dev):
        return pltpu.make_async_remote_copy(src_ref=src, dst_ref=dst, send_sem=ss, recv_sem=rs, device_id=dev, device_id_type=MESH)

    blocks = block_slices((wm, wt, wo, we, wr))
    room = SLOTS * 4
    def stage(j): return W.at[(j % room) // 4, j % 4]
    def load_in(j): return pltpu.make_async_copy(blocks[j], stage(j), loc.at[j])
    def load_out(j, slot): return pltpu.make_async_copy(slot, G.at[z, j], loc2.at[j])
    for j in range(min(room, NB)): load_in(j).start()
    inputs = [pltpu.make_async_copy(a, b, insem.at[i]) for i, (a, b) in enumerate(
        ((hid, X.at[HID]), (skp, X.at[SKP]), (cot_in, X.at[COT]), (mask_in, MASK), (vec_in, VEC)))]
    for cp in inputs: cp.start()
    for j in range(min(room, NB)):
        load_in(j).wait()
        load_out(j, stage(j)).start()
    for j in range(AHEAD + 2): load_out(j, stage(j)).wait()
    for j in range(room, NB):
        load_in(j).start()
    pl.semaphore_wait(bar, nz + 2)

    half = R // 2; third = half // 3
    base = half * c
    zp = ((x + y) % 2) * (2 - x)
    yp = 1 + y
    def reg(s, b, start, n):
        return G.at[s, b, pl.ds(pl.multiple_of(start, 16), n), :]
    def same(region, ss, rs, dev): return rc(region, region, ss, rs, dev)
    def zcopy(b, d, k):
        s = z - k if d == 0 else z + k
        return same(reg(s, b, base + third * zp, third), zs.at[b, d, k], zr.at[b, d, k], (dp, z + 1 if d == 0 else z - 1))
    def zsend_ok(d, k):
        return (z >= k) & (z < nz - 1) if d == 0 else (z + k <= nz - 1) & (z > 0)
    def zrecv_ok(d, k):
        return z >= k + 1 if d == 0 else z + 1 + k <= nz - 1
    def shard_in(d, k):
        return z - 1 - k if d == 0 else z + 1 + k
    def xcopy(b, s): return same(reg(s, b, base + third * zp, third), xs.at[b, s], xr.at[b, s], (xn, z))
    def ycopy(b, s): return same(reg(s, b, base + third * yp, third), ys.at[b, s], yr.at[b, s], (yn, z))
    def ccopy(b, s): return same(reg(s, b, base, half), cs.at[b, s], cr.at[b, s], (cn, z))
    def own(b):
        for d in (0, 1):
            @pl.when(zsend_ok(d, 0))
            def _(): zcopy(b, d, 0).start()
    def zarr(b, d, k):
        zcopy(b, d, k).wait_recv()
        if k + 1 < nz - 1:
            @pl.when(zsend_ok(d, k + 1))
            def _(): zcopy(b, d, k + 1).start()
        s = shard_in(d, k)
        xcopy(b, s).start()
        @pl.when((x + y) % 2 == 1)
        def _(): ycopy(b, s).start()
    def xarr(b, d, k):
        s = shard_in(d, k)
        xcopy(b, s).wait_recv()
        @pl.when((x + y) % 2 == 0)
        def _(): ycopy(b, s).start()
    def yarr(b, d, k):
        s = shard_in(d, k)
        ycopy(b, s).wait_recv()
        ccopy(b, s).start()
    def fin(b, d, k):
        s = shard_in(d, k)
        ccopy(b, s).wait()
        xcopy(b, s).wait_send()
        ycopy(b, s).wait_send()
    for j in range(AHEAD): own(j)
    def gather_tick(t):
        @pl.when(t < NB - AHEAD)
        def _():
            own(t + AHEAD)
        for off, fn in ((0, zarr), (1, xarr), (2, yarr), (3, fin)):
            for k in range(nz - 1):
                b = t - off - k
                @pl.when((b >= 0) & (b < NB))
                def _():
                    for d in (0, 1):
                        @pl.when(zrecv_ok(d, k))
                        def _(): fn(b, d, k)
                        if off == 3:
                            @pl.when(zsend_ok(d, k))
                            def _(): zcopy(b, d, k).wait_send()

    T = K.shape[2]
    def ring(q): return q % RING
    def typ(q, s): return (q + s) % 2
    def keep(q, s): return x + typ(q, s) * (y - x)
    def near(q, s): return xn + typ(q, s) * (yn - xn)
    def far(q, s): return yn + typ(q, s) * (xn - yn)
    def piece(q, h):
        return NP - 1 - q // SUB, pl.ds(pl.multiple_of(half * h + T * (q % SUB), 16), T)
    def load(q, s):
        p, rows = piece(q, keep(q, s))
        return pltpu.make_async_copy(D.at[s, p, rows], K.at[ring(q), s], ld.at[s, q])
    def first(q, s):
        p, rows = piece(q, 1 - keep(q, s))
        return rc(D.at[s, p, rows], R1.at[ring(q), s], s1.at[s, q], r1.at[s, q], (near(q, s), z))
    def up(q, s):
        return rc(K.at[ring(q), s], R2.at[ring(q), s], s2.at[s, q], r2.at[s, q], (dp, z + 1))
    def down(q, s):
        away = jnp.minimum(z - 1 - s, 1)
        slot = nz + away * (s - nz)
        return rc(K.at[ring(q), s], R2.at[ring(q), slot], s2.at[s, q], r2.at[slot, q], (dp, z - 1))
    def got(slot, q):
        return rc(K.at[ring(q), 0], R2.at[ring(q), slot], s2.at[0, q], r2.at[slot, q], (dp, z))
    def last(q):
        return rc(K.at[ring(q), z], R3.at[ring(q)], s3.at[q], r3.at[q], (far(q, z), z))
    def frow(q, h, cc):
        p, rows = piece(q, h)
        return F.at[2 * p + cc, rows]
    def keepf(q): return pltpu.make_async_copy(O.at[ring(q)], frow(q, keep(q, z), c), st.at[q])
    def spread(q): return rc(O.at[ring(q)], frow(q, keep(q, z), c), sf.at[q], rf.at[q], (near(q, z), z))
    def spread_in(q):
        r = frow(q, 1 - keep(q, z), c)
        return rc(r, r, sf.at[q], rf.at[q], (near(q, z), z))
    def cross(q): return rc(O.at[ring(q)], frow(q, keep(q, z), c), sc.at[0, q], rcv.at[0, q], (cn, z))
    def cross2(q):
        r = frow(q, 1 - keep(q, z), c)
        return rc(r, r, sc.at[1, q], rcv.at[1, q], (cn, z))
    def add(a, b): return (a.astype(f32) + b.astype(f32)).astype(bf16)
    def issue(q):
        for s in range(nz):
            first(q, s).start(); load(q, s).start()
    def start(q):
        for s in range(nz):
            load(q, s).wait(); first(q, s).wait_recv()
            K[ring(q), s] = add(K[ring(q), s], R1[ring(q), s])
            if s > 0:
                @pl.when(z == 0)
                def _(): up(q, s).start()
            if s < nz - 1:
                @pl.when(z == nz - 1)
                def _(): down(q, s).start()
    def hop(q, k):
        for s in range(nz):
            if s > k:
                @pl.when(z == k)
                def _():
                    got(s, q).wait_recv()
                    K[ring(q), s] = add(K[ring(q), s], R2[ring(q), s])
                    up(q, s).start()
            if s < nz - 1 - k:
                @pl.when(z == nz - 1 - k)
                def _():
                    got(s, q).wait_recv()
                    K[ring(q), s] = add(K[ring(q), s], R2[ring(q), s])
                    down(q, s).start()
    def arrive(q):
        @pl.when(z > 0)
        def _():
            got(z, q).wait_recv()
            K[ring(q), z] = add(K[ring(q), z], R2[ring(q), z])
        @pl.when(z < nz - 1)
        def _():
            got(nz, q).wait_recv()
            K[ring(q), z] = add(K[ring(q), z], R2[ring(q), nz])
        last(q).start()
    def final(q):
        last(q).wait_recv()
        O[ring(q)] = add(K[ring(q), z], R3[ring(q)])
        keepf(q).start(); spread(q).start(); cross(q).start()
    def relay(q):
        spread_in(q).wait_recv()
        cross2(q).start()
        for s in range(nz):
            first(q, s).wait_send()
            if s > 0:
                @pl.when(z < s)
                def _(): up(q, s).wait_send()
            if s < nz - 1:
                @pl.when(z > s)
                def _(): down(q, s).wait_send()
        last(q).wait_send()
    def drain(q):
        keepf(q).wait(); spread(q).wait_send()
        cross(q).wait_send(); cross(q).wait_recv(); cross2(q).wait_send(); cross2(q).wait_recv()
    steps = [(0, start)] + [(k, functools.partial(hop, k=k)) for k in range(1, nz - 1)] + [
        (nz - 1, arrive), (nz, final), (nz + 1, relay), (nz + 3, drain)]
    def sum_tick(t):
        @pl.when((t >= 0) & (t < Q))
        def _(): issue(t)
        for off, fn in steps:
            q = t - AHEAD - off
            @pl.when((q >= 0) & (q < Q))
            def _(): fn(q)

    devs = ((cn, z), (xn, z), (yn, z))
    def swap(i): return rc(VB.at[2 * i], VB.at[2 * i + 1], vs.at[i], vr.at[i], devs[i])
    def vstep(i):
        if i > 0:
            swap(i - 1).wait()
            VB[2 * i] = VB[2 * i - 2] + VB[2 * i - 1]
        if i < 3:
            swap(i).start()
    def line(d):
        return rc(VB.at[6], VB.at[6 + d], vs.at[2 + d], vr.at[2 + d], (dp, (z + d) % nz))
    def vline():
        vstep(3)
        for d in range(1, nz): line(d).start()
    def vend():
        for d in range(1, nz): line(d).wait()
        def plane(s): return VB[6 + (z - s + nz) % nz]
        total = plane(0)
        for s in range(1, nz): total = total + plane(s)
        VB[0] = total
        cp = pltpu.make_async_copy(VB.at[0], WV, vl.at[1])
        cp.start(); cp.wait()

    def pair(i, src, dst): return rc(src, dst, es.at[i], er.at[i], (cn, z))
    def both(i, a): return pair(i, X.at[a], X.at[a + 1])
    ex = {
        "hid": both(0, HID), "skp": both(1, SKP), "cot": both(2, COT), "normed": both(3, NORMED), "att": both(4, ATT), "two": both(5, TWO),
        "px0": pair(10, X.at[EXP + co], X.at[PX]), "px1": pair(11, X.at[EXP + co + 2], X.at[PX + 1]), "br": both(12, BR),
        "qk": both(13, TG + 2 * co), "v": both(14, TG + 4), "gr": both(15, GR),
    }
    def qk_in(): return both(13, TG + 2 * c)
    def send_act(i): return both(6 + i, ACT + 2 * i)
    def arrived(*names):
        for n in names: ex[n].wait()

    def fetch(n):
        code = lookup(UNITS, n)
        kind, arg = code % 4, code // 4
        for i in range(4):
            s = jnp.where(kind == 0, i, jnp.where(kind == 1, arg, 2 * arg + i // 2))
            j = jnp.where(kind == 0, arg, jnp.where(kind == 1, 10 + i, i % 2))
            pltpu.make_async_copy(G.at[s, j], W.at[n % SLOTS, i], fsem.at[n % SLOTS, i]).start()
    def fetched(n):
        for i in range(4):
            pltpu.make_async_copy(G.at[0, 0], W.at[n % SLOTS, i], fsem.at[n % SLOTS, i]).wait()
    def weight(n): return W[n % SLOTS].reshape(4 * R, C)
    def vec(i): return VEC[pl.ds(i, 1), :]
    def tally(i, v): VB[0, pl.ds(i, 1), :] = jnp.sum(v, axis=0, keepdims=True)

    def do_matmul(dot, a, n, acc, e, wait, pre, post):
        @pl.when(pre > 0)
        def _(): fetch(pre - 1)
        @pl.when(wait > 0)
        def _(): fetched(n)
        v = dot(X[a], weight(n))
        E[e] = jnp.where(acc > 0, E[e], 0.0) + v
        @pl.when(post > 0)
        def _(): fetch(post - 1)
    def do_cast(a):
        X[a] = E[0].astype(bf16)
    def do_norm(k):
        v = jnp.where(k > 0, MID[...], 0.0) + E[0] + vec(3 * k)
        MID[...] = v
        m = v - jnp.mean(v, axis=-1, keepdims=True)
        r = lax.rsqrt(jnp.mean(m * m, axis=-1, keepdims=True) + EPS)
        XH[k] = m * r
        INV[k] = jnp.broadcast_to(r, INV.shape[1:])
        a = NORMED + (TWO - NORMED) * k
        X[a] = (m * r * vec(3 * k + 1) + vec(3 * k + 2)).astype(bf16)
        both(3 + 2 * k, a).start()
    def do_norm_back(k):
        e = E[0]
        xhat = XH[k]
        tally(3 * k + 1, e * xhat); tally(3 * k + 2, e)
        t = e * vec(3 * k + 1)
        a = jnp.mean(t, axis=-1, keepdims=True)
        b = jnp.mean(t * xhat, axis=-1, keepdims=True)
        v = MID[...] + (t - a - xhat * b) * INV[k, :, 0:1]
        MID[...] = v
        low = v.astype(bf16)
        a = GR + (BR - GR) * k
        X[a] = low
        tally(3 * k, low.astype(f32))
        both(15 - 3 * k, a).start()
    step = C // 3
    def part(n): return pl.ds(pl.multiple_of(step * n, 128), step)
    def do_gelu(i):
        def one(n, _):
            v = E[0, :, part(n)] + VEC[pl.ds(7 + i, 1), part(n)]
            cdf = 0.5 * (1.0 + lax.erf(v * (0.5 ** 0.5)))
            X[ACT + 2 * i, :, part(n)] = (v * cdf).astype(bf16)
            X[EXP + i, :, part(n)] = (cdf + v * jnp.exp(-0.5 * v * v) * 0.3989422804014327).astype(bf16)
            return 0
        lax.fori_loop(0, 3, one, 0)
        send_act(i).start()
    def do_gelu_back(i):
        def one(n, _):
            low = (E[1, :, part(n)] * X[EXP + i, :, part(n)].astype(f32)).astype(bf16)
            X[EXP + i, :, part(n)] = low
            VB[0, pl.ds(7 + i, 1), part(n)] = jnp.sum(low.astype(f32), axis=0, keepdims=True)
            return 0
        lax.fori_loop(0, 3, one, 0)
    hs = C // HEADS
    group = HEADS // 4
    def do_attend(i):
        for g in range(4):
            @pl.when(i == g)
            def _():
                for h in range(group * g, group * g + group):
                    sl = slice(hs * h, hs * h + hs)
                    scores = nt(X[TRI + 1, :, sl], X[TRI, :, sl]) * scale
                    scores = jnp.where(MASK[:, 0:1] > 0, scores, NEGATIVE)
                    e = jnp.exp(scores - jnp.max(scores, axis=0, keepdims=True))
                    p = (e * (1.0 / jnp.sum(e, axis=0, keepdims=True))).astype(bf16)
                    PR[h] = p
                    X[ATT, :, sl] = tn(p, X[TRI + 2, :, sl]).astype(bf16)
    def do_attend_back(i):
        for g in range(4):
            @pl.when(i == g)
            def _():
                for h in range(group * g, group * g + group):
                    sl = slice(hs * h, hs * h + hs)
                    q, k, v, d, p = X[TRI, :, sl], X[TRI + 1, :, sl], X[TRI + 2, :, sl], X[ATTG, :, sl], PR[h]
                    X[TG + 4, :, sl] = nn(p, d).astype(bf16)
                    pg = nt(v, d)
                    pf = p.astype(f32)
                    sg = (pf * (pg - jnp.sum(pf * pg, axis=0, keepdims=True))).astype(bf16)
                    X[TG, :, sl] = (tn(sg, k) * scale).astype(bf16)
                    X[TG + 2, :, sl] = (nn(sg, q) * scale).astype(bf16)
    def put(p):
        cps = [pltpu.make_async_copy(DB.at[pl.ds(R * s, R)], D.at[s, p], dsem.at[s]) for s in range(4)]
        for cp in cps: cp.start()
        for cp in cps: cp.wait()
    def do_rows(kind):
        merge = kind // 2
        right = COT + (GR - COT) * merge
        def one(s, _):
            left = ACT + 2 * s + merge * (HID + 2 * (s // 2) - ACT - 2 * s)
            cut = merge * (2 * (s % 2)) + (1 - merge) * 2 * (1 - kind) + c
            rows = pl.ds(pl.multiple_of(R * s, 16), R)
            for v in range(4):
                @pl.when(cut == v)
                def _():
                    sl = slice(R * v, R * v + R)
                    DB[rows] = (tn(X[left, :, sl], X[right]) + tn(X[left + 1, :, sl], X[right + 1])).astype(bf16)
            return 0
        lax.fori_loop(0, 4, one, 0)
        put(6 - kind - 4 * merge)
    def do_full(kind):
        left = jnp.where(kind < 2, TWO, jnp.where(kind == 2, NORMED + (ATT - NORMED) * c, NORMED))
        right = jnp.where(kind == 0, EXP + 2 + c, jnp.where(kind == 1, EXP + c, jnp.where(kind == 2, TG + 4 + (BR - TG - 4) * c, TG + 2 * c)))
        other = jnp.where(kind == 0, PX + 1, jnp.where(kind == 1, PX, right + 1))
        def one(n, _):
            DB[pl.ds(pl.multiple_of(step * n, 128), step)] = (tn(X[left, :, part(n)], X[right]) + tn(X[left + 1, :, part(n)], X[other])).astype(bf16)
            return 0
        lax.fori_loop(0, 3, one, 0)
        put(4 - kind)

    def x_begin():
        VB[0] = jnp.zeros_like(VB[0])
        for cp in inputs: cp.wait()
        for n in ("hid", "skp", "cot"): ex[n].start()
        for j in range(room, NB):
            load_in(j).wait()
            load_out(j, stage(j)).start()
    def x_stored():
        for j in range(AHEAD + 2, NB): load_out(j, stage(j)).wait()
    def x_attended(): ex["att"].start()
    def x_acts():
        arrived("cot")
        for i in range(4): send_act(i).wait()
    def x_result():
        ex["px0"].start(); ex["px1"].start()
        X[OUT] = (MID[...] + E[0] + vec(6)).astype(bf16)
        pltpu.make_async_copy(X.at[OUT], res, osem.at[0]).start()
        up_ = X[COT].astype(f32)
        MID[...] = up_
        tally(6, up_)
    def x_px(): arrived("px0", "px1", "two")
    def x_triple():
        ex["qk"].start(); ex["v"].start()
    def x_heads():
        arrived("normed", "att", "br", "v")
        ex["qk"].wait_send(); qk_in().wait_recv()
    def x_merge(): arrived("hid", "skp", "gr")
    def x_outs():
        pltpu.make_async_copy(X.at[OUT], res, osem.at[0]).wait()
    def x_last():
        outs = [pltpu.make_async_copy(X.at[OUT + i], (hgrad, sgrad)[i], osem.at[1 + i]) for i in range(2)]
        for cp in outs: cp.start()
        for cp in outs: cp.wait()
    extras = [x_begin, x_stored, x_attended, x_acts, x_result, x_px, x_triple, x_heads, x_merge, x_outs, x_last,
              functools.partial(vstep, 0), functools.partial(vstep, 1), functools.partial(vstep, 2), vline, vend]
    def do_extra(i):
        for k, fn in enumerate(extras):
            @pl.when(i == k)
            def _(): fn()

    def run(n, _):
        code = lookup([op for _, op in OPS], n)
        mode, a, w = code % 16, code // 16 % 64, code // 1024 % 32
        acc, e, wait = code // 2 ** 15 % 2, code // 2 ** 16 % 2, code // 2 ** 17 % 2
        pre, post = code // 2 ** 18 % 32, code // 2 ** 23 % 32
        small = ((do_extra, EXTRA), (do_cast, CAST), (fetch, FETCH), (do_norm, NORM), (do_norm_back, NORM_BACK), (do_gelu, GELU),
                 (do_gelu_back, GELU_BACK), (do_attend, ATTEND), (do_attend_back, ATTEND_BACK), (do_rows, ROWS), (do_full, FULL))
        for dot, m in ((nn, NN), (nt, NT)):
            @pl.when(mode == m)
            def _(): do_matmul(dot, a, w, acc, e, wait, pre, post)
        for fn, m in small:
            @pl.when(mode == m)
            def _(): fn(a)
        return 0

    def tick(t, _):
        @pl.when(t < NB + nz - 2 + 3)
        def _(): gather_tick(t)
        @pl.when(t >= LEAD)
        def _(): sum_tick(t - LEAD)
        lax.fori_loop(lookup(STARTS, t), lookup(STARTS, t + 1), run, 0)
        return 0
    lax.fori_loop(0, LEAD + AHEAD + Q + nz + 3, tick, 0)


def block(hidden, skipped, cotangent, mask, vectors, weights, nz):
    L, C = hidden.shape
    R = weights[2].shape[0]
    T = R // 2 // SUB
    S = pltpu.SemaphoreType.DMA
    V = pltpu.VMEM
    rows = jax.ShapeDtypeStruct((L, C), bf16)
    hbm = pl.BlockSpec(memory_space=pl.ANY)
    out_shape = (rows, rows, rows, jax.ShapeDtypeStruct((NB, R, C), bf16), jax.ShapeDtypeStruct((VR, C), f32),
                 jax.ShapeDtypeStruct((nz, NB, R, C), bf16), jax.ShapeDtypeStruct((nz, NP, R, C), bf16))
    scratch = [
        V((SLOTS, 4, R, C), bf16), V((PLACES, L, C), bf16), V((HEADS, L, L), bf16), V((2, L, C), f32), V((L, C), f32),
        V((2, L, C), f32), V((2, L, 128), f32), V((L, 128), f32), V((VR, C), f32), V((4 * R, C), bf16),
        V((RING, nz, T, C), bf16), V((RING, nz, T, C), bf16), V((RING, nz + 1, T, C), bf16), V((RING, T, C), bf16), V((RING, T, C), bf16),
        V((6 + nz, VR, C), f32),
        S((NB,)), S((NB,)), S((NB, 2, nz - 1)), S((NB, 2, nz - 1)), S((NB, nz)), S((NB, nz)), S((NB, nz)), S((NB, nz)), S((NB, nz)), S((NB, nz)),
        S((SLOTS, 4)), S((5,)), S((16,)), S((16,)), S((4,)), S((3,)),
        S((nz, Q)), S((nz, Q)), S((nz, Q)), S((nz, Q)), S((nz + 1, Q)), S((Q,)), S((Q,)), S((Q,)), S((Q,)), S((Q,)), S((2, Q)), S((2, Q)),
        S((2,)), S((2 + nz,)), S((2 + nz,)),
    ]
    return pl.pallas_call(
        functools.partial(block_kernel, nz=nz),
        out_shape=out_shape, in_specs=[hbm] * 10, out_specs=(hbm,) * 7, scratch_shapes=scratch,
        compiler_params=pltpu.CompilerParams(collective_id=0, has_side_effects=True, vmem_limit_bytes=63 * 2**20),
    )(hidden, skipped, cotangent, mask, vectors, *weights)[:5]


def unpack_kernel(F, m, t, o, e, r):
    i = pl.program_id(0)
    for out, lo, n in ((m, 0, 2), (t, 2, 3), (o, 5, 1), (e, 6, 4), (r, 10, 4)):
        @pl.when((i >= lo) & (i < lo + n))
        def _(): out[...] = F[0].astype(f32)


def unpack(F):
    R, C = F.shape[1:]
    def spot(lo, n, along):
        def index(i):
            j = jnp.clip(i - lo, 0, n - 1)
            return (j, 0) if along == 0 else (0, j)
        return pl.BlockSpec((R, C), index)
    shapes = [(2 * R, C), (R, 3 * C), (R, C), (R, 4 * C), (4 * R, C)]
    return pl.pallas_call(
        unpack_kernel, grid=(NB,),
        out_shape=[jax.ShapeDtypeStruct(s, f32) for s in shapes],
        in_specs=[pl.BlockSpec((1, R, C), lambda i: (i, 0, 0))],
        out_specs=[spot(0, 2, 0), spot(2, 3, 1), spot(5, 1, 0), spot(6, 4, 1), spot(10, 4, 0)],
        compiler_params=pltpu.CompilerParams(vmem_limit_bytes=48 * 2**20),
    )(F)

def pack(m, t, o, e, r):
    R, C = o.shape
    def cut(w):
        a, b = w.shape
        return w.reshape(a // R, R, b // C, C).transpose(0, 2, 1, 3).reshape(-1, R, C)
    return jnp.concatenate([cut(w) for w in (m, t, o, e, r)])


def against(left, right):
    return lax.dot_general(left, right, (((1,), (1,)), ((), ())), preferred_element_type=jnp.float32)


def weight_grad(left, right):
    return lax.dot_general(left, right, (((0,), (0,)), ((), ())), preferred_element_type=jnp.float32)


def norm_parts(v):
    c = v - jnp.mean(v, axis=-1, keepdims=True)
    inv = lax.rsqrt(jnp.mean(c * c, axis=-1, keepdims=True) + EPS)
    return c * inv, inv


def norm_back(e, xhat, inv, gain):
    t = e * gain
    return (t - jnp.mean(t, axis=-1, keepdims=True) - xhat * jnp.mean(t * xhat, axis=-1, keepdims=True)) * inv


def plain(hidden, skipped, row_mask, cotangent, merge_weight, merge_bias, first_gain, first_shift, triple_weight,
         output_weight, output_bias, second_gain, second_shift, expand_weight, expand_bias, reduce_weight, reduce_bias):
    length, D = hidden.shape[1:]
    hs = D // HEADS
    nz = lax.axis_size("seq")
    z = lax.axis_index("seq")
    c = lax.axis_index("dp") % 2
    weights = (merge_weight, triple_weight, output_weight, expand_weight, reduce_weight)
    G = lax.all_gather(pack(*weights), "seq")
    R = G.shape[2]
    merge_full = G[:, 0:2].reshape(2 * D, D)
    triple_full = G[:, 2:5].transpose(1, 0, 2, 3).reshape(3, D, D)
    output_full = G[:, 5].reshape(D, D)
    expand_full = G[:, 6:10].transpose(1, 0, 2, 3).reshape(4, D, D)
    reduce_full = G[:, 10:14].reshape(4 * D, D)
    gain_a, shift_a, gain_b, shift_b = (v.astype(f32) for v in (first_gain, first_shift, second_gain, second_shift))
    joined = jnp.concatenate([hidden[0], skipped[0]], axis=-1)
    merged = jnp.dot(joined, merge_full, preferred_element_type=f32) + merge_bias.astype(f32)
    xhat_a, inv_a = norm_parts(merged)
    normed = (xhat_a * gain_a + shift_a).astype(bf16)
    triple = jnp.einsum("ld,jde->jle", normed, triple_full, preferred_element_type=f32).astype(bf16)
    queries, key_heads, value_heads = (triple[j].reshape(length, HEADS, hs) for j in range(3))
    valid = lax.dynamic_index_in_dim(row_mask, z, 0, False)
    scores = jnp.einsum("qhd,khd->hqk", queries, key_heads, preferred_element_type=f32) * hs ** -0.5
    scores = jnp.where(valid[None, None, :] > 0, scores, NEGATIVE)
    weights_ = jnp.exp(scores - jnp.max(scores, axis=-1, keepdims=True))
    probs = weights_ / jnp.sum(weights_, axis=-1, keepdims=True)
    probs_low = probs.astype(bf16)
    attended = jnp.einsum("hqk,khd->qhd", probs_low, value_heads, preferred_element_type=f32).astype(bf16).reshape(length, D)
    middle = merged + jnp.dot(attended, output_full, preferred_element_type=f32) + output_bias.astype(f32)
    xhat_b, inv_b = norm_parts(middle)
    normed_two = (xhat_b * gain_b + shift_b).astype(bf16)
    expanded = jnp.einsum("ld,jde->jle", normed_two, expand_full, preferred_element_type=f32) + expand_bias.astype(f32).reshape(4, 1, D)
    activated, gelu_back = jax.vjp(functools.partial(jax.nn.gelu, approximate=False), expanded)
    activated = activated.astype(bf16).transpose(1, 0, 2).reshape(length, 4 * D)
    result = middle + jnp.dot(activated, reduce_full, preferred_element_type=f32) + reduce_bias.astype(f32)
    result = result.astype(bf16)
    upstream = cotangent[0]
    wide = upstream.astype(f32)
    activated_grad = jnp.einsum("le,jde->jld", upstream, reduce_full.reshape(4, D, D), preferred_element_type=f32)
    expanded_grad = gelu_back(activated_grad)[0].astype(bf16)
    e_two = jnp.einsum("jle,jde->ld", expanded_grad, expand_full, preferred_element_type=f32)
    middle_grad = wide + norm_back(e_two, xhat_b, inv_b, gain_b)
    branch_grad = middle_grad.astype(bf16)
    attended_grad = against(branch_grad, output_full).astype(bf16).reshape(length, HEADS, hs)
    prob_grad = jnp.einsum("qhd,khd->hqk", attended_grad, value_heads, preferred_element_type=f32)
    values_grad = jnp.einsum("hqk,qhd->khd", probs_low, attended_grad, preferred_element_type=f32)
    score_grad = (probs * (prob_grad - jnp.sum(probs * prob_grad, axis=-1, keepdims=True))).astype(bf16)
    queries_grad = jnp.einsum("hqk,khd->qhd", score_grad, key_heads, preferred_element_type=f32) * hs ** -0.5
    keys_grad = jnp.einsum("hqk,qhd->khd", score_grad, queries, preferred_element_type=f32) * hs ** -0.5
    triple_grad = jnp.stack([g.astype(bf16).reshape(length, D) for g in (queries_grad, keys_grad, values_grad)])
    e_one = jnp.einsum("jle,jde->ld", triple_grad, triple_full, preferred_element_type=f32)
    merged_grad = (middle_grad + norm_back(e_one, xhat_a, inv_a, gain_a)).astype(bf16)
    joined_grad = against(merged_grad, merge_full).astype(bf16)
    vectors = jnp.stack([
        jnp.sum(merged_grad.astype(f32), 0), jnp.sum(e_one * xhat_a, 0), jnp.sum(e_one, 0),
        jnp.sum(branch_grad.astype(f32), 0), jnp.sum(e_two * xhat_b, 0), jnp.sum(e_two, 0), jnp.sum(wide, 0),
    ])
    vectors = jnp.concatenate([vectors, jnp.sum(expanded_grad.astype(f32), 1), jnp.zeros((VR - 11, D), f32)])

    count = lax.axis_size("dp")
    def both(v):
        other = lax.ppermute(v, "dp", [(i, i + 1 - 2 * (i % 2)) for i in range(count)])
        return jnp.concatenate([v, other], axis=-2)
    joined2, normed2, triple2, attended2, branch2, normed_two2, expanded2, activated2, upstream2 = (
        both(v) for v in (joined, normed, triple_grad, attended, branch_grad, normed_two, expanded_grad, activated, upstream))
    def pick(v, axis, index):
        return lax.dynamic_index_in_dim(v, index, axis, False)
    def rows(left, right):
        return jnp.einsum("lsr,le->sre", left, right, preferred_element_type=f32).astype(bf16)
    def split(left):
        return left.reshape(left.shape[0], nz, -1, R)
    parts = [
        rows(pick(split(joined2), 2, c), both(merged_grad)),
        rows(split(normed2)[:, :, 0], pick(triple2, 0, c)),
        rows(split(jnp.where(c == 0, normed2, attended2))[:, :, 0], jnp.where(c == 0, triple2[2], branch2)),
        rows(split(normed_two2)[:, :, 0], pick(expanded2, 0, c)),
        rows(split(normed_two2)[:, :, 0], pick(expanded2, 0, c + 2)),
        rows(pick(split(activated2), 2, c), upstream2),
        rows(pick(split(activated2), 2, c + 2), upstream2),
    ]
    grads = jnp.stack(parts, axis=1)
    wide_grads = jnp.stack([jnp.where(c == i, grads, 0) for i in range(2)], axis=2).reshape(nz, NB, R, D)
    F = lax.psum(lax.psum_scatter(wide_grads, "seq", scatter_dimension=0, tiled=False), "dp")
    vectors = lax.psum(vectors, ("dp", "seq"))
    F = F.astype(f32)
    def columns(blocks):
        return blocks.transpose(1, 0, 2).reshape(R, -1)
    summed = (F[0:2].reshape(-1, D), columns(F[2:5]), F[5], columns(F[6:10]), F[10:14].reshape(-1, D))
    return outputs((result, joined_grad[:, :D], joined_grad[:, D:]), summed, vectors)


def outputs(images, summed, vectors):
    result, hidden_grad, skipped_grad = images
    merge, triple, output, expand, reduce = summed
    return (result[None], hidden_grad[None], skipped_grad[None], merge, vectors[0], vectors[1], vectors[2], triple, output,
            vectors[3], vectors[4], vectors[5], expand, vectors[7:11].reshape(-1), reduce, vectors[6])


def body(hidden, skipped, row_mask, cotangent, merge_weight, merge_bias, first_gain, first_shift, triple_weight,
         output_weight, output_bias, second_gain, second_shift, expand_weight, expand_bias, reduce_weight, reduce_bias):
    L, C = hidden.shape[1:]
    nz = lax.axis_size("seq")
    valid = lax.dynamic_index_in_dim(row_mask, lax.axis_index("seq"), 0, False)
    mask = jnp.broadcast_to(valid.astype(f32)[:, None], (L, 128))
    vectors = jnp.concatenate([
        merge_bias, first_gain, first_shift, output_bias, second_gain, second_shift, reduce_bias, expand_bias,
        jnp.zeros(((VR - 11) * C,), bf16)]).astype(f32).reshape(VR, C)
    weights = (merge_weight, triple_weight, output_weight, expand_weight, reduce_weight)
    *images, F, sums = block(hidden[0], skipped[0], cotangent[0], mask, vectors, weights, nz)
    return outputs(images, unpack(F), sums)


def solution(mesh):
    rows, held, copied = P(("dp", "seq"), None, None), P("seq", None), P()
    fast = mesh.shape["dp"] == 8 and mesh.shape["seq"] == 4
    return jax.shard_map(
        body if fast else plain,
        mesh=mesh,
        in_specs=(rows, rows, P("dp", None), rows, held, copied, copied, copied, held, held, copied, copied, copied,
                  held, copied, held, copied),
        out_specs=(rows, rows, rows, held, copied, copied, copied, held, held, copied, copied, copied, held, copied,
                   held, copied),
        check_vma=False,
    )
```

```python
import functools

import jax
import jax.numpy as jnp
from jax import lax
from jax.experimental import pallas as pl
from jax.experimental.pallas import tpu as pltpu
from jax.sharding import PartitionSpec as P

MESH = pl.DeviceIdType.MESH
HEADS = 16
EPS = 1e-05
NEGATIVE = -1e30
NB = 14
NP, SUB = 7, 3
Q = NP * SUB
AHEAD = 2
RING = 8
SLOTS = 3
VR = 16
READY = 5
LEAD = READY + 10
f32, bf16 = jnp.float32, jnp.bfloat16


def block_slices(refs):
    merge, triple, output, expand, reduce = refs
    R, C = output.shape
    out = []
    for j in range(merge.shape[0] // R): out.append(merge.at[pl.ds(j * R, R), :])
    for j in range(triple.shape[1] // C): out.append(triple.at[:, pl.ds(j * C, C)])
    out.append(output.at[:, :])
    for j in range(expand.shape[1] // C): out.append(expand.at[:, pl.ds(j * C, C)])
    for j in range(reduce.shape[0] // R): out.append(reduce.at[pl.ds(j * R, R), :])
    return out


def nn(a, b):
    return jnp.dot(a, b, preferred_element_type=f32)


def nt(a, b):
    return lax.dot_general(a, b, (((1,), (1,)), ((), ())), preferred_element_type=f32)


def tn(a, b):
    return lax.dot_general(a, b, (((0,), (0,)), ((), ())), preferred_element_type=f32)


HID, SKP, COT, NORMED, ATT, TWO, ACT, TRI, BR, TG, GR, EXP, PX, ATTG, OUT, PLACES = 0, 2, 4, 6, 8, 10, 12, 20, 23, 25, 31, 33, 37, 39, 40, 42
NN, NT, EXTRA, CAST, FETCH, NORM, NORM_BACK, GELU, GELU_BACK, ATTEND, ATTEND_BACK, ROWS, FULL = range(1, 14)


def op(mode, a=0, w=0, acc=0, e=0, wait=1, pre=None, post=None):
    pre, post = (0 if v is None else v + 1 for v in (pre, post))
    return mode + 16 * (a + 64 * (w + 32 * (acc + 2 * (e + 2 * (wait + 2 * (pre + 32 * post))))))


def plan():
    B = READY
    ops = [(0, op(EXTRA, 0)), (1, op(EXTRA, 1))]
    ops += [(B + 1, o) for o in (op(FETCH, 0), op(NN, HID, 0, pre=1), op(NN, SKP, 1, acc=1), op(NORM, 0))]
    for j in range(3):
        ops += [(B + 2 + j, o) for o in (op(NN, NORMED, 2 + j, pre=2 + j), op(CAST, TRI + j))]
    ops += [(B + 4, op(ATTEND, 0)), (B + 4, op(ATTEND, 1)), (B + 5, op(ATTEND, 2)), (B + 5, op(ATTEND, 3)), (B + 5, op(EXTRA, 2))]
    ops += [(B + 5, op(NN, ATT, 5, pre=5)), (B + 5, op(NORM, 1))]
    for i in range(4):
        ops += [(B + 6 + i, op(NN, TWO, 6 + i, pre=6 + i)), (B + 6 + i, op(GELU, i))]
    ops += [(B + 9, op(EXTRA, 3)), (B + 9, op(ROWS, 0)), (B + 10, op(ROWS, 1))]
    ops += [(B + 13, op(FETCH, 10 + i)) for i in range(3)]
    for i in range(4):
        ops += [(B + 13 + i // 2, o) for o in (
            op(NN, ACT + 2 * i, 10 + i, acc=int(i > 0)), op(NT, COT, 10 + i, e=1, wait=0, post=13 + i), op(GELU_BACK, i))]
    ops += [(B + 14, op(EXTRA, 4)), (B + 15, op(EXTRA, 5)), (B + 15, op(FULL, 0)), (B + 16, op(FULL, 1))]
    for i in range(4):
        ops += [(B + 16 + (i > 0), op(NT, EXP + i, 14 + i, acc=int(i > 0), post=17 + i))]
    ops += [(B + 17, op(NORM_BACK, 1)), (B + 18, op(NT, BR, 18, post=21)), (B + 18, op(CAST, ATTG))]
    ops += [(B + 18 + g // 2, op(ATTEND_BACK, g)) for g in range(4)]
    ops += [(B + 19, op(EXTRA, 6)), (B + 20, op(EXTRA, 7)), (B + 20, op(FULL, 2)), (B + 21, op(FULL, 3))]
    for j in range(3):
        ops += [(B + 22, op(NT, TG + 2 * j, 19 + j, acc=int(j > 0), post=22 + j if j < 2 else None))]
    ops += [(B + 23, op(NORM_BACK, 0)), (B + 24, op(EXTRA, 8)), (B + 24, op(ROWS, 2)), (B + 25, op(EXTRA, 9))]
    for i in range(2):
        ops += [(B + 25, op(NT, GR, 22 + i)), (B + 25, op(CAST, OUT + i))]
    ops += [(B + 25, op(EXTRA, 10))]
    ops += [(B + t, op(EXTRA, 11 + i)) for i, t in enumerate((26, 27, 28, 29, 32))]
    return ops


OPS = plan()
STARTS = [sum(t < tick for t, _ in OPS) for tick in range(LEAD + AHEAD + Q + 10)]
UNITS = [2, 6] + [4 * j for j in range(2, 10)] + [1 + 4 * s for s in range(4)] + [4 * j for j in (6, 7, 8, 9, 5, 2, 3, 4)] + [2, 6]


def lookup(values, i):
    total = jnp.int32(values[0])
    for k in range(1, len(values)):
        if values[k] != values[k - 1]:
            total = total + jnp.where(i >= k, values[k] - values[k - 1], 0)
    return total


def block_kernel(hid, skp, cot_in, mask_in, *refs, nz):
    (b0, b1, b2, b3, b4, b5, b6, b7, wm, wt, wo, we, wr,
     res, hgrad, sgrad, F, WV, G, D,
     W, X, PR, XH, MID, E, INV, MASK, VEC, DB, MROWS, v0, v1, v2, v3, v4, v5, v6, v7,
     K, R1, R2, R3, O, VB,
     loc, loc2, zs, zr, xs, xr, ys, yr, cs, cr, fsem, insem, es, er, dsem, osem,
     ld, s1, r1, s2, r2, s3, r3, st, sf, rf, sc, rcv, vl, vs, vr) = refs
    dp = lax.axis_index("dp"); z = lax.axis_index("seq")
    c = dp % 2; x = (dp // 2) % 2; y = dp // 4
    xn = dp + 2 - 4 * x; yn = dp + 4 - 8 * y; cn = dp + 1 - 2 * c; co = 1 - c
    L, C = X.shape[1:]
    R = G.shape[2]
    scale = (C // HEADS) ** -0.5
    bar = pltpu.get_barrier_semaphore()
    for tgt in (xn, yn, cn):
        pl.semaphore_signal(bar, inc=1, device_id=(tgt, z), device_id_type=MESH)
    for d in range(1, nz):
        pl.semaphore_signal(bar, inc=1, device_id=(dp, (z + d) % nz), device_id_type=MESH)

    def rc(src, dst, ss, rs, dev):
        return pltpu.make_async_remote_copy(src_ref=src, dst_ref=dst, send_sem=ss, recv_sem=rs, device_id=dev, device_id_type=MESH)

    blocks = block_slices((wm, wt, wo, we, wr))
    room = SLOTS * 4
    def stage(j): return W.at[(j % room) // 4, j % 4]
    def load_in(j): return pltpu.make_async_copy(blocks[j], stage(j), loc.at[j])
    def load_out(j, slot): return pltpu.make_async_copy(slot, G.at[z, j], loc2.at[j])
    for j in range(min(room, NB)): load_in(j).start()
    inputs = [pltpu.make_async_copy(a, b, insem.at[i]) for i, (a, b) in enumerate(
        ((hid.at[0], X.at[HID]), (skp.at[0], X.at[SKP]), (cot_in.at[0], X.at[COT]), (mask_in, MROWS),
         (b0, v0), (b1, v1), (b2, v2), (b3, v3), (b4, v4), (b5, v5), (b6, v6), (b7, v7)))]
    for cp in inputs: cp.start()
    for j in range(4):
        load_in(j).wait()
        load_out(j, stage(j)).start()
    pl.semaphore_wait(bar, nz + 2)

    half = R // 2; third = half // 3
    base = half * c
    zp = ((x + y) % 2) * (2 - x)
    yp = 1 + y
    def reg(s, b, start, n):
        return G.at[s, b, pl.ds(pl.multiple_of(start, 16), n), :]
    def same(region, ss, rs, dev): return rc(region, region, ss, rs, dev)
    def zcopy(b, d, k):
        s = z - k if d == 0 else z + k
        return same(reg(s, b, base + third * zp, third), zs.at[b % RING, d, k], zr.at[b % RING, d, k], (dp, z + 1 if d == 0 else z - 1))
    def zsend_ok(d, k):
        return (z >= k) & (z < nz - 1) if d == 0 else (z + k <= nz - 1) & (z > 0)
    def zrecv_ok(d, k):
        return z >= k + 1 if d == 0 else z + 1 + k <= nz - 1
    def shard_in(d, k):
        return z - 1 - k if d == 0 else z + 1 + k
    def xcopy(b, s): return same(reg(s, b, base + third * zp, third), xs.at[b % 6, s], xr.at[b % 6, s], (xn, z))
    def ycopy(b, s): return same(reg(s, b, base + third * yp, third), ys.at[b % 6, s], yr.at[b % 6, s], (yn, z))
    def ccopy(b, s): return same(reg(s, b, base, half), cs.at[b % 6, s], cr.at[b % 6, s], (cn, z))
    def own(b):
        for d in (0, 1):
            @pl.when(zsend_ok(d, 0))
            def _(): zcopy(b, d, 0).start()
    def zarr(b, d, k):
        zcopy(b, d, k).wait_recv()
        if k + 1 < nz - 1:
            @pl.when(zsend_ok(d, k + 1))
            def _(): zcopy(b, d, k + 1).start()
        s = shard_in(d, k)
        xcopy(b, s).start()
        @pl.when((x + y) % 2 == 1)
        def _(): ycopy(b, s).start()
    def xarr(b, d, k):
        s = shard_in(d, k)
        xcopy(b, s).wait_recv()
        @pl.when((x + y) % 2 == 0)
        def _(): ycopy(b, s).start()
    def yarr(b, d, k):
        s = shard_in(d, k)
        ycopy(b, s).wait_recv()
        ccopy(b, s).start()
    def fin(b, d, k):
        s = shard_in(d, k)
        ccopy(b, s).wait()
        xcopy(b, s).wait_send()
        ycopy(b, s).wait_send()
    for j in range(4):
        load_out(j, stage(j)).wait()
        if j < AHEAD: own(j)
    def gather_tick(t):
        @pl.when(t < NB - AHEAD)
        def _():
            own(t + AHEAD)
        for off, fn in ((0, zarr), (1, xarr), (2, yarr), (3, fin)):
            for k in range(nz - 1):
                b = t - off - k
                @pl.when((b >= 0) & (b < NB))
                def _():
                    for d in (0, 1):
                        @pl.when(zrecv_ok(d, k))
                        def _(): fn(b, d, k)
                        if off == 3:
                            @pl.when(zsend_ok(d, k))
                            def _(): zcopy(b, d, k).wait_send()

    T = K.shape[2]
    def ring(q): return q % RING
    def typ(q, s): return (q + s) % 2
    def keep(q, s): return x + typ(q, s) * (y - x)
    def near(q, s): return xn + typ(q, s) * (yn - xn)
    def far(q, s): return yn + typ(q, s) * (xn - yn)
    def piece(q, h):
        return NP - 1 - q // SUB, pl.ds(pl.multiple_of(half * h + T * (q % SUB), 16), T)
    def load(q, s):
        p, rows = piece(q, keep(q, s))
        return pltpu.make_async_copy(D.at[s, p, rows], K.at[ring(q), s], ld.at[s, ring(q)])
    def first(q, s):
        p, rows = piece(q, 1 - keep(q, s))
        return rc(D.at[s, p, rows], R1.at[ring(q), s], s1.at[s, ring(q)], r1.at[s, ring(q)], (near(q, s), z))
    def up(q, s):
        return rc(K.at[ring(q), s], R2.at[ring(q), s], s2.at[s, ring(q)], r2.at[s, ring(q)], (dp, z + 1))
    def down(q, s):
        away = jnp.minimum(z - 1 - s, 1)
        slot = nz + away * (s - nz)
        return rc(K.at[ring(q), s], R2.at[ring(q), slot], s2.at[s, ring(q)], r2.at[slot, ring(q)], (dp, z - 1))
    def got(slot, q):
        return rc(K.at[ring(q), 0], R2.at[ring(q), slot], s2.at[0, ring(q)], r2.at[slot, ring(q)], (dp, z))
    def last(q):
        return rc(K.at[ring(q), z], R3.at[ring(q)], s3.at[ring(q)], r3.at[ring(q)], (far(q, z), z))
    def frow(q, h, cc):
        p, rows = piece(q, h)
        return F.at[2 * p + cc, rows]
    def keepf(q): return pltpu.make_async_copy(O.at[ring(q)], frow(q, keep(q, z), c), st.at[ring(q)])
    def spread(q): return rc(O.at[ring(q)], frow(q, keep(q, z), c), sf.at[ring(q)], rf.at[ring(q)], (near(q, z), z))
    def spread_in(q):
        r = frow(q, 1 - keep(q, z), c)
        return rc(r, r, sf.at[ring(q)], rf.at[ring(q)], (near(q, z), z))
    def cross(q): return rc(O.at[ring(q)], frow(q, keep(q, z), c), sc.at[0, ring(q)], rcv.at[0, ring(q)], (cn, z))
    def cross2(q):
        r = frow(q, 1 - keep(q, z), c)
        return rc(r, r, sc.at[1, ring(q)], rcv.at[1, ring(q)], (cn, z))
    def add(a, b): return (a.astype(f32) + b.astype(f32)).astype(bf16)
    def issue(q):
        for s in range(nz):
            first(q, s).start(); load(q, s).start()
    def start(q):
        for s in range(nz):
            load(q, s).wait(); first(q, s).wait_recv()
            K[ring(q), s] = add(K[ring(q), s], R1[ring(q), s])
            if s > 0:
                @pl.when(z == 0)
                def _(): up(q, s).start()
            if s < nz - 1:
                @pl.when(z == nz - 1)
                def _(): down(q, s).start()
    def hop(q, k):
        for s in range(nz):
            if s > k:
                @pl.when(z == k)
                def _():
                    got(s, q).wait_recv()
                    K[ring(q), s] = add(K[ring(q), s], R2[ring(q), s])
                    up(q, s).start()
            if s < nz - 1 - k:
                @pl.when(z == nz - 1 - k)
                def _():
                    got(s, q).wait_recv()
                    K[ring(q), s] = add(K[ring(q), s], R2[ring(q), s])
                    down(q, s).start()
    def arrive(q):
        @pl.when(z > 0)
        def _():
            got(z, q).wait_recv()
            K[ring(q), z] = add(K[ring(q), z], R2[ring(q), z])
        @pl.when(z < nz - 1)
        def _():
            got(nz, q).wait_recv()
            K[ring(q), z] = add(K[ring(q), z], R2[ring(q), nz])
        last(q).start()
    def final(q):
        last(q).wait_recv()
        O[ring(q)] = add(K[ring(q), z], R3[ring(q)])
        keepf(q).start(); spread(q).start(); cross(q).start()
    def relay(q):
        spread_in(q).wait_recv()
        cross2(q).start()
        for s in range(nz):
            first(q, s).wait_send()
            if s > 0:
                @pl.when(z < s)
                def _(): up(q, s).wait_send()
            if s < nz - 1:
                @pl.when(z > s)
                def _(): down(q, s).wait_send()
        last(q).wait_send()
    def drain(q):
        keepf(q).wait(); spread(q).wait_send()
        cross(q).wait_send(); cross(q).wait_recv(); cross2(q).wait_send(); cross2(q).wait_recv()
    steps = [(0, start)] + [(k, functools.partial(hop, k=k)) for k in range(1, nz - 1)] + [
        (nz - 1, arrive), (nz, final), (nz + 1, relay), (nz + 3, drain)]
    def sum_tick(t):
        @pl.when((t >= 0) & (t < Q))
        def _(): issue(t)
        for off, fn in steps:
            q = t - AHEAD - off
            @pl.when((q >= 0) & (q < Q))
            def _(): fn(q)

    devs = ((cn, z), (xn, z), (yn, z))
    def swap(i): return rc(VB.at[2 * i], VB.at[2 * i + 1], vs.at[i], vr.at[i], devs[i])
    def vstep(i):
        if i > 0:
            swap(i - 1).wait()
            VB[2 * i] = VB[2 * i - 2] + VB[2 * i - 1]
        if i < 3:
            swap(i).start()
    def line(d):
        return rc(VB.at[6], VB.at[6 + d], vs.at[2 + d], vr.at[2 + d], (dp, (z + d) % nz))
    def vline():
        vstep(3)
        for d in range(1, nz): line(d).start()
    def vend():
        for d in range(1, nz): line(d).wait()
        def plane(s): return VB[6 + (z - s + nz) % nz]
        total = plane(0)
        for s in range(1, nz): total = total + plane(s)
        VB[0] = total
        cp = pltpu.make_async_copy(VB.at[0], WV, vl.at[1])
        cp.start(); cp.wait()

    def pair(i, src, dst): return rc(src, dst, es.at[i], er.at[i], (cn, z))
    def both(i, a): return pair(i, X.at[a], X.at[a + 1])
    ex = {
        "hid": both(0, HID), "skp": both(1, SKP), "cot": both(2, COT), "normed": both(3, NORMED), "att": both(4, ATT), "two": both(5, TWO),
        "px0": pair(10, X.at[EXP + co], X.at[PX]), "px1": pair(11, X.at[EXP + co + 2], X.at[PX + 1]), "br": both(12, BR),
        "qk": both(13, TG + 2 * co), "v": both(14, TG + 4), "gr": both(15, GR),
    }
    def qk_in(): return both(13, TG + 2 * c)
    def send_act(i): return both(6 + i, ACT + 2 * i)
    def arrived(*names):
        for n in names: ex[n].wait()

    def fetch(n):
        code = lookup(UNITS, n)
        kind, arg = code % 4, code // 4
        for i in range(4):
            s = jnp.where(kind == 0, i, jnp.where(kind == 1, arg, 2 * arg + i // 2))
            j = jnp.where(kind == 0, arg, jnp.where(kind == 1, 10 + i, i % 2))
            pltpu.make_async_copy(G.at[s, j], W.at[n % SLOTS, i], fsem.at[n % SLOTS, i]).start()
    def fetched(n):
        for i in range(4):
            pltpu.make_async_copy(G.at[0, 0], W.at[n % SLOTS, i], fsem.at[n % SLOTS, i]).wait()
    def weight(n): return W[n % SLOTS].reshape(4 * R, C)
    def vec(i): return VEC[pl.ds(i, 1), :]
    def tally(i, v): VB[0, pl.ds(i, 1), :] = jnp.sum(v, axis=0, keepdims=True)

    def do_matmul(dot, a, n, acc, e, wait, pre, post):
        @pl.when(pre > 0)
        def _(): fetch(pre - 1)
        @pl.when(wait > 0)
        def _(): fetched(n)
        v = dot(X[a], weight(n))
        E[e] = jnp.where(acc > 0, E[e], 0.0) + v
        @pl.when(post > 0)
        def _(): fetch(post - 1)
    def do_cast(a):
        X[a] = E[0].astype(bf16)
    def do_norm(k):
        v = jnp.where(k > 0, MID[...], 0.0) + E[0] + vec(3 * k)
        MID[...] = v
        m = v - jnp.mean(v, axis=-1, keepdims=True)
        r = lax.rsqrt(jnp.mean(m * m, axis=-1, keepdims=True) + EPS)
        XH[k] = m * r
        INV[k] = jnp.broadcast_to(r, INV.shape[1:])
        a = NORMED + (TWO - NORMED) * k
        X[a] = (m * r * vec(3 * k + 1) + vec(3 * k + 2)).astype(bf16)
        both(3 + 2 * k, a).start()
    def do_norm_back(k):
        e = E[0]
        xhat = XH[k]
        tally(3 * k + 1, e * xhat); tally(3 * k + 2, e)
        t = e * vec(3 * k + 1)
        a = jnp.mean(t, axis=-1, keepdims=True)
        b = jnp.mean(t * xhat, axis=-1, keepdims=True)
        v = MID[...] + (t - a - xhat * b) * INV[k, :, 0:1]
        MID[...] = v
        low = v.astype(bf16)
        a = GR + (BR - GR) * k
        X[a] = low
        tally(3 * k, low.astype(f32))
        both(15 - 3 * k, a).start()
    step = C // 3
    def part(n): return pl.ds(pl.multiple_of(step * n, 128), step)
    def do_gelu(i):
        def one(n, _):
            v = E[0, :, part(n)] + VEC[pl.ds(7 + i, 1), part(n)]
            cdf = 0.5 * (1.0 + lax.erf(v * (0.5 ** 0.5)))
            X[ACT + 2 * i, :, part(n)] = (v * cdf).astype(bf16)
            X[EXP + i, :, part(n)] = (cdf + v * jnp.exp(-0.5 * v * v) * 0.3989422804014327).astype(bf16)
            return 0
        lax.fori_loop(0, 3, one, 0)
        send_act(i).start()
    def do_gelu_back(i):
        def one(n, _):
            low = (E[1, :, part(n)] * X[EXP + i, :, part(n)].astype(f32)).astype(bf16)
            X[EXP + i, :, part(n)] = low
            VB[0, pl.ds(7 + i, 1), part(n)] = jnp.sum(low.astype(f32), axis=0, keepdims=True)
            return 0
        lax.fori_loop(0, 3, one, 0)
    hs = C // HEADS
    group = HEADS // 4
    def do_attend(i):
        for g in range(4):
            @pl.when(i == g)
            def _():
                for h in range(group * g, group * g + group):
                    sl = slice(hs * h, hs * h + hs)
                    scores = nt(X[TRI + 1, :, sl], X[TRI, :, sl]) * scale
                    scores = jnp.where(MASK[:, 0:1] > 0, scores, NEGATIVE)
                    e = jnp.exp(scores - jnp.max(scores, axis=0, keepdims=True))
                    p = (e * (1.0 / jnp.sum(e, axis=0, keepdims=True))).astype(bf16)
                    PR[h] = p
                    X[ATT, :, sl] = tn(p, X[TRI + 2, :, sl]).astype(bf16)
    def do_attend_back(i):
        for g in range(4):
            @pl.when(i == g)
            def _():
                for h in range(group * g, group * g + group):
                    sl = slice(hs * h, hs * h + hs)
                    q, k, v, d, p = X[TRI, :, sl], X[TRI + 1, :, sl], X[TRI + 2, :, sl], X[ATTG, :, sl], PR[h]
                    X[TG + 4, :, sl] = nn(p, d).astype(bf16)
                    pg = nt(v, d)
                    pf = p.astype(f32)
                    sg = (pf * (pg - jnp.sum(pf * pg, axis=0, keepdims=True))).astype(bf16)
                    X[TG, :, sl] = (tn(sg, k) * scale).astype(bf16)
                    X[TG + 2, :, sl] = (nn(sg, q) * scale).astype(bf16)
    def put(p):
        cps = [pltpu.make_async_copy(DB.at[pl.ds(R * s, R)], D.at[s, p], dsem.at[s]) for s in range(4)]
        for cp in cps: cp.start()
        for cp in cps: cp.wait()
    def do_rows(kind):
        merge = kind // 2
        right = COT + (GR - COT) * merge
        def one(s, _):
            left = ACT + 2 * s + merge * (HID + 2 * (s // 2) - ACT - 2 * s)
            cut = merge * (2 * (s % 2)) + (1 - merge) * 2 * (1 - kind) + c
            rows = pl.ds(pl.multiple_of(R * s, 16), R)
            for v in range(4):
                @pl.when(cut == v)
                def _():
                    sl = slice(R * v, R * v + R)
                    DB[rows] = (tn(X[left, :, sl], X[right]) + tn(X[left + 1, :, sl], X[right + 1])).astype(bf16)
            return 0
        lax.fori_loop(0, 4, one, 0)
        put(6 - kind - 4 * merge)
    def do_full(kind):
        left = jnp.where(kind < 2, TWO, jnp.where(kind == 2, NORMED + (ATT - NORMED) * c, NORMED))
        right = jnp.where(kind == 0, EXP + 2 + c, jnp.where(kind == 1, EXP + c, jnp.where(kind == 2, TG + 4 + (BR - TG - 4) * c, TG + 2 * c)))
        other = jnp.where(kind == 0, PX + 1, jnp.where(kind == 1, PX, right + 1))
        def one(n, _):
            DB[pl.ds(pl.multiple_of(step * n, 128), step)] = (tn(X[left, :, part(n)], X[right]) + tn(X[left + 1, :, part(n)], X[other])).astype(bf16)
            return 0
        lax.fori_loop(0, 3, one, 0)
        put(4 - kind)

    def x_begin():
        VB[0] = jnp.zeros_like(VB[0])
        for cp in inputs: cp.wait()
        for n in ("hid", "skp", "cot"): ex[n].start()
        valid = MROWS[pl.ds(z, 1), :].astype(f32)
        MASK[...] = jnp.broadcast_to(valid, (MASK.shape[1], L)).T
        for i, v in enumerate((v0, v1, v2, v3, v4, v5, v6)):
            VEC[i:i + 1, :] = v[...].astype(f32).reshape(1, C)
        for i in range(4):
            VEC[7 + i:8 + i, :] = v7[C * i:C * (i + 1)].astype(f32).reshape(1, C)
        for j in range(room, NB): load_in(j).start()
        for j in range(4, NB):
            load_in(j).wait()
            load_out(j, stage(j)).start()
    def x_stored():
        for j in range(4, NB): load_out(j, stage(j)).wait()
    def x_attended(): ex["att"].start()
    def x_acts():
        arrived("cot")
        for i in range(4): send_act(i).wait()
    def x_result():
        ex["px0"].start(); ex["px1"].start()
        X[OUT] = (MID[...] + E[0] + vec(6)).astype(bf16)
        pltpu.make_async_copy(X.at[OUT], res.at[0], osem.at[0]).start()
        up_ = X[COT].astype(f32)
        MID[...] = up_
        tally(6, up_)
    def x_px(): arrived("px0", "px1", "two")
    def x_triple():
        ex["qk"].start(); ex["v"].start()
    def x_heads():
        arrived("normed", "att", "br", "v")
        ex["qk"].wait_send(); qk_in().wait_recv()
    def x_merge(): arrived("hid", "skp", "gr")
    def x_outs():
        pltpu.make_async_copy(X.at[OUT], res.at[0], osem.at[0]).wait()
    def x_last():
        outs = [pltpu.make_async_copy(X.at[OUT + i], (hgrad, sgrad)[i].at[0], osem.at[1 + i]) for i in range(2)]
        for cp in outs: cp.start()
        for cp in outs: cp.wait()
    extras = [x_begin, x_stored, x_attended, x_acts, x_result, x_px, x_triple, x_heads, x_merge, x_outs, x_last,
              functools.partial(vstep, 0), functools.partial(vstep, 1), functools.partial(vstep, 2), vline, vend]
    def do_extra(i):
        for k, fn in enumerate(extras):
            @pl.when(i == k)
            def _(): fn()

    def run(n, _):
        code = lookup([op for _, op in OPS], n)
        mode, a, w = code % 16, code // 16 % 64, code // 1024 % 32
        acc, e, wait = code // 2 ** 15 % 2, code // 2 ** 16 % 2, code // 2 ** 17 % 2
        pre, post = code // 2 ** 18 % 32, code // 2 ** 23 % 32
        small = ((do_extra, EXTRA), (do_cast, CAST), (fetch, FETCH), (do_norm, NORM), (do_norm_back, NORM_BACK), (do_gelu, GELU),
                 (do_gelu_back, GELU_BACK), (do_attend, ATTEND), (do_attend_back, ATTEND_BACK), (do_rows, ROWS), (do_full, FULL))
        for dot, m in ((nn, NN), (nt, NT)):
            @pl.when(mode == m)
            def _(): do_matmul(dot, a, w, acc, e, wait, pre, post)
        for fn, m in small:
            @pl.when(mode == m)
            def _(): fn(a)
        return 0

    def tick(t, _):
        @pl.when(t < NB + nz - 2 + 3)
        def _(): gather_tick(t)
        @pl.when(t >= LEAD)
        def _(): sum_tick(t - LEAD)
        lax.fori_loop(lookup(STARTS, t), lookup(STARTS, t + 1), run, 0)
        return 0
    lax.fori_loop(0, LEAD + AHEAD + Q + nz + 3, tick, 0)


def block(hidden, skipped, cotangent, mask, vectors, weights, nz):
    L, C = hidden.shape[1:]
    R = weights[2].shape[0]
    T = R // 2 // SUB
    S = pltpu.SemaphoreType.DMA
    V = pltpu.VMEM
    rows = jax.ShapeDtypeStruct((1, L, C), bf16)
    hbm = pl.BlockSpec(memory_space=pl.ANY)
    out_shape = (rows, rows, rows, jax.ShapeDtypeStruct((NB, R, C), bf16), jax.ShapeDtypeStruct((VR, C), f32),
                 jax.ShapeDtypeStruct((nz, NB, R, C), bf16), jax.ShapeDtypeStruct((nz, NP, R, C), bf16))
    scratch = [
        V((SLOTS, 4, R, C), bf16), V((PLACES, L, C), bf16), V((HEADS, L, L), bf16), V((2, L, C), f32), V((L, C), f32),
        V((2, L, C), f32), V((2, L, 128), f32), V((L, 128), f32), V((VR, C), f32), V((4 * R, C), bf16),
        V(mask.shape, jnp.int32), *[V(v.shape, bf16) for v in vectors],
        V((RING, nz, T, C), bf16), V((RING, nz, T, C), bf16), V((RING, nz + 1, T, C), bf16), V((RING, T, C), bf16), V((RING, T, C), bf16),
        V((6 + nz, VR, C), f32),
        S((NB,)), S((NB,)), S((RING, 2, nz - 1)), S((RING, 2, nz - 1)), S((6, nz)), S((6, nz)), S((6, nz)), S((6, nz)), S((6, nz)), S((6, nz)),
        S((SLOTS, 4)), S((12,)), S((16,)), S((16,)), S((4,)), S((3,)),
        S((nz, RING)), S((nz, RING)), S((nz, RING)), S((nz, RING)), S((nz + 1, RING)), S((RING,)), S((RING,)), S((RING,)), S((RING,)), S((RING,)), S((2, RING)), S((2, RING)),
        S((2,)), S((2 + nz,)), S((2 + nz,)),
    ]
    return pl.pallas_call(
        functools.partial(block_kernel, nz=nz),
        out_shape=out_shape, in_specs=[hbm] * 17, out_specs=(hbm,) * 7, scratch_shapes=scratch,
        compiler_params=pltpu.CompilerParams(collective_id=0, has_side_effects=True, vmem_limit_bytes=63 * 2**20),
    )(hidden, skipped, cotangent, mask, *vectors, *weights)[:5]


def unpack_kernel(F, WV, i0, i1, i2, m, t, o, e, r, o0, o1, o2, *rest):
    vec_outs, (FB, OB, VB, IB), vbufs, (fin, fout, vin, vout, iin, iout) = rest[:8], rest[8:12], rest[12:20], rest[20:]
    R, C = FB.shape[1:]
    outs = block_slices((m, t, o, e, r))
    takes = [pltpu.make_async_copy(F.at[j], FB.at[j], fin.at[j]) for j in range(NB)]
    puts = [pltpu.make_async_copy(OB.at[j], outs[j], fout.at[j]) for j in range(NB)]
    sums = pltpu.make_async_copy(WV, VB, vin.at[0])
    images = [(pltpu.make_async_copy(a, IB.at[i], iin.at[i]), pltpu.make_async_copy(IB.at[i], b, iout.at[i]))
              for i, (a, b) in enumerate(((i0, o0), (i1, o1), (i2, o2)))]
    for cp in takes[:4]: cp.start()
    sums.start()
    for a, _ in images: a.start()
    for cp in takes[4:]: cp.start()
    for j in range(NB):
        takes[j].wait()
        OB[j] = FB[j].astype(f32)
        puts[j].start()
        if j == 3:
            sums.wait()
            for i in range(7): vbufs[i][...] = VB[i:i + 1, :].reshape(C)
            for i in range(4): vbufs[7][C * i:C * (i + 1)] = VB[7 + i:8 + i, :].reshape(C)
            small = [pltpu.make_async_copy(a, b, vout.at[i]) for i, (a, b) in enumerate(zip(vbufs, vec_outs))]
            for cp in small: cp.start()
            for a, b in images:
                a.wait()
                b.start()
    for cp in puts: cp.wait()
    for cp in small: cp.wait()
    for _, b in images: b.wait()


def unpack(images, F, sums):
    R, C = F.shape[1:]
    S = pltpu.SemaphoreType.DMA
    hbm = pl.BlockSpec(memory_space=pl.ANY)
    vecs = [jax.ShapeDtypeStruct((n * C,), f32) for n in (1, 1, 1, 1, 1, 1, 1, 4)]
    shapes = [jax.ShapeDtypeStruct(s, f32) for s in ((2 * R, C), (R, 3 * C), (R, C), (R, 4 * C), (4 * R, C))]
    shapes += [jax.ShapeDtypeStruct(a.shape, a.dtype) for a in images] + vecs
    return pl.pallas_call(
        unpack_kernel, out_shape=shapes, in_specs=[hbm] * 5, out_specs=[hbm] * len(shapes),
        scratch_shapes=[pltpu.VMEM((NB, R, C), bf16), pltpu.VMEM((NB, R, C), f32), pltpu.VMEM(sums.shape, f32),
                        pltpu.VMEM((3,) + images[0].shape, bf16), *[pltpu.VMEM(v.shape, f32) for v in vecs],
                        S((NB,)), S((NB,)), S((1,)), S((8,)), S((3,)), S((3,))],
        compiler_params=pltpu.CompilerParams(vmem_limit_bytes=63 * 2**20),
    )(F, sums, *images)


def pack(m, t, o, e, r):
    R, C = o.shape
    def cut(w):
        a, b = w.shape
        return w.reshape(a // R, R, b // C, C).transpose(0, 2, 1, 3).reshape(-1, R, C)
    return jnp.concatenate([cut(w) for w in (m, t, o, e, r)])


def against(left, right):
    return lax.dot_general(left, right, (((1,), (1,)), ((), ())), preferred_element_type=jnp.float32)


def weight_grad(left, right):
    return lax.dot_general(left, right, (((0,), (0,)), ((), ())), preferred_element_type=jnp.float32)


def norm_parts(v):
    c = v - jnp.mean(v, axis=-1, keepdims=True)
    inv = lax.rsqrt(jnp.mean(c * c, axis=-1, keepdims=True) + EPS)
    return c * inv, inv


def norm_back(e, xhat, inv, gain):
    t = e * gain
    return (t - jnp.mean(t, axis=-1, keepdims=True) - xhat * jnp.mean(t * xhat, axis=-1, keepdims=True)) * inv


def plain(hidden, skipped, row_mask, cotangent, merge_weight, merge_bias, first_gain, first_shift, triple_weight,
         output_weight, output_bias, second_gain, second_shift, expand_weight, expand_bias, reduce_weight, reduce_bias):
    length, D = hidden.shape[1:]
    hs = D // HEADS
    nz = lax.axis_size("seq")
    z = lax.axis_index("seq")
    c = lax.axis_index("dp") % 2
    weights = (merge_weight, triple_weight, output_weight, expand_weight, reduce_weight)
    G = lax.all_gather(pack(*weights), "seq")
    R = G.shape[2]
    merge_full = G[:, 0:2].reshape(2 * D, D)
    triple_full = G[:, 2:5].transpose(1, 0, 2, 3).reshape(3, D, D)
    output_full = G[:, 5].reshape(D, D)
    expand_full = G[:, 6:10].transpose(1, 0, 2, 3).reshape(4, D, D)
    reduce_full = G[:, 10:14].reshape(4 * D, D)
    gain_a, shift_a, gain_b, shift_b = (v.astype(f32) for v in (first_gain, first_shift, second_gain, second_shift))
    joined = jnp.concatenate([hidden[0], skipped[0]], axis=-1)
    merged = jnp.dot(joined, merge_full, preferred_element_type=f32) + merge_bias.astype(f32)
    xhat_a, inv_a = norm_parts(merged)
    normed = (xhat_a * gain_a + shift_a).astype(bf16)
    triple = jnp.einsum("ld,jde->jle", normed, triple_full, preferred_element_type=f32).astype(bf16)
    queries, key_heads, value_heads = (triple[j].reshape(length, HEADS, hs) for j in range(3))
    valid = lax.dynamic_index_in_dim(row_mask, z, 0, False)
    scores = jnp.einsum("qhd,khd->hqk", queries, key_heads, preferred_element_type=f32) * hs ** -0.5
    scores = jnp.where(valid[None, None, :] > 0, scores, NEGATIVE)
    weights_ = jnp.exp(scores - jnp.max(scores, axis=-1, keepdims=True))
    probs = weights_ / jnp.sum(weights_, axis=-1, keepdims=True)
    probs_low = probs.astype(bf16)
    attended = jnp.einsum("hqk,khd->qhd", probs_low, value_heads, preferred_element_type=f32).astype(bf16).reshape(length, D)
    middle = merged + jnp.dot(attended, output_full, preferred_element_type=f32) + output_bias.astype(f32)
    xhat_b, inv_b = norm_parts(middle)
    normed_two = (xhat_b * gain_b + shift_b).astype(bf16)
    expanded = jnp.einsum("ld,jde->jle", normed_two, expand_full, preferred_element_type=f32) + expand_bias.astype(f32).reshape(4, 1, D)
    activated, gelu_back = jax.vjp(functools.partial(jax.nn.gelu, approximate=False), expanded)
    activated = activated.astype(bf16).transpose(1, 0, 2).reshape(length, 4 * D)
    result = middle + jnp.dot(activated, reduce_full, preferred_element_type=f32) + reduce_bias.astype(f32)
    result = result.astype(bf16)
    upstream = cotangent[0]
    wide = upstream.astype(f32)
    activated_grad = jnp.einsum("le,jde->jld", upstream, reduce_full.reshape(4, D, D), preferred_element_type=f32)
    expanded_grad = gelu_back(activated_grad)[0].astype(bf16)
    e_two = jnp.einsum("jle,jde->ld", expanded_grad, expand_full, preferred_element_type=f32)
    middle_grad = wide + norm_back(e_two, xhat_b, inv_b, gain_b)
    branch_grad = middle_grad.astype(bf16)
    attended_grad = against(branch_grad, output_full).astype(bf16).reshape(length, HEADS, hs)
    prob_grad = jnp.einsum("qhd,khd->hqk", attended_grad, value_heads, preferred_element_type=f32)
    values_grad = jnp.einsum("hqk,qhd->khd", probs_low, attended_grad, preferred_element_type=f32)
    score_grad = (probs * (prob_grad - jnp.sum(probs * prob_grad, axis=-1, keepdims=True))).astype(bf16)
    queries_grad = jnp.einsum("hqk,khd->qhd", score_grad, key_heads, preferred_element_type=f32) * hs ** -0.5
    keys_grad = jnp.einsum("hqk,qhd->khd", score_grad, queries, preferred_element_type=f32) * hs ** -0.5
    triple_grad = jnp.stack([g.astype(bf16).reshape(length, D) for g in (queries_grad, keys_grad, values_grad)])
    e_one = jnp.einsum("jle,jde->ld", triple_grad, triple_full, preferred_element_type=f32)
    merged_grad = (middle_grad + norm_back(e_one, xhat_a, inv_a, gain_a)).astype(bf16)
    joined_grad = against(merged_grad, merge_full).astype(bf16)
    vectors = jnp.stack([
        jnp.sum(merged_grad.astype(f32), 0), jnp.sum(e_one * xhat_a, 0), jnp.sum(e_one, 0),
        jnp.sum(branch_grad.astype(f32), 0), jnp.sum(e_two * xhat_b, 0), jnp.sum(e_two, 0), jnp.sum(wide, 0),
    ])
    vectors = jnp.concatenate([vectors, jnp.sum(expanded_grad.astype(f32), 1), jnp.zeros((VR - 11, D), f32)])

    count = lax.axis_size("dp")
    def both(v):
        other = lax.ppermute(v, "dp", [(i, i + 1 - 2 * (i % 2)) for i in range(count)])
        return jnp.concatenate([v, other], axis=-2)
    joined2, normed2, triple2, attended2, branch2, normed_two2, expanded2, activated2, upstream2 = (
        both(v) for v in (joined, normed, triple_grad, attended, branch_grad, normed_two, expanded_grad, activated, upstream))
    def pick(v, axis, index):
        return lax.dynamic_index_in_dim(v, index, axis, False)
    def rows(left, right):
        return jnp.einsum("lsr,le->sre", left, right, preferred_element_type=f32).astype(bf16)
    def split(left):
        return left.reshape(left.shape[0], nz, -1, R)
    parts = [
        rows(pick(split(joined2), 2, c), both(merged_grad)),
        rows(split(normed2)[:, :, 0], pick(triple2, 0, c)),
        rows(split(jnp.where(c == 0, normed2, attended2))[:, :, 0], jnp.where(c == 0, triple2[2], branch2)),
        rows(split(normed_two2)[:, :, 0], pick(expanded2, 0, c)),
        rows(split(normed_two2)[:, :, 0], pick(expanded2, 0, c + 2)),
        rows(pick(split(activated2), 2, c), upstream2),
        rows(pick(split(activated2), 2, c + 2), upstream2),
    ]
    grads = jnp.stack(parts, axis=1)
    wide_grads = jnp.stack([jnp.where(c == i, grads, 0) for i in range(2)], axis=2).reshape(nz, NB, R, D)
    F = lax.psum(lax.psum_scatter(wide_grads, "seq", scatter_dimension=0, tiled=False), "dp")
    vectors = lax.psum(vectors, ("dp", "seq"))
    F = F.astype(f32)
    def columns(blocks):
        return blocks.transpose(1, 0, 2).reshape(R, -1)
    summed = (F[0:2].reshape(-1, D), columns(F[2:5]), F[5], columns(F[6:10]), F[10:14].reshape(-1, D))
    return outputs((result, joined_grad[:, :D], joined_grad[:, D:]), summed, vectors)


def outputs(images, summed, vectors):
    result, hidden_grad, skipped_grad = images
    merge, triple, output, expand, reduce = summed
    return (result[None], hidden_grad[None], skipped_grad[None], merge, vectors[0], vectors[1], vectors[2], triple, output,
            vectors[3], vectors[4], vectors[5], expand, vectors[7:11].reshape(-1), reduce, vectors[6])


def body(hidden, skipped, row_mask, cotangent, merge_weight, merge_bias, first_gain, first_shift, triple_weight,
         output_weight, output_bias, second_gain, second_shift, expand_weight, expand_bias, reduce_weight, reduce_bias):
    vectors = (merge_bias, first_gain, first_shift, output_bias, second_gain, second_shift, reduce_bias, expand_bias)
    weights = (merge_weight, triple_weight, output_weight, expand_weight, reduce_weight)
    *images, F, sums = block(hidden, skipped, cotangent, row_mask, vectors, weights, lax.axis_size("seq"))
    merge, triple, output, expand, reduce, result, hidden_grad, skipped_grad, *v = unpack(images, F, sums)
    return (result, hidden_grad, skipped_grad, merge, v[0], v[1], v[2], triple, output, v[3], v[4], v[5], expand, v[7],
            reduce, v[6])


def solution(mesh):
    rows, held, copied = P(("dp", "seq"), None, None), P("seq", None), P()
    fast = mesh.shape["dp"] == 8 and mesh.shape["seq"] == 4
    return jax.shard_map(
        body if fast else plain,
        mesh=mesh,
        in_specs=(rows, rows, P("dp", None), rows, held, copied, copied, copied, held, held, copied, copied, copied,
                  held, copied, held, copied),
        out_specs=(rows, rows, rows, held, copied, copied, copied, held, held, copied, copied, copied, held, copied,
                   held, copied),
        check_vma=False,
    )
```

```python
import functools

import jax
import jax.numpy as jnp
from jax import lax
from jax.experimental import pallas as pl
from jax.experimental.pallas import tpu as pltpu
from jax.sharding import PartitionSpec as P

MESH = pl.DeviceIdType.MESH
HEADS = 16
EPS = 1e-05
NEGATIVE = -1e30
NB = 14
NP, SUB = 7, 3
Q = NP * SUB
AHEAD = 2
RING = 8
SLOTS = 3
VR = 16
READY = 5
LEAD = READY + 11
f32, bf16 = jnp.float32, jnp.bfloat16


def block_slices(refs):
    merge, triple, output, expand, reduce = refs
    R, C = output.shape
    out = []
    for j in range(merge.shape[0] // R): out.append(merge.at[pl.ds(j * R, R), :])
    for j in range(triple.shape[1] // C): out.append(triple.at[:, pl.ds(j * C, C)])
    out.append(output.at[:, :])
    for j in range(expand.shape[1] // C): out.append(expand.at[:, pl.ds(j * C, C)])
    for j in range(reduce.shape[0] // R): out.append(reduce.at[pl.ds(j * R, R), :])
    return out


def nn(a, b):
    return jnp.dot(a, b, preferred_element_type=f32)


def nt(a, b):
    return lax.dot_general(a, b, (((1,), (1,)), ((), ())), preferred_element_type=f32)


def tn(a, b):
    return lax.dot_general(a, b, (((0,), (0,)), ((), ())), preferred_element_type=f32)


HID, SKP, COT, NORMED, ATT, TWO, ACT, TRI, BR, TG, GR, EXP, ATTG, PLACES = 0, 2, 4, 6, 8, 10, 12, 20, 23, 25, 31, 33, 41, 42
HGRAD, SGRAD, RESULT = NORMED, TWO, ATT
NN, NT, EXTRA, CAST, FETCH, NORM, NORM_BACK, GELU, GELU_BACK, ATTEND, ATTEND_BACK, ROWS, FULL = range(1, 14)


def op(mode, a=0, w=0, acc=0, wait=1, pre=None, post=None):
    pre, post = (0 if v is None else v + 1 for v in (pre, post))
    return mode + 16 * (a + 64 * (w + 32 * (acc + 2 * (wait + 2 * (pre + 32 * post)))))


def plan():
    B = READY
    ops = []
    def at(tick, *what): ops.extend((tick, o) for o in what)
    (begin, stored, cot, attended, acts, pairs, px, triple, heads, merge, joined, result, outs, *sums) = (op(EXTRA, i) for i in range(18))
    at(0, begin)
    at(1, stored)
    at(2, cot)
    at(B + 1, op(FETCH, 0), op(NN, HID, 0, pre=1), op(NN, SKP, 1, acc=1), op(NORM, 0))
    for j in range(3):
        at(B + 2 + j, op(NN, NORMED, 2 + j, pre=2 + j), op(CAST, TRI + j))
    at(B + 4, op(ATTEND, 0), op(ATTEND, 1))
    at(B + 5, op(ATTEND, 2), op(ATTEND, 3), attended, op(NN, ATT, 5, pre=5), op(NORM, 1))
    for i in range(4):
        at(B + 6 + i, op(NN, TWO, 6 + i, pre=6 + i), op(GELU, i))
    at(B + 9, acts, op(ROWS, 0))
    at(B + 11, op(ROWS, 1))
    at(B + 13, op(FETCH, 10), op(FETCH, 11), op(FETCH, 12))
    for i in range(4):
        at(B + 13 + i // 2, op(NT, COT, 10 + i, post=13 + i), op(GELU_BACK, i))
    at(B + 14, pairs)
    at(B + 15, px, op(FULL, 0))
    for i in range(4):
        at(B + 16 + i // 2, op(NT, EXP + 2 * i, 14 + i, acc=int(i > 0), post=17 + i))
    at(B + 17, op(NORM_BACK, 1))
    at(B + 18, op(NT, BR, 18, post=21), op(CAST, ATTG), op(FULL, 1))
    at(B + 19, op(ATTEND_BACK, 0), op(ATTEND_BACK, 1))
    at(B + 20, op(ATTEND_BACK, 2), op(ATTEND_BACK, 3), triple)
    at(B + 21, heads, op(FULL, 2))
    at(B + 22, op(NT, TG, 19, post=22), op(NT, TG + 2, 20, acc=1, post=23))
    at(B + 23, op(NT, TG + 4, 21, acc=1, post=24), op(NORM_BACK, 0))
    at(B + 24, op(FULL, 3))
    at(B + 26, merge, op(ROWS, 2))
    at(B + 26, sums[0], op(NT, GR, 22, post=25), op(CAST, HGRAD))
    at(B + 27, sums[1], op(NT, GR, 23, post=26), op(CAST, SGRAD), joined)
    at(B + 28, sums[2], op(NN, ACT, 24, post=27), op(NN, ACT + 2, 25, acc=1))
    at(B + 29, sums[3], op(NN, ACT + 4, 26, acc=1), op(NN, ACT + 6, 27, acc=1), result)
    at(B + 30, outs)
    at(B + 32, sums[4])
    return ops


OPS = plan()
STARTS = [sum(t < tick for t, _ in OPS) for tick in range(LEAD + AHEAD + Q + 10)]
UNITS = [2, 6] + [4 * j for j in range(2, 10)] + [1 + 4 * s for s in range(4)] + [4 * j for j in (6, 7, 8, 9, 5, 2, 3, 4)] + [2, 6] + [1 + 4 * s for s in range(4)]


def lookup(values, i):
    total = jnp.int32(values[0])
    for k in range(1, len(values)):
        if values[k] != values[k - 1]:
            total = total + jnp.where(i >= k, values[k] - values[k - 1], 0)
    return total


def block_kernel(hid, skp, cot_in, mask_in, *refs, nz):
    (b0, b1, b2, b3, b4, b5, b6, b7, wm, wt, wo, we, wr,
     res, hgrad, sgrad, F, WV, G, D,
     W, X, PR, XH, MID, MG, E, INV, MASK, VEC, DB, MROWS, v0, v1, v2, v3, v4, v5, v6, v7,
     K, R1, R2, R3, O, VB,
     loc, loc2, zs, zr, xs, xr, ys, yr, cs, cr, fsem, insem, es, er, dsem, osem,
     ld, s1, r1, s2, r2, s3, r3, st, sf, rf, sc, rcv, vl, vs, vr) = refs
    dp = lax.axis_index("dp"); z = lax.axis_index("seq")
    c = dp % 2; x = (dp // 2) % 2; y = dp // 4
    xn = dp + 2 - 4 * x; yn = dp + 4 - 8 * y; cn = dp + 1 - 2 * c; co = 1 - c
    L, C = X.shape[1:]
    R = G.shape[2]
    scale = (C // HEADS) ** -0.5
    bar = pltpu.get_barrier_semaphore()
    for tgt in (xn, yn, cn):
        pl.semaphore_signal(bar, inc=1, device_id=(tgt, z), device_id_type=MESH)
    for d in range(1, nz):
        pl.semaphore_signal(bar, inc=1, device_id=(dp, (z + d) % nz), device_id_type=MESH)

    def rc(src, dst, ss, rs, dev):
        return pltpu.make_async_remote_copy(src_ref=src, dst_ref=dst, send_sem=ss, recv_sem=rs, device_id=dev, device_id_type=MESH)

    blocks = block_slices((wm, wt, wo, we, wr))
    room = SLOTS * 4
    def stage(j): return W.at[(j % room) // 4, j % 4]
    def load_in(j): return pltpu.make_async_copy(blocks[j], stage(j), loc.at[j])
    def load_out(j, slot): return pltpu.make_async_copy(slot, G.at[z, j], loc2.at[j])
    for j in range(min(room, NB)): load_in(j).start()
    inputs = [pltpu.make_async_copy(a, b, insem.at[i]) for i, (a, b) in enumerate(
        ((hid.at[0], X.at[HID]), (skp.at[0], X.at[SKP]), (cot_in.at[0], X.at[COT]), (mask_in, MROWS),
         (b0, v0), (b1, v1), (b2, v2), (b3, v3), (b4, v4), (b5, v5), (b6, v6), (b7, v7)))]
    for cp in inputs: cp.start()
    for j in range(4):
        load_in(j).wait()
        load_out(j, stage(j)).start()
    pl.semaphore_wait(bar, nz + 2)

    half = R // 2; third = half // 3
    base = half * c
    zp = ((x + y) % 2) * (2 - x)
    yp = 1 + y
    def reg(s, b, start, n):
        return G.at[s, b, pl.ds(pl.multiple_of(start, 16), n), :]
    def same(region, ss, rs, dev): return rc(region, region, ss, rs, dev)
    def zcopy(b, d, k):
        s = z - k if d == 0 else z + k
        return same(reg(s, b, base + third * zp, third), zs.at[b % RING, d, k], zr.at[b % RING, d, k], (dp, z + 1 if d == 0 else z - 1))
    def zsend_ok(d, k):
        return (z >= k) & (z < nz - 1) if d == 0 else (z + k <= nz - 1) & (z > 0)
    def zrecv_ok(d, k):
        return z >= k + 1 if d == 0 else z + 1 + k <= nz - 1
    def shard_in(d, k):
        return z - 1 - k if d == 0 else z + 1 + k
    def xcopy(b, s): return same(reg(s, b, base + third * zp, third), xs.at[b % 6, s], xr.at[b % 6, s], (xn, z))
    def ycopy(b, s): return same(reg(s, b, base + third * yp, third), ys.at[b % 6, s], yr.at[b % 6, s], (yn, z))
    def ccopy(b, s): return same(reg(s, b, base, half), cs.at[b % 6, s], cr.at[b % 6, s], (cn, z))
    def own(b):
        for d in (0, 1):
            @pl.when(zsend_ok(d, 0))
            def _(): zcopy(b, d, 0).start()
    def zarr(b, d, k):
        zcopy(b, d, k).wait_recv()
        if k + 1 < nz - 1:
            @pl.when(zsend_ok(d, k + 1))
            def _(): zcopy(b, d, k + 1).start()
        s = shard_in(d, k)
        xcopy(b, s).start()
        @pl.when((x + y) % 2 == 1)
        def _(): ycopy(b, s).start()
    def xarr(b, d, k):
        s = shard_in(d, k)
        xcopy(b, s).wait_recv()
        @pl.when((x + y) % 2 == 0)
        def _(): ycopy(b, s).start()
    def yarr(b, d, k):
        s = shard_in(d, k)
        ycopy(b, s).wait_recv()
        ccopy(b, s).start()
    def fin(b, d, k):
        s = shard_in(d, k)
        ccopy(b, s).wait()
        xcopy(b, s).wait_send()
        ycopy(b, s).wait_send()
    for j in range(4):
        load_out(j, stage(j)).wait()
        if j < AHEAD: own(j)
    def gather_tick(t):
        @pl.when(t < NB - AHEAD)
        def _():
            own(t + AHEAD)
        for off, fn in ((0, zarr), (1, xarr), (2, yarr), (3, fin)):
            for k in range(nz - 1):
                b = t - off - k
                @pl.when((b >= 0) & (b < NB))
                def _():
                    for d in (0, 1):
                        @pl.when(zrecv_ok(d, k))
                        def _(): fn(b, d, k)
                        if off == 3:
                            @pl.when(zsend_ok(d, k))
                            def _(): zcopy(b, d, k).wait_send()

    T = K.shape[2]
    def ring(q): return q % RING
    def typ(q, s): return (q + s) % 2
    def keep(q, s): return x + typ(q, s) * (y - x)
    def near(q, s): return xn + typ(q, s) * (yn - xn)
    def far(q, s): return yn + typ(q, s) * (xn - yn)
    def piece(q, h):
        return NP - 1 - q // SUB, pl.ds(pl.multiple_of(half * h + T * (q % SUB), 16), T)
    def load(q, s):
        p, rows = piece(q, keep(q, s))
        return pltpu.make_async_copy(D.at[s, p, rows], K.at[ring(q), s], ld.at[s, ring(q)])
    def first(q, s):
        p, rows = piece(q, 1 - keep(q, s))
        return rc(D.at[s, p, rows], R1.at[ring(q), s], s1.at[s, ring(q)], r1.at[s, ring(q)], (near(q, s), z))
    def up(q, s):
        return rc(K.at[ring(q), s], R2.at[ring(q), s], s2.at[s, ring(q)], r2.at[s, ring(q)], (dp, z + 1))
    def down(q, s):
        away = jnp.minimum(z - 1 - s, 1)
        slot = nz + away * (s - nz)
        return rc(K.at[ring(q), s], R2.at[ring(q), slot], s2.at[s, ring(q)], r2.at[slot, ring(q)], (dp, z - 1))
    def got(slot, q):
        return rc(K.at[ring(q), 0], R2.at[ring(q), slot], s2.at[0, ring(q)], r2.at[slot, ring(q)], (dp, z))
    def last(q):
        return rc(K.at[ring(q), z], R3.at[ring(q)], s3.at[ring(q)], r3.at[ring(q)], (far(q, z), z))
    def frow(q, h, cc):
        p, rows = piece(q, h)
        return F.at[2 * p + cc, rows]
    def keepf(q): return pltpu.make_async_copy(O.at[ring(q)], frow(q, keep(q, z), c), st.at[ring(q)])
    def spread(q): return rc(O.at[ring(q)], frow(q, keep(q, z), c), sf.at[ring(q)], rf.at[ring(q)], (near(q, z), z))
    def spread_in(q):
        r = frow(q, 1 - keep(q, z), c)
        return rc(r, r, sf.at[ring(q)], rf.at[ring(q)], (near(q, z), z))
    def cross(q): return rc(O.at[ring(q)], frow(q, keep(q, z), c), sc.at[0, ring(q)], rcv.at[0, ring(q)], (cn, z))
    def cross2(q):
        r = frow(q, 1 - keep(q, z), c)
        return rc(r, r, sc.at[1, ring(q)], rcv.at[1, ring(q)], (cn, z))
    def add(a, b): return (a.astype(f32) + b.astype(f32)).astype(bf16)
    def issue(q):
        for s in range(nz):
            first(q, s).start(); load(q, s).start()
    def start(q):
        for s in range(nz):
            load(q, s).wait(); first(q, s).wait_recv()
            K[ring(q), s] = add(K[ring(q), s], R1[ring(q), s])
        for s in range(nz):
            if s < nz - 1:
                @pl.when(z == nz - 1)
                def _(): down(q, s).start()
            if nz - 1 - s > 0:
                @pl.when(z == 0)
                def _(): up(q, nz - 1 - s).start()
    def hop(q, k):
        for s in range(nz):
            if s > k:
                @pl.when(z == k)
                def _():
                    got(s, q).wait_recv()
                    K[ring(q), s] = add(K[ring(q), s], R2[ring(q), s])
                    up(q, s).start()
            if s < nz - 1 - k:
                @pl.when(z == nz - 1 - k)
                def _():
                    got(s, q).wait_recv()
                    K[ring(q), s] = add(K[ring(q), s], R2[ring(q), s])
                    down(q, s).start()
    def arrive(q):
        @pl.when(z > 0)
        def _():
            got(z, q).wait_recv()
            K[ring(q), z] = add(K[ring(q), z], R2[ring(q), z])
        @pl.when(z < nz - 1)
        def _():
            got(nz, q).wait_recv()
            K[ring(q), z] = add(K[ring(q), z], R2[ring(q), nz])
        last(q).start()
    def final(q):
        last(q).wait_recv()
        O[ring(q)] = add(K[ring(q), z], R3[ring(q)])
        keepf(q).start(); spread(q).start(); cross(q).start()
    def relay(q):
        spread_in(q).wait_recv()
        cross2(q).start()
        for s in range(nz):
            first(q, s).wait_send()
            if s > 0:
                @pl.when(z < s)
                def _(): up(q, s).wait_send()
            if s < nz - 1:
                @pl.when(z > s)
                def _(): down(q, s).wait_send()
        last(q).wait_send()
    def drain(q):
        keepf(q).wait(); spread(q).wait_send()
        cross(q).wait_send(); cross(q).wait_recv(); cross2(q).wait_send(); cross2(q).wait_recv()
    steps = [(0, start)] + [(k, functools.partial(hop, k=k)) for k in range(1, nz - 1)] + [
        (nz - 1, arrive), (nz, final), (nz + 1, relay), (nz + 3, drain)]
    def sum_tick(t):
        for off, fn in steps:
            q = t - AHEAD - off
            @pl.when((q >= 0) & (q < Q))
            def _(): fn(q)
        @pl.when((t % SUB == 0) & (t < Q))
        def _():
            for cp in puts(NP - 1 - t // SUB): cp.wait()
        @pl.when(t < Q)
        def _(): issue(t)

    devs = ((cn, z), (xn, z), (yn, z))
    def swap(i): return rc(VB.at[2 * i], VB.at[2 * i + 1], vs.at[i], vr.at[i], devs[i])
    def vstep(i):
        if i > 0:
            swap(i - 1).wait()
            VB[2 * i] = VB[2 * i - 2] + VB[2 * i - 1]
        if i < 3:
            swap(i).start()
    def line(d):
        return rc(VB.at[6], VB.at[6 + d], vs.at[2 + d], vr.at[2 + d], (dp, (z + d) % nz))
    def vline():
        vstep(3)
        for d in range(1, nz): line(d).start()
    def vend():
        for d in range(1, nz): line(d).wait()
        def plane(s): return VB[6 + (z - s + nz) % nz]
        total = plane(0)
        for s in range(1, nz): total = total + plane(s)
        VB[0] = total
        cp = pltpu.make_async_copy(VB.at[0], WV, vl.at[1])
        cp.start(); cp.wait()

    def pair(i, src, dst): return rc(src, dst, es.at[i], er.at[i], (cn, z))
    def both(i, a): return pair(i, X.at[a], X.at[a + 1])
    ex = {
        "hid": both(0, HID), "skp": both(1, SKP), "cot": both(2, COT), "normed": both(3, NORMED), "att": both(4, ATT), "two": both(5, TWO),
        "px0": both(10, EXP + 2 * co), "px1": both(11, EXP + 2 * co + 4), "br": both(12, BR),
        "qk": both(13, TG + 2 * co), "v": both(14, TG + 4), "gr": both(15, GR),
    }
    def arrives(i, a): return both(i, a).wait_recv()
    def send_act(i): return both(6 + i, ACT + 2 * i)
    def arrived(*names):
        for n in names: ex[n].wait()

    def fetch(n):
        code = lookup(UNITS, n)
        kind, arg = code % 4, code // 4
        for i in range(4):
            s = jnp.where(kind == 0, i, jnp.where(kind == 1, arg, 2 * arg + i // 2))
            j = jnp.where(kind == 0, arg, jnp.where(kind == 1, 10 + i, i % 2))
            pltpu.make_async_copy(G.at[s, j], W.at[n % SLOTS, i], fsem.at[n % SLOTS, i]).start()
    def fetched(n):
        for i in range(4):
            pltpu.make_async_copy(G.at[0, 0], W.at[n % SLOTS, i], fsem.at[n % SLOTS, i]).wait()
    def weight(n): return W[n % SLOTS].reshape(4 * R, C)
    def vec(i): return VEC[pl.ds(i, 1), :]
    def tally(i, v): VB[0, pl.ds(i, 1), :] = jnp.sum(v, axis=0, keepdims=True)

    def do_matmul(dot, a, n, acc, wait, pre, post):
        @pl.when(pre > 0)
        def _(): fetch(pre - 1)
        @pl.when(wait > 0)
        def _(): fetched(n)
        v = dot(X[a], weight(n))
        E[...] = jnp.where(acc > 0, E[...], 0.0) + v
        @pl.when(post > 0)
        def _(): fetch(post - 1)
    def do_cast(a):
        X[a] = E[...].astype(bf16)
    def do_norm(k):
        v = jnp.where(k > 0, MID[...], 0.0) + E[...] + vec(3 * k)
        MID[...] = v
        m = v - jnp.mean(v, axis=-1, keepdims=True)
        r = lax.rsqrt(jnp.mean(m * m, axis=-1, keepdims=True) + EPS)
        XH[k] = m * r
        INV[k] = jnp.broadcast_to(r, INV.shape[1:])
        a = NORMED + (TWO - NORMED) * k
        X[a] = (m * r * vec(3 * k + 1) + vec(3 * k + 2)).astype(bf16)
        both(3 + 2 * k, a).start()
    def do_norm_back(k):
        e = E[...]
        xhat = XH[k]
        tally(3 * k + 1, e * xhat); tally(3 * k + 2, e)
        t = e * vec(3 * k + 1)
        a = jnp.mean(t, axis=-1, keepdims=True)
        b = jnp.mean(t * xhat, axis=-1, keepdims=True)
        v = jnp.where(k > 0, X[COT].astype(f32), MG[...]) + (t - a - xhat * b) * INV[k, :, 0:1]
        MG[...] = v
        low = v.astype(bf16)
        a = GR + (BR - GR) * k
        X[a] = low
        tally(3 * k, low.astype(f32))
        both(15 - 3 * k, a).start()
    step = C // 3
    def part(n): return pl.ds(pl.multiple_of(step * n, 128), step)
    def do_gelu(i):
        def one(n, _):
            v = E[:, part(n)] + VEC[pl.ds(7 + i, 1), part(n)]
            cdf = 0.5 * (1.0 + lax.erf(v * (0.5 ** 0.5)))
            X[ACT + 2 * i, :, part(n)] = (v * cdf).astype(bf16)
            X[EXP + 2 * i, :, part(n)] = (cdf + v * jnp.exp(-0.5 * v * v) * 0.3989422804014327).astype(bf16)
            return 0
        lax.fori_loop(0, 3, one, 0)
        send_act(i).start()
    def do_gelu_back(i):
        def one(n, _):
            low = (E[:, part(n)] * X[EXP + 2 * i, :, part(n)].astype(f32)).astype(bf16)
            X[EXP + 2 * i, :, part(n)] = low
            VB[0, pl.ds(7 + i, 1), part(n)] = jnp.sum(low.astype(f32), axis=0, keepdims=True)
            return 0
        lax.fori_loop(0, 3, one, 0)
    hs = C // HEADS
    group = HEADS // 4
    def do_attend(i):
        for g in range(4):
            @pl.when(i == g)
            def _():
                for h in range(group * g, group * g + group):
                    sl = slice(hs * h, hs * h + hs)
                    scores = nt(X[TRI + 1, :, sl], X[TRI, :, sl]) * scale
                    scores = jnp.where(MASK[:, 0:1] > 0, scores, NEGATIVE)
                    e = jnp.exp(scores - jnp.max(scores, axis=0, keepdims=True))
                    p = (e * (1.0 / jnp.sum(e, axis=0, keepdims=True))).astype(bf16)
                    PR[h] = p
                    X[ATT, :, sl] = tn(p, X[TRI + 2, :, sl]).astype(bf16)
    def do_attend_back(i):
        for g in range(4):
            @pl.when(i == g)
            def _():
                for h in range(group * g, group * g + group):
                    sl = slice(hs * h, hs * h + hs)
                    q, k, v, d, p = X[TRI, :, sl], X[TRI + 1, :, sl], X[TRI + 2, :, sl], X[ATTG, :, sl], PR[h]
                    X[TG + 4, :, sl] = nn(p, d).astype(bf16)
                    pg = nt(v, d)
                    pf = p.astype(f32)
                    sg = (pf * (pg - jnp.sum(pf * pg, axis=0, keepdims=True))).astype(bf16)
                    X[TG, :, sl] = (tn(sg, k) * scale).astype(bf16)
                    X[TG + 2, :, sl] = (nn(sg, q) * scale).astype(bf16)
    def puts(p): return [pltpu.make_async_copy(DB.at[pl.ds(R * s, R)], D.at[s, p], dsem.at[s]) for s in range(4)]
    def put(p):
        for cp in puts(p): cp.start()
    def pair_of(a, cols=slice(None)): return X[pl.ds(a, 2), :, cols].reshape(2 * L, -1)
    def do_rows(kind):
        merge = kind // 2
        right = COT + (GR - COT) * merge
        def one(s, _):
            left = ACT + 2 * s + merge * (HID + 2 * (s // 2) - ACT - 2 * s)
            cut = merge * (2 * (s % 2)) + (1 - merge) * 2 * (1 - kind) + c
            rows = pl.ds(pl.multiple_of(R * s, 16), R)
            for v in range(4):
                @pl.when(cut == v)
                def _():
                    DB[rows] = tn(pair_of(left, slice(R * v, R * v + R)), pair_of(right)).astype(bf16)
            return 0
        lax.fori_loop(0, 4, one, 0)
        put(6 - kind - 4 * merge)
    def do_full(kind):
        left = jnp.where(kind < 2, TWO, jnp.where(kind == 2, NORMED + (ATT - NORMED) * c, NORMED))
        right = jnp.where(kind < 2, EXP + 2 * c + 4 * (1 - kind), jnp.where(kind == 2, TG + 4 + (BR - TG - 4) * c, TG + 2 * c))
        def one(n, _):
            DB[pl.ds(pl.multiple_of(step * n, 128), step)] = tn(pair_of(left, part(n)), pair_of(right)).astype(bf16)
            return 0
        lax.fori_loop(0, 3, one, 0)
        put(4 - kind)

    def x_begin():
        VB[0] = jnp.zeros_like(VB[0])
        for cp in inputs: cp.wait()
        for n in ("hid", "skp", "cot"): ex[n].start()
        valid = MROWS[pl.ds(z, 1), :].astype(f32)
        MASK[...] = jnp.broadcast_to(valid, (MASK.shape[1], L)).T
        for i, v in enumerate((v0, v1, v2, v3, v4, v5, v6)):
            VEC[i:i + 1, :] = v[...].astype(f32).reshape(1, C)
        for i in range(4):
            VEC[7 + i:8 + i, :] = v7[C * i:C * (i + 1)].astype(f32).reshape(1, C)
        for j in range(room, NB): load_in(j).start()
        for j in range(4, NB):
            load_in(j).wait()
            load_out(j, stage(j)).start()
    def x_stored():
        for j in range(4, NB): load_out(j, stage(j)).wait()
    def x_attended(): ex["att"].start()
    def x_acts():
        arrived("cot")
        for i in range(4): send_act(i).wait()
    def x_cot(): tally(6, X[COT].astype(f32))
    def x_pairs():
        ex["px0"].start(); ex["px1"].start()
    def out(i):
        return pltpu.make_async_copy(X.at[(RESULT, HGRAD, SGRAD)[i]], (res, hgrad, sgrad)[i].at[0], osem.at[i])
    def x_result():
        X[RESULT] = (MID[...] + E[...] + vec(6)).astype(bf16)
        out(0).start()
    def x_joined():
        out(1).start(); out(2).start()
    def x_outs():
        for i in range(3): out(i).wait()
    def x_px():
        arrived("two")
        for i in range(2):
            ex["px" + str(i)].wait_send(); arrives(10 + i, EXP + 2 * c + 4 * i)
    def x_triple():
        ex["qk"].start(); ex["v"].start()
    def x_heads():
        arrived("normed", "att", "br", "v")
        ex["qk"].wait_send(); arrives(13, TG + 2 * c)
    def x_merge(): arrived("hid", "skp", "gr")
    extras = [x_begin, x_stored, x_cot, x_attended, x_acts, x_pairs, x_px, x_triple, x_heads, x_merge, x_joined, x_result, x_outs,
              functools.partial(vstep, 0), functools.partial(vstep, 1), functools.partial(vstep, 2), vline, vend]
    def do_extra(i):
        for k, fn in enumerate(extras):
            @pl.when(i == k)
            def _(): fn()

    def run(n, _):
        code = lookup([op for _, op in OPS], n)
        mode, a, w = code % 16, code // 16 % 64, code // 1024 % 32
        acc, wait = code // 2 ** 15 % 2, code // 2 ** 16 % 2
        pre, post = code // 2 ** 17 % 32, code // 2 ** 22 % 32
        small = ((do_extra, EXTRA), (do_cast, CAST), (fetch, FETCH), (do_norm, NORM), (do_norm_back, NORM_BACK), (do_gelu, GELU),
                 (do_gelu_back, GELU_BACK), (do_attend, ATTEND), (do_attend_back, ATTEND_BACK), (do_rows, ROWS), (do_full, FULL))
        for dot, m in ((nn, NN), (nt, NT)):
            @pl.when(mode == m)
            def _(): do_matmul(dot, a, w, acc, wait, pre, post)
        for fn, m in small:
            @pl.when(mode == m)
            def _(): fn(a)
        return 0

    def tick(t, _):
        @pl.when(t < NB + nz - 2 + 3)
        def _(): gather_tick(t)
        @pl.when(t >= LEAD)
        def _(): sum_tick(t - LEAD)
        lax.fori_loop(lookup(STARTS, t), lookup(STARTS, t + 1), run, 0)
        return 0
    lax.fori_loop(0, LEAD + AHEAD + Q + nz + 3, tick, 0)


def block(hidden, skipped, cotangent, mask, vectors, weights, nz):
    L, C = hidden.shape[1:]
    R = weights[2].shape[0]
    T = R // 2 // SUB
    S = pltpu.SemaphoreType.DMA
    V = pltpu.VMEM
    rows = jax.ShapeDtypeStruct((1, L, C), bf16)
    hbm = pl.BlockSpec(memory_space=pl.ANY)
    out_shape = (rows, rows, rows, jax.ShapeDtypeStruct((NB, R, C), bf16), jax.ShapeDtypeStruct((VR, C), f32),
                 jax.ShapeDtypeStruct((nz, NB, R, C), bf16), jax.ShapeDtypeStruct((nz, NP, R, C), bf16))
    scratch = [
        V((SLOTS, 4, R, C), bf16), V((PLACES, L, C), bf16), V((HEADS, L, L), bf16), V((2, L, C), f32), V((L, C), f32), V((L, C), f32),
        V((L, C), f32), V((2, L, 128), f32), V((L, 128), f32), V((VR, C), f32), V((4 * R, C), bf16),
        V(mask.shape, jnp.int32), *[V(v.shape, bf16) for v in vectors],
        V((RING, nz, T, C), bf16), V((RING, nz, T, C), bf16), V((RING, nz + 1, T, C), bf16), V((RING, T, C), bf16), V((RING, T, C), bf16),
        V((6 + nz, VR, C), f32),
        S((NB,)), S((NB,)), S((RING, 2, nz - 1)), S((RING, 2, nz - 1)), S((6, nz)), S((6, nz)), S((6, nz)), S((6, nz)), S((6, nz)), S((6, nz)),
        S((SLOTS, 4)), S((12,)), S((16,)), S((16,)), S((4,)), S((3,)),
        S((nz, RING)), S((nz, RING)), S((nz, RING)), S((nz, RING)), S((nz + 1, RING)), S((RING,)), S((RING,)), S((RING,)), S((RING,)), S((RING,)), S((2, RING)), S((2, RING)),
        S((2,)), S((2 + nz,)), S((2 + nz,)),
    ]
    return pl.pallas_call(
        functools.partial(block_kernel, nz=nz),
        out_shape=out_shape, in_specs=[hbm] * 17, out_specs=(hbm,) * 7, scratch_shapes=scratch,
        compiler_params=pltpu.CompilerParams(collective_id=0, has_side_effects=True, vmem_limit_bytes=63 * 2**20),
    )(hidden, skipped, cotangent, mask, *vectors, *weights)[:5]


def unpack_kernel(F, WV, i0, i1, i2, m, t, o, e, r, o0, o1, o2, *rest):
    vec_outs, (FB, OB, VB, IB), vbufs, (fin, fout, vin, vout, iin, iout) = rest[:8], rest[8:12], rest[12:20], rest[20:]
    R, C = FB.shape[1:]
    outs = block_slices((m, t, o, e, r))
    takes = [pltpu.make_async_copy(F.at[j], FB.at[j], fin.at[j]) for j in range(NB)]
    puts = [pltpu.make_async_copy(OB.at[j], outs[j], fout.at[j]) for j in range(NB)]
    sums = pltpu.make_async_copy(WV, VB, vin.at[0])
    images = [(pltpu.make_async_copy(a, IB.at[i], iin.at[i]), pltpu.make_async_copy(IB.at[i], b, iout.at[i]))
              for i, (a, b) in enumerate(((i0, o0), (i1, o1), (i2, o2)))]
    for cp in takes[:4]: cp.start()
    sums.start()
    for a, _ in images: a.start()
    for cp in takes[4:]: cp.start()
    for j in range(NB):
        takes[j].wait()
        OB[j] = FB[j].astype(f32)
        puts[j].start()
        if j == 3:
            sums.wait()
            for i in range(7): vbufs[i][...] = VB[i:i + 1, :].reshape(C)
            for i in range(4): vbufs[7][C * i:C * (i + 1)] = VB[7 + i:8 + i, :].reshape(C)
            small = [pltpu.make_async_copy(a, b, vout.at[i]) for i, (a, b) in enumerate(zip(vbufs, vec_outs))]
            for cp in small: cp.start()
            for a, b in images:
                a.wait()
                b.start()
    for cp in puts: cp.wait()
    for cp in small: cp.wait()
    for _, b in images: b.wait()


def unpack(images, F, sums):
    R, C = F.shape[1:]
    S = pltpu.SemaphoreType.DMA
    hbm = pl.BlockSpec(memory_space=pl.ANY)
    vecs = [jax.ShapeDtypeStruct((n * C,), f32) for n in (1, 1, 1, 1, 1, 1, 1, 4)]
    shapes = [jax.ShapeDtypeStruct(s, f32) for s in ((2 * R, C), (R, 3 * C), (R, C), (R, 4 * C), (4 * R, C))]
    shapes += [jax.ShapeDtypeStruct(a.shape, a.dtype) for a in images] + vecs
    return pl.pallas_call(
        unpack_kernel, out_shape=shapes, in_specs=[hbm] * 5, out_specs=[hbm] * len(shapes),
        scratch_shapes=[pltpu.VMEM((NB, R, C), bf16), pltpu.VMEM((NB, R, C), f32), pltpu.VMEM(sums.shape, f32),
                        pltpu.VMEM((3,) + images[0].shape, bf16), *[pltpu.VMEM(v.shape, f32) for v in vecs],
                        S((NB,)), S((NB,)), S((1,)), S((8,)), S((3,)), S((3,))],
        compiler_params=pltpu.CompilerParams(vmem_limit_bytes=63 * 2**20),
    )(F, sums, *images)


def pack(m, t, o, e, r):
    R, C = o.shape
    def cut(w):
        a, b = w.shape
        return w.reshape(a // R, R, b // C, C).transpose(0, 2, 1, 3).reshape(-1, R, C)
    return jnp.concatenate([cut(w) for w in (m, t, o, e, r)])


def against(left, right):
    return lax.dot_general(left, right, (((1,), (1,)), ((), ())), preferred_element_type=jnp.float32)


def weight_grad(left, right):
    return lax.dot_general(left, right, (((0,), (0,)), ((), ())), preferred_element_type=jnp.float32)


def norm_parts(v):
    c = v - jnp.mean(v, axis=-1, keepdims=True)
    inv = lax.rsqrt(jnp.mean(c * c, axis=-1, keepdims=True) + EPS)
    return c * inv, inv


def norm_back(e, xhat, inv, gain):
    t = e * gain
    return (t - jnp.mean(t, axis=-1, keepdims=True) - xhat * jnp.mean(t * xhat, axis=-1, keepdims=True)) * inv


def plain(hidden, skipped, row_mask, cotangent, merge_weight, merge_bias, first_gain, first_shift, triple_weight,
         output_weight, output_bias, second_gain, second_shift, expand_weight, expand_bias, reduce_weight, reduce_bias):
    length, D = hidden.shape[1:]
    hs = D // HEADS
    nz = lax.axis_size("seq")
    z = lax.axis_index("seq")
    c = lax.axis_index("dp") % 2
    weights = (merge_weight, triple_weight, output_weight, expand_weight, reduce_weight)
    G = lax.all_gather(pack(*weights), "seq")
    R = G.shape[2]
    merge_full = G[:, 0:2].reshape(2 * D, D)
    triple_full = G[:, 2:5].transpose(1, 0, 2, 3).reshape(3, D, D)
    output_full = G[:, 5].reshape(D, D)
    expand_full = G[:, 6:10].transpose(1, 0, 2, 3).reshape(4, D, D)
    reduce_full = G[:, 10:14].reshape(4 * D, D)
    gain_a, shift_a, gain_b, shift_b = (v.astype(f32) for v in (first_gain, first_shift, second_gain, second_shift))
    joined = jnp.concatenate([hidden[0], skipped[0]], axis=-1)
    merged = jnp.dot(joined, merge_full, preferred_element_type=f32) + merge_bias.astype(f32)
    xhat_a, inv_a = norm_parts(merged)
    normed = (xhat_a * gain_a + shift_a).astype(bf16)
    triple = jnp.einsum("ld,jde->jle", normed, triple_full, preferred_element_type=f32).astype(bf16)
    queries, key_heads, value_heads = (triple[j].reshape(length, HEADS, hs) for j in range(3))
    valid = lax.dynamic_index_in_dim(row_mask, z, 0, False)
    scores = jnp.einsum("qhd,khd->hqk", queries, key_heads, preferred_element_type=f32) * hs ** -0.5
    scores = jnp.where(valid[None, None, :] > 0, scores, NEGATIVE)
    weights_ = jnp.exp(scores - jnp.max(scores, axis=-1, keepdims=True))
    probs = weights_ / jnp.sum(weights_, axis=-1, keepdims=True)
    probs_low = probs.astype(bf16)
    attended = jnp.einsum("hqk,khd->qhd", probs_low, value_heads, preferred_element_type=f32).astype(bf16).reshape(length, D)
    middle = merged + jnp.dot(attended, output_full, preferred_element_type=f32) + output_bias.astype(f32)
    xhat_b, inv_b = norm_parts(middle)
    normed_two = (xhat_b * gain_b + shift_b).astype(bf16)
    expanded = jnp.einsum("ld,jde->jle", normed_two, expand_full, preferred_element_type=f32) + expand_bias.astype(f32).reshape(4, 1, D)
    activated, gelu_back = jax.vjp(functools.partial(jax.nn.gelu, approximate=False), expanded)
    activated = activated.astype(bf16).transpose(1, 0, 2).reshape(length, 4 * D)
    result = middle + jnp.dot(activated, reduce_full, preferred_element_type=f32) + reduce_bias.astype(f32)
    result = result.astype(bf16)
    upstream = cotangent[0]
    wide = upstream.astype(f32)
    activated_grad = jnp.einsum("le,jde->jld", upstream, reduce_full.reshape(4, D, D), preferred_element_type=f32)
    expanded_grad = gelu_back(activated_grad)[0].astype(bf16)
    e_two = jnp.einsum("jle,jde->ld", expanded_grad, expand_full, preferred_element_type=f32)
    middle_grad = wide + norm_back(e_two, xhat_b, inv_b, gain_b)
    branch_grad = middle_grad.astype(bf16)
    attended_grad = against(branch_grad, output_full).astype(bf16).reshape(length, HEADS, hs)
    prob_grad = jnp.einsum("qhd,khd->hqk", attended_grad, value_heads, preferred_element_type=f32)
    values_grad = jnp.einsum("hqk,qhd->khd", probs_low, attended_grad, preferred_element_type=f32)
    score_grad = (probs * (prob_grad - jnp.sum(probs * prob_grad, axis=-1, keepdims=True))).astype(bf16)
    queries_grad = jnp.einsum("hqk,khd->qhd", score_grad, key_heads, preferred_element_type=f32) * hs ** -0.5
    keys_grad = jnp.einsum("hqk,qhd->khd", score_grad, queries, preferred_element_type=f32) * hs ** -0.5
    triple_grad = jnp.stack([g.astype(bf16).reshape(length, D) for g in (queries_grad, keys_grad, values_grad)])
    e_one = jnp.einsum("jle,jde->ld", triple_grad, triple_full, preferred_element_type=f32)
    merged_grad = (middle_grad + norm_back(e_one, xhat_a, inv_a, gain_a)).astype(bf16)
    joined_grad = against(merged_grad, merge_full).astype(bf16)
    vectors = jnp.stack([
        jnp.sum(merged_grad.astype(f32), 0), jnp.sum(e_one * xhat_a, 0), jnp.sum(e_one, 0),
        jnp.sum(branch_grad.astype(f32), 0), jnp.sum(e_two * xhat_b, 0), jnp.sum(e_two, 0), jnp.sum(wide, 0),
    ])
    vectors = jnp.concatenate([vectors, jnp.sum(expanded_grad.astype(f32), 1), jnp.zeros((VR - 11, D), f32)])

    count = lax.axis_size("dp")
    def both(v):
        other = lax.ppermute(v, "dp", [(i, i + 1 - 2 * (i % 2)) for i in range(count)])
        return jnp.concatenate([v, other], axis=-2)
    joined2, normed2, triple2, attended2, branch2, normed_two2, expanded2, activated2, upstream2 = (
        both(v) for v in (joined, normed, triple_grad, attended, branch_grad, normed_two, expanded_grad, activated, upstream))
    def pick(v, axis, index):
        return lax.dynamic_index_in_dim(v, index, axis, False)
    def rows(left, right):
        return jnp.einsum("lsr,le->sre", left, right, preferred_element_type=f32).astype(bf16)
    def split(left):
        return left.reshape(left.shape[0], nz, -1, R)
    parts = [
        rows(pick(split(joined2), 2, c), both(merged_grad)),
        rows(split(normed2)[:, :, 0], pick(triple2, 0, c)),
        rows(split(jnp.where(c == 0, normed2, attended2))[:, :, 0], jnp.where(c == 0, triple2[2], branch2)),
        rows(split(normed_two2)[:, :, 0], pick(expanded2, 0, c)),
        rows(split(normed_two2)[:, :, 0], pick(expanded2, 0, c + 2)),
        rows(pick(split(activated2), 2, c), upstream2),
        rows(pick(split(activated2), 2, c + 2), upstream2),
    ]
    grads = jnp.stack(parts, axis=1)
    wide_grads = jnp.stack([jnp.where(c == i, grads, 0) for i in range(2)], axis=2).reshape(nz, NB, R, D)
    F = lax.psum(lax.psum_scatter(wide_grads, "seq", scatter_dimension=0, tiled=False), "dp")
    vectors = lax.psum(vectors, ("dp", "seq"))
    F = F.astype(f32)
    def columns(blocks):
        return blocks.transpose(1, 0, 2).reshape(R, -1)
    summed = (F[0:2].reshape(-1, D), columns(F[2:5]), F[5], columns(F[6:10]), F[10:14].reshape(-1, D))
    return outputs((result, joined_grad[:, :D], joined_grad[:, D:]), summed, vectors)


def outputs(images, summed, vectors):
    result, hidden_grad, skipped_grad = images
    merge, triple, output, expand, reduce = summed
    return (result[None], hidden_grad[None], skipped_grad[None], merge, vectors[0], vectors[1], vectors[2], triple, output,
            vectors[3], vectors[4], vectors[5], expand, vectors[7:11].reshape(-1), reduce, vectors[6])


def body(hidden, skipped, row_mask, cotangent, merge_weight, merge_bias, first_gain, first_shift, triple_weight,
         output_weight, output_bias, second_gain, second_shift, expand_weight, expand_bias, reduce_weight, reduce_bias):
    vectors = (merge_bias, first_gain, first_shift, output_bias, second_gain, second_shift, reduce_bias, expand_bias)
    weights = (merge_weight, triple_weight, output_weight, expand_weight, reduce_weight)
    *images, F, sums = block(hidden, skipped, cotangent, row_mask, vectors, weights, lax.axis_size("seq"))
    merge, triple, output, expand, reduce, result, hidden_grad, skipped_grad, *v = unpack(images, F, sums)
    return (result, hidden_grad, skipped_grad, merge, v[0], v[1], v[2], triple, output, v[3], v[4], v[5], expand, v[7],
            reduce, v[6])


def solution(mesh):
    rows, held, copied = P(("dp", "seq"), None, None), P("seq", None), P()
    fast = mesh.shape["dp"] == 8 and mesh.shape["seq"] == 4
    return jax.shard_map(
        body if fast else plain,
        mesh=mesh,
        in_specs=(rows, rows, P("dp", None), rows, held, copied, copied, copied, held, held, copied, copied, copied,
                  held, copied, held, copied),
        out_specs=(rows, rows, rows, held, copied, copied, copied, held, held, copied, copied, copied, held, copied,
                   held, copied),
        check_vma=False,
    )
```

```python
import functools

import jax
import jax.numpy as jnp
from jax import lax
from jax.experimental import pallas as pl
from jax.experimental.pallas import tpu as pltpu
from jax.sharding import PartitionSpec as P

MESH = pl.DeviceIdType.MESH
HEADS = 16
EPS = 1e-05
NEGATIVE = -1e30
NB = 14
NP, SUB = 7, 3
Q = NP * SUB
AHEAD = 2
RING = 8
SLOTS = 3
VR = 16
READY = 5
LEAD = READY + 9
f32, bf16 = jnp.float32, jnp.bfloat16


def block_slices(refs):
    merge, triple, output, expand, reduce = refs
    R, C = output.shape
    out = []
    for j in range(merge.shape[0] // R): out.append(merge.at[pl.ds(j * R, R), :])
    for j in range(triple.shape[1] // C): out.append(triple.at[:, pl.ds(j * C, C)])
    out.append(output.at[:, :])
    for j in range(expand.shape[1] // C): out.append(expand.at[:, pl.ds(j * C, C)])
    for j in range(reduce.shape[0] // R): out.append(reduce.at[pl.ds(j * R, R), :])
    return out


def nn(a, b):
    return jnp.dot(a, b, preferred_element_type=f32)


def nt(a, b):
    return lax.dot_general(a, b, (((1,), (1,)), ((), ())), preferred_element_type=f32)


def tn(a, b):
    return lax.dot_general(a, b, (((0,), (0,)), ((), ())), preferred_element_type=f32)


HID, SKP, COT, NORMED, ATT, TWO, ACT, TRI, BR, TG, GR, EXP, ATTG, PLACES = 0, 2, 4, 6, 8, 10, 12, 20, 23, 25, 31, 33, 41, 42
HGRAD, SGRAD, RESULT = NORMED, TWO, ATT
NN, NT, EXTRA, CAST, FETCH, NORM, NORM_BACK, GELU, GELU_BACK, ATTEND, ATTEND_BACK, ROWS, FULL = range(1, 14)


def op(mode, a=0, w=0, acc=0, wait=1, pre=None, post=None):
    pre, post = (0 if v is None else v + 1 for v in (pre, post))
    return mode + 16 * (a + 64 * (w + 32 * (acc + 2 * (wait + 2 * (pre + 32 * post)))))


def plan():
    B = READY
    ops = []
    def at(tick, *what): ops.extend((tick, o) for o in what)
    (begin, stored, cot, attended, acts, pairs, px, triple, heads, merge, joined, result, outs, *sums) = (op(EXTRA, i) for i in range(18))
    at(0, begin)
    at(1, stored)
    at(2, cot)
    at(B + 1, op(FETCH, 0), op(NN, HID, 0, pre=1), op(NN, SKP, 1, acc=1), op(NORM, 0))
    for j in range(3):
        at(B + 2 + j, op(NN, NORMED, 2 + j, pre=2 + j), op(CAST, TRI + j))
    at(B + 4, op(ATTEND, 0))
    at(B + 5, op(ATTEND, 1), op(ATTEND, 2))
    at(B + 6, op(ATTEND, 3), attended, op(NN, ATT, 5, pre=5), op(NORM, 1))
    at(B + 7, op(NN, TWO, 6, pre=6), op(GELU, 0), op(NN, TWO, 7, pre=7), op(GELU, 1))
    at(B + 8, acts, op(ROWS, 0), op(NN, TWO, 8, pre=8), op(GELU, 2), op(ROWS, 4))
    at(B + 9, op(NN, TWO, 9, pre=9), op(GELU, 3), op(ROWS, 8), op(ROWS, 12))
    at(B + 11, op(ROWS, 1))
    at(B + 13, op(FETCH, 10), op(FETCH, 11), op(FETCH, 12))
    for i in range(4):
        at(B + 13, op(NT, COT, 10 + i, post=13 + i), op(GELU_BACK, i))
    at(B + 14, pairs, px, op(FULL, 0))
    for i in range(4):
        at(B + 15 + i // 2, op(NT, EXP + 2 * i, 14 + i, acc=int(i > 0), post=17 + i))
    at(B + 16, op(NORM_BACK, 1))
    at(B + 17, op(NT, BR, 18, post=21), op(CAST, ATTG), op(FULL, 1))
    at(B + 18, op(ATTEND_BACK, 0), op(ATTEND_BACK, 1))
    at(B + 19, op(ATTEND_BACK, 2), op(ATTEND_BACK, 3), triple)
    at(B + 20, heads, op(FULL, 2))
    at(B + 21, op(NT, TG, 19, post=22), op(NT, TG + 2, 20, acc=1, post=23))
    at(B + 22, op(NT, TG + 4, 21, acc=1, post=24), op(NORM_BACK, 0))
    at(B + 23, op(FULL, 3))
    at(B + 24, merge, op(ROWS, 2))
    at(B + 25, sums[0], op(NT, GR, 22, post=25), op(CAST, HGRAD))
    at(B + 26, sums[1], op(NT, GR, 23, post=26), op(CAST, SGRAD), joined)
    at(B + 27, sums[2], op(NN, ACT, 24, post=27), op(NN, ACT + 2, 25, acc=1))
    at(B + 28, sums[3], op(NN, ACT + 4, 26, acc=1), op(NN, ACT + 6, 27, acc=1), result)
    at(B + 29, outs)
    at(B + 32, sums[4])
    spread = []
    for tick in sorted({t for t, _ in ops}):
        mine = [o for t, o in ops if t == tick]
        spread += [(2 * tick + 1 + 2 * i // len(mine), o) for i, o in enumerate(mine)]
    return spread


OPS = plan()
STARTS = [sum(t < half for t, _ in OPS) for half in range(2 * (LEAD + AHEAD + Q + 10))]
UNITS = [2, 6] + [4 * j for j in range(2, 10)] + [1 + 4 * s for s in range(4)] + [4 * j for j in (6, 7, 8, 9, 5, 2, 3, 4)] + [2, 6] + [1 + 4 * s for s in range(4)]


def lookup(values, i):
    total = jnp.int32(values[0])
    for k in range(1, len(values)):
        if values[k] != values[k - 1]:
            total = total + jnp.where(i >= k, values[k] - values[k - 1], 0)
    return total


def block_kernel(hid, skp, cot_in, mask_in, *refs, nz):
    (b0, b1, b2, b3, b4, b5, b6, b7, wm, wt, wo, we, wr,
     res, hgrad, sgrad, F, WV, G, D,
     W, X, PR, XH, MID, MG, E, INV, MASK, VEC, DB, MROWS, v0, v1, v2, v3, v4, v5, v6, v7,
     K, R1, R2, R3, O, VB,
     loc, loc2, zs, zr, xs, xr, ys, yr, cs, cr, fsem, insem, es, er, dsem, osem,
     ld, s1, r1, s2, r2, s3, r3, st, sf, rf, sc, rcv, vl, vs, vr) = refs
    dp = lax.axis_index("dp"); z = lax.axis_index("seq")
    c = dp % 2; x = (dp // 2) % 2; y = dp // 4
    xn = dp + 2 - 4 * x; yn = dp + 4 - 8 * y; cn = dp + 1 - 2 * c; co = 1 - c
    L, C = X.shape[1:]
    R = G.shape[2]
    scale = (C // HEADS) ** -0.5
    bar = pltpu.get_barrier_semaphore()
    for tgt in (xn, yn, cn):
        pl.semaphore_signal(bar, inc=1, device_id=(tgt, z), device_id_type=MESH)
    for d in range(1, nz):
        pl.semaphore_signal(bar, inc=1, device_id=(dp, (z + d) % nz), device_id_type=MESH)

    def rc(src, dst, ss, rs, dev):
        return pltpu.make_async_remote_copy(src_ref=src, dst_ref=dst, send_sem=ss, recv_sem=rs, device_id=dev, device_id_type=MESH)

    blocks = block_slices((wm, wt, wo, we, wr))
    room = SLOTS * 4
    def stage(j): return W.at[(j % room) // 4, j % 4]
    def load_in(j): return pltpu.make_async_copy(blocks[j], stage(j), loc.at[j])
    def load_out(j, slot): return pltpu.make_async_copy(slot, G.at[z, j], loc2.at[j])
    for j in range(min(room, NB)): load_in(j).start()
    inputs = [pltpu.make_async_copy(a, b, insem.at[i]) for i, (a, b) in enumerate(
        ((hid.at[0], X.at[HID]), (skp.at[0], X.at[SKP]), (cot_in.at[0], X.at[COT]), (mask_in, MROWS),
         (b0, v0), (b1, v1), (b2, v2), (b3, v3), (b4, v4), (b5, v5), (b6, v6), (b7, v7)))]
    for cp in inputs: cp.start()
    pl.semaphore_wait(bar, nz + 2)

    half = R // 2; third = half // 3
    base = half * c
    zp = ((x + y) % 2) * (2 - x)
    yp = 1 + y
    def reg(s, b, start, n):
        return G.at[s, b, pl.ds(pl.multiple_of(start, 16), n), :]
    def same(region, ss, rs, dev): return rc(region, region, ss, rs, dev)
    def zcopy(b, d, k):
        s = z - k if d == 0 else z + k
        return same(reg(s, b, base + third * zp, third), zs.at[b % RING, d, k], zr.at[b % RING, d, k], (dp, z + 1 if d == 0 else z - 1))
    def zsend_ok(d, k):
        return (z >= k) & (z < nz - 1) if d == 0 else (z + k <= nz - 1) & (z > 0)
    def zrecv_ok(d, k):
        return z >= k + 1 if d == 0 else z + 1 + k <= nz - 1
    def shard_in(d, k):
        return z - 1 - k if d == 0 else z + 1 + k
    def xcopy(b, s): return same(reg(s, b, base + third * zp, third), xs.at[b % 6, s], xr.at[b % 6, s], (xn, z))
    def ycopy(b, s): return same(reg(s, b, base + third * yp, third), ys.at[b % 6, s], yr.at[b % 6, s], (yn, z))
    def ccopy(b, s): return same(reg(s, b, base, half), cs.at[b % 6, s], cr.at[b % 6, s], (cn, z))
    def own(b):
        for d in (0, 1):
            @pl.when(zsend_ok(d, 0))
            def _(): zcopy(b, d, 0).start()
    def zarr(b, d, k):
        zcopy(b, d, k).wait_recv()
        if k + 1 < nz - 1:
            @pl.when(zsend_ok(d, k + 1))
            def _(): zcopy(b, d, k + 1).start()
        s = shard_in(d, k)
        xcopy(b, s).start()
        @pl.when((x + y) % 2 == 1)
        def _(): ycopy(b, s).start()
    def xarr(b, d, k):
        s = shard_in(d, k)
        xcopy(b, s).wait_recv()
        @pl.when((x + y) % 2 == 0)
        def _(): ycopy(b, s).start()
    def yarr(b, d, k):
        s = shard_in(d, k)
        ycopy(b, s).wait_recv()
        ccopy(b, s).start()
    def fin(b, d, k):
        s = shard_in(d, k)
        ccopy(b, s).wait()
        xcopy(b, s).wait_send()
        ycopy(b, s).wait_send()
    for j in range(AHEAD):
        for d in (0, 1):
            @pl.when(zsend_ok(d, 0))
            def _():
                rc(blocks[j].at[pl.ds(pl.multiple_of(base + third * zp, 16), third)], reg(z, j, base + third * zp, third),
                   zs.at[j, d, 0], zr.at[j, d, 0], (dp, z + 1 if d == 0 else z - 1)).start()
    for j in range(4):
        load_in(j).wait()
        load_out(j, stage(j)).start()
    for j in range(4): load_out(j, stage(j)).wait()
    FIRST = [(zarr, 0, 0), (zarr, 0, 1), (zarr, 0, 2), (None, 0, 0)]
    SECOND = [(xarr, 1, k) for k in range(3)] + [(yarr, 2, k) for k in range(3)] + [(fin, 3, k) for k in range(3)]
    def gather_half(t, todo):
        for fn, off, k in todo:
            if fn is None:
                @pl.when(t < NB - AHEAD)
                def _(): own(t + AHEAD)
                continue
            b = t - off - k
            @pl.when((b >= 0) & (b < NB))
            def _():
                for d in (0, 1):
                    @pl.when(zrecv_ok(d, k))
                    def _(): fn(b, d, k)
                    if fn is fin:
                        @pl.when(zsend_ok(d, k))
                        def _(): zcopy(b, d, k).wait_send()

    T = K.shape[2]
    def ring(q): return q % RING
    def typ(q, s): return (q + s) % 2
    def keep(q, s): return x + typ(q, s) * (y - x)
    def near(q, s): return xn + typ(q, s) * (yn - xn)
    def far(q, s): return yn + typ(q, s) * (xn - yn)
    def piece(q, h):
        return NP - 1 - q // SUB, pl.ds(pl.multiple_of(half * h + T * (q % SUB), 16), T)
    def load(q, s):
        p, rows = piece(q, keep(q, s))
        return pltpu.make_async_copy(D.at[s, p, rows], K.at[ring(q), s], ld.at[s, ring(q)])
    def first(q, s):
        p, rows = piece(q, 1 - keep(q, s))
        return rc(D.at[s, p, rows], R1.at[ring(q), s], s1.at[s, ring(q)], r1.at[s, ring(q)], (near(q, s), z))
    def up(q, s):
        return rc(K.at[ring(q), s], R2.at[ring(q), s], s2.at[s, ring(q)], r2.at[s, ring(q)], (dp, z + 1))
    def down(q, s):
        away = jnp.minimum(z - 1 - s, 1)
        slot = nz + away * (s - nz)
        return rc(K.at[ring(q), s], R2.at[ring(q), slot], s2.at[s, ring(q)], r2.at[slot, ring(q)], (dp, z - 1))
    def got(slot, q):
        return rc(K.at[ring(q), 0], R2.at[ring(q), slot], s2.at[0, ring(q)], r2.at[slot, ring(q)], (dp, z))
    def last(q):
        return rc(K.at[ring(q), z], R3.at[ring(q)], s3.at[ring(q)], r3.at[ring(q)], (far(q, z), z))
    def frow(q, h, cc):
        p, rows = piece(q, h)
        return F.at[2 * p + cc, rows]
    def keepf(q): return pltpu.make_async_copy(O.at[ring(q)], frow(q, keep(q, z), c), st.at[ring(q)])
    def spread(q): return rc(O.at[ring(q)], frow(q, keep(q, z), c), sf.at[ring(q)], rf.at[ring(q)], (near(q, z), z))
    def spread_in(q):
        r = frow(q, 1 - keep(q, z), c)
        return rc(r, r, sf.at[ring(q)], rf.at[ring(q)], (near(q, z), z))
    def cross(q): return rc(O.at[ring(q)], frow(q, keep(q, z), c), sc.at[0, ring(q)], rcv.at[0, ring(q)], (cn, z))
    def cross2(q):
        r = frow(q, 1 - keep(q, z), c)
        return rc(r, r, sc.at[1, ring(q)], rcv.at[1, ring(q)], (cn, z))
    def add(a, b): return (a.astype(f32) + b.astype(f32)).astype(bf16)
    def issue(q):
        for s in range(nz):
            first(q, s).start(); load(q, s).start()
    def start(q):
        for s in range(nz):
            load(q, s).wait(); first(q, s).wait_recv()
            K[ring(q), s] = add(K[ring(q), s], R1[ring(q), s])
        for s in range(nz):
            if s < nz - 1:
                @pl.when(z == nz - 1)
                def _(): down(q, s).start()
            if nz - 1 - s > 0:
                @pl.when(z == 0)
                def _(): up(q, nz - 1 - s).start()
    def hop(q, k):
        for s in range(nz):
            if s > k:
                @pl.when(z == k)
                def _():
                    got(s, q).wait_recv()
                    K[ring(q), s] = add(K[ring(q), s], R2[ring(q), s])
                    up(q, s).start()
            if s < nz - 1 - k:
                @pl.when(z == nz - 1 - k)
                def _():
                    got(s, q).wait_recv()
                    K[ring(q), s] = add(K[ring(q), s], R2[ring(q), s])
                    down(q, s).start()
    def arrive(q):
        @pl.when(z > 0)
        def _():
            got(z, q).wait_recv()
            K[ring(q), z] = add(K[ring(q), z], R2[ring(q), z])
        @pl.when(z < nz - 1)
        def _():
            got(nz, q).wait_recv()
            K[ring(q), z] = add(K[ring(q), z], R2[ring(q), nz])
        last(q).start()
    def final(q):
        last(q).wait_recv()
        O[ring(q)] = add(K[ring(q), z], R3[ring(q)])
        keepf(q).start(); spread(q).start(); cross(q).start()
    def relay(q):
        spread_in(q).wait_recv()
        cross2(q).start()
        for s in range(nz):
            first(q, s).wait_send()
            if s > 0:
                @pl.when(z < s)
                def _(): up(q, s).wait_send()
            if s < nz - 1:
                @pl.when(z > s)
                def _(): down(q, s).wait_send()
        last(q).wait_send()
    def drain(q):
        keepf(q).wait(); spread(q).wait_send()
        cross(q).wait_send(); cross(q).wait_recv(); cross2(q).wait_send(); cross2(q).wait_recv()
    steps = [(0, start)] + [(k, functools.partial(hop, k=k)) for k in range(1, nz - 1)] + [
        (nz - 1, arrive), (nz, final), (nz + 1, relay), (nz + 3, drain)]
    def sum_half(t, todo):
        for off, fn in todo:
            q = t - AHEAD - off
            @pl.when((q >= 0) & (q < Q))
            def _(): fn(q)
    def sum_issue(t):
        @pl.when(((t % SUB == 0) & (t > 0) & (t < Q)) | (t == 1))
        def _():
            for cp in puts(NP - 1 - t // SUB): cp.wait()
        @pl.when(t == 1)
        def _(): issue(0)
        @pl.when((t > 0) & (t < Q))
        def _(): issue(t)

    devs = ((cn, z), (xn, z), (yn, z))
    def swap(i): return rc(VB.at[2 * i], VB.at[2 * i + 1], vs.at[i], vr.at[i], devs[i])
    def vstep(i):
        if i > 0:
            swap(i - 1).wait()
            VB[2 * i] = VB[2 * i - 2] + VB[2 * i - 1]
        if i < 3:
            swap(i).start()
    def line(d):
        return rc(VB.at[6], VB.at[6 + d], vs.at[2 + d], vr.at[2 + d], (dp, (z + d) % nz))
    def vline():
        vstep(3)
        for d in range(1, nz): line(d).start()
    def vend():
        for d in range(1, nz): line(d).wait()
        def plane(s): return VB[6 + (z - s + nz) % nz]
        total = plane(0)
        for s in range(1, nz): total = total + plane(s)
        VB[0] = total
        cp = pltpu.make_async_copy(VB.at[0], WV, vl.at[1])
        cp.start(); cp.wait()

    def pair(i, src, dst): return rc(src, dst, es.at[i], er.at[i], (cn, z))
    def both(i, a): return pair(i, X.at[a], X.at[a + 1])
    ex = {
        "hid": both(0, HID), "skp": both(1, SKP), "cot": both(2, COT), "normed": both(3, NORMED), "att": both(4, ATT), "two": both(5, TWO),
        "px0": both(10, EXP + 2 * co), "px1": both(11, EXP + 2 * co + 4), "br": both(12, BR),
        "qk": both(13, TG + 2 * co), "v": both(14, TG + 4), "gr": both(15, GR),
    }
    def arrives(i, a): return both(i, a).wait_recv()
    def send_act(i): return both(6 + i, ACT + 2 * i)
    def arrived(*names):
        for n in names: ex[n].wait()

    def fetch(n):
        code = lookup(UNITS, n)
        kind, arg = code % 4, code // 4
        for i in range(4):
            s = jnp.where(kind == 0, i, jnp.where(kind == 1, arg, 2 * arg + i // 2))
            j = jnp.where(kind == 0, arg, jnp.where(kind == 1, 10 + i, i % 2))
            pltpu.make_async_copy(G.at[s, j], W.at[n % SLOTS, i], fsem.at[n % SLOTS, i]).start()
    def fetched(n):
        for i in range(4):
            pltpu.make_async_copy(G.at[0, 0], W.at[n % SLOTS, i], fsem.at[n % SLOTS, i]).wait()
    def weight(n): return W[n % SLOTS].reshape(4 * R, C)
    def vec(i): return VEC[pl.ds(i, 1), :]
    def tally(i, v): VB[0, pl.ds(i, 1), :] = jnp.sum(v, axis=0, keepdims=True)

    def do_matmul(dot, a, n, acc, wait, pre, post):
        @pl.when(pre > 0)
        def _(): fetch(pre - 1)
        @pl.when(wait > 0)
        def _(): fetched(n)
        v = dot(X[a], weight(n))
        E[...] = jnp.where(acc > 0, E[...], 0.0) + v
        @pl.when(post > 0)
        def _(): fetch(post - 1)
    def do_cast(a):
        X[a] = E[...].astype(bf16)
    def do_norm(k):
        v = jnp.where(k > 0, MID[...], 0.0) + E[...] + vec(3 * k)
        MID[...] = v
        m = v - jnp.mean(v, axis=-1, keepdims=True)
        r = lax.rsqrt(jnp.mean(m * m, axis=-1, keepdims=True) + EPS)
        XH[k] = m * r
        INV[k] = jnp.broadcast_to(r, INV.shape[1:])
        a = NORMED + (TWO - NORMED) * k
        X[a] = (m * r * vec(3 * k + 1) + vec(3 * k + 2)).astype(bf16)
        both(3 + 2 * k, a).start()
    def do_norm_back(k):
        e = E[...]
        xhat = XH[k]
        tally(3 * k + 1, e * xhat); tally(3 * k + 2, e)
        t = e * vec(3 * k + 1)
        a = jnp.mean(t, axis=-1, keepdims=True)
        b = jnp.mean(t * xhat, axis=-1, keepdims=True)
        v = jnp.where(k > 0, X[COT].astype(f32), MG[...]) + (t - a - xhat * b) * INV[k, :, 0:1]
        MG[...] = v
        low = v.astype(bf16)
        a = GR + (BR - GR) * k
        X[a] = low
        tally(3 * k, low.astype(f32))
        both(15 - 3 * k, a).start()
    step = C // 3
    def part(n): return pl.ds(pl.multiple_of(step * n, 128), step)
    def do_gelu(i):
        def one(n, _):
            v = E[:, part(n)] + VEC[pl.ds(7 + i, 1), part(n)]
            cdf = 0.5 * (1.0 + lax.erf(v * (0.5 ** 0.5)))
            X[ACT + 2 * i, :, part(n)] = (v * cdf).astype(bf16)
            X[EXP + 2 * i, :, part(n)] = (cdf + v * jnp.exp(-0.5 * v * v) * 0.3989422804014327).astype(bf16)
            return 0
        lax.fori_loop(0, 3, one, 0)
        send_act(i).start()
    def do_gelu_back(i):
        def one(n, _):
            low = (E[:, part(n)] * X[EXP + 2 * i, :, part(n)].astype(f32)).astype(bf16)
            X[EXP + 2 * i, :, part(n)] = low
            VB[0, pl.ds(7 + i, 1), part(n)] = jnp.sum(low.astype(f32), axis=0, keepdims=True)
            return 0
        lax.fori_loop(0, 3, one, 0)
    hs = C // HEADS
    group = HEADS // 4
    def do_attend(i):
        for g in range(4):
            @pl.when(i == g)
            def _():
                for h in range(group * g, group * g + group):
                    sl = slice(hs * h, hs * h + hs)
                    scores = nt(X[TRI + 1, :, sl], X[TRI, :, sl]) * scale
                    scores = jnp.where(MASK[:, 0:1] > 0, scores, NEGATIVE)
                    e = jnp.exp(scores - jnp.max(scores, axis=0, keepdims=True))
                    p = (e * (1.0 / jnp.sum(e, axis=0, keepdims=True))).astype(bf16)
                    PR[h] = p
                    X[ATT, :, sl] = tn(p, X[TRI + 2, :, sl]).astype(bf16)
    def do_attend_back(i):
        for g in range(4):
            @pl.when(i == g)
            def _():
                for h in range(group * g, group * g + group):
                    sl = slice(hs * h, hs * h + hs)
                    q, k, v, d, p = X[TRI, :, sl], X[TRI + 1, :, sl], X[TRI + 2, :, sl], X[ATTG, :, sl], PR[h]
                    X[TG + 4, :, sl] = nn(p, d).astype(bf16)
                    pg = nt(v, d)
                    pf = p.astype(f32)
                    sg = (pf * (pg - jnp.sum(pf * pg, axis=0, keepdims=True))).astype(bf16)
                    X[TG, :, sl] = (tn(sg, k) * scale).astype(bf16)
                    X[TG + 2, :, sl] = (nn(sg, q) * scale).astype(bf16)
    def puts(p): return [pltpu.make_async_copy(DB.at[pl.ds(R * s, R)], D.at[s, p], dsem.at[s]) for s in range(4)]
    def put(p):
        for cp in puts(p): cp.start()
    def pair_of(a, cols=slice(None)): return X[pl.ds(a, 2), :, cols].reshape(2 * L, -1)
    def do_rows(a):
        kind = a % 4
        merge = kind // 2
        lo = a // 4
        hi = jnp.where(kind == 0, lo + 1, 4)
        @pl.when(kind == 0)
        def _(): send_act(lo).wait()
        right = COT + (GR - COT) * merge
        def one(s, _):
            left = ACT + 2 * s + merge * (HID + 2 * (s // 2) - ACT - 2 * s)
            cut = merge * (2 * (s % 2)) + (1 - merge) * 2 * (1 - kind) + c
            rows = pl.ds(pl.multiple_of(R * s, 16), R)
            for v in range(4):
                @pl.when(cut == v)
                def _():
                    DB[rows] = tn(pair_of(left, slice(R * v, R * v + R)), pair_of(right)).astype(bf16)
            pltpu.make_async_copy(DB.at[rows], D.at[s, 6 - kind - 4 * merge], dsem.at[s]).start()
            return 0
        lax.fori_loop(lo, hi, one, 0)
    def do_full(kind):
        left = jnp.where(kind < 2, TWO, jnp.where(kind == 2, NORMED + (ATT - NORMED) * c, NORMED))
        right = jnp.where(kind < 2, EXP + 2 * c + 4 * (1 - kind), jnp.where(kind == 2, TG + 4 + (BR - TG - 4) * c, TG + 2 * c))
        def one(n, _):
            DB[pl.ds(pl.multiple_of(step * n, 128), step)] = tn(pair_of(left, part(n)), pair_of(right)).astype(bf16)
            return 0
        lax.fori_loop(0, 3, one, 0)
        put(4 - kind)

    def x_begin():
        VB[0] = jnp.zeros_like(VB[0])
        for cp in inputs: cp.wait()
        for n in ("hid", "skp", "cot"): ex[n].start()
        valid = MROWS[pl.ds(z, 1), :].astype(f32)
        MASK[...] = jnp.broadcast_to(valid, (MASK.shape[1], L)).T
        for i, v in enumerate((v0, v1, v2, v3, v4, v5, v6)):
            VEC[i:i + 1, :] = v[...].astype(f32).reshape(1, C)
        for i in range(4):
            VEC[7 + i:8 + i, :] = v7[C * i:C * (i + 1)].astype(f32).reshape(1, C)
        for j in range(room, NB): load_in(j).start()
        for j in range(4, NB):
            load_in(j).wait()
            load_out(j, stage(j)).start()
    def x_stored():
        for j in range(4, NB): load_out(j, stage(j)).wait()
    def x_attended(): ex["att"].start()
    def x_acts():
        arrived("cot")
    def x_cot(): tally(6, X[COT].astype(f32))
    def x_pairs():
        ex["px0"].start(); ex["px1"].start()
    def out(i):
        return pltpu.make_async_copy(X.at[(RESULT, HGRAD, SGRAD)[i]], (res, hgrad, sgrad)[i].at[0], osem.at[i])
    def x_result():
        X[RESULT] = (MID[...] + E[...] + vec(6)).astype(bf16)
        out(0).start()
    def x_joined():
        out(1).start(); out(2).start()
    def x_outs():
        for i in range(3): out(i).wait()
    def x_px():
        arrived("two")
        for i in range(2):
            ex["px" + str(i)].wait_send(); arrives(10 + i, EXP + 2 * c + 4 * i)
    def x_triple():
        ex["qk"].start(); ex["v"].start()
    def x_heads():
        arrived("normed", "att", "br", "v")
        ex["qk"].wait_send(); arrives(13, TG + 2 * c)
    def x_merge(): arrived("hid", "skp", "gr")
    extras = [x_begin, x_stored, x_cot, x_attended, x_acts, x_pairs, x_px, x_triple, x_heads, x_merge, x_joined, x_result, x_outs,
              functools.partial(vstep, 0), functools.partial(vstep, 1), functools.partial(vstep, 2), vline, vend]
    def do_extra(i):
        for k, fn in enumerate(extras):
            @pl.when(i == k)
            def _(): fn()

    def run(n, _):
        code = lookup([op for _, op in OPS], n)
        mode, a, w = code % 16, code // 16 % 64, code // 1024 % 32
        acc, wait = code // 2 ** 15 % 2, code // 2 ** 16 % 2
        pre, post = code // 2 ** 17 % 32, code // 2 ** 22 % 32
        small = ((do_extra, EXTRA), (do_cast, CAST), (fetch, FETCH), (do_norm, NORM), (do_norm_back, NORM_BACK), (do_gelu, GELU),
                 (do_gelu_back, GELU_BACK), (do_attend, ATTEND), (do_attend_back, ATTEND_BACK), (do_rows, ROWS), (do_full, FULL))
        for dot, m in ((nn, NN), (nt, NT)):
            @pl.when(mode == m)
            def _(): do_matmul(dot, a, w, acc, wait, pre, post)
        for fn, m in small:
            @pl.when(mode == m)
            def _(): fn(a)
        return 0

    cut = nz - 1
    def tick(h, _):
        t = h // 2
        @pl.when((h % 2 == 0) & (t < NB + nz + 2))
        def _(): gather_half(t, FIRST)
        @pl.when((h % 2 == 1) & (t < NB + nz + 2))
        def _(): gather_half(t, SECOND)
        @pl.when((h % 2 == 0) & (t >= LEAD))
        def _(): sum_half(t - LEAD, steps[:cut])
        @pl.when((h % 2 == 1) & (t >= LEAD))
        def _():
            sum_half(t - LEAD, steps[cut:])
            sum_issue(t - LEAD)
        lax.fori_loop(lookup(STARTS, h), lookup(STARTS, h + 1), run, 0)
        return 0
    lax.fori_loop(0, 2 * (LEAD + AHEAD + Q + nz + 3), tick, 0)


def block(hidden, skipped, cotangent, mask, vectors, weights, nz):
    L, C = hidden.shape[1:]
    R = weights[2].shape[0]
    T = R // 2 // SUB
    S = pltpu.SemaphoreType.DMA
    V = pltpu.VMEM
    rows = jax.ShapeDtypeStruct((1, L, C), bf16)
    hbm = pl.BlockSpec(memory_space=pl.ANY)
    out_shape = (rows, rows, rows, jax.ShapeDtypeStruct((NB, R, C), bf16), jax.ShapeDtypeStruct((VR, C), f32),
                 jax.ShapeDtypeStruct((nz, NB, R, C), bf16), jax.ShapeDtypeStruct((nz, NP, R, C), bf16))
    scratch = [
        V((SLOTS, 4, R, C), bf16), V((PLACES, L, C), bf16), V((HEADS, L, L), bf16), V((2, L, C), f32), V((L, C), f32), V((L, C), f32),
        V((L, C), f32), V((2, L, 128), f32), V((L, 128), f32), V((VR, C), f32), V((4 * R, C), bf16),
        V(mask.shape, jnp.int32), *[V(v.shape, bf16) for v in vectors],
        V((RING, nz, T, C), bf16), V((RING, nz, T, C), bf16), V((RING, nz + 1, T, C), bf16), V((RING, T, C), bf16), V((RING, T, C), bf16),
        V((6 + nz, VR, C), f32),
        S((NB,)), S((NB,)), S((RING, 2, nz - 1)), S((RING, 2, nz - 1)), S((6, nz)), S((6, nz)), S((6, nz)), S((6, nz)), S((6, nz)), S((6, nz)),
        S((SLOTS, 4)), S((12,)), S((16,)), S((16,)), S((4,)), S((3,)),
        S((nz, RING)), S((nz, RING)), S((nz, RING)), S((nz, RING)), S((nz + 1, RING)), S((RING,)), S((RING,)), S((RING,)), S((RING,)), S((RING,)), S((2, RING)), S((2, RING)),
        S((2,)), S((2 + nz,)), S((2 + nz,)),
    ]
    return pl.pallas_call(
        functools.partial(block_kernel, nz=nz),
        out_shape=out_shape, in_specs=[hbm] * 17, out_specs=(hbm,) * 7, scratch_shapes=scratch,
        compiler_params=pltpu.CompilerParams(collective_id=0, has_side_effects=True, vmem_limit_bytes=63 * 2**20),
    )(hidden, skipped, cotangent, mask, *vectors, *weights)[:5]


def unpack_kernel(F, WV, i0, i1, i2, m, t, o, e, r, o0, o1, o2, *rest):
    vec_outs, (FB, OB, VB, IB), vbufs, (fin, fout, vin, vout, iin, iout) = rest[:8], rest[8:12], rest[12:20], rest[20:]
    R, C = FB.shape[1:]
    outs = block_slices((m, t, o, e, r))
    takes = [pltpu.make_async_copy(F.at[j], FB.at[j], fin.at[j]) for j in range(NB)]
    puts = [pltpu.make_async_copy(OB.at[j], outs[j], fout.at[j]) for j in range(NB)]
    sums = pltpu.make_async_copy(WV, VB, vin.at[0])
    images = [(pltpu.make_async_copy(a, IB.at[i], iin.at[i]), pltpu.make_async_copy(IB.at[i], b, iout.at[i]))
              for i, (a, b) in enumerate(((i0, o0), (i1, o1), (i2, o2)))]
    for cp in takes[:4]: cp.start()
    sums.start()
    for a, _ in images: a.start()
    for cp in takes[4:]: cp.start()
    for j in range(NB):
        takes[j].wait()
        def widen(i, _):
            part = pl.ds(pl.multiple_of(i * 32, 16), 32)
            OB[j, part] = FB[j, part].astype(f32)
            return 0
        lax.fori_loop(0, R // 32, widen, 0)
        puts[j].start()
        if j == 3:
            sums.wait()
            for i in range(7): vbufs[i][...] = VB[i:i + 1, :].reshape(C)
            for i in range(4): vbufs[7][C * i:C * (i + 1)] = VB[7 + i:8 + i, :].reshape(C)
            small = [pltpu.make_async_copy(a, b, vout.at[i]) for i, (a, b) in enumerate(zip(vbufs, vec_outs))]
            for cp in small: cp.start()
            for a, b in images:
                a.wait()
                b.start()
    for cp in puts: cp.wait()
    for cp in small: cp.wait()
    for _, b in images: b.wait()


def unpack(images, F, sums):
    R, C = F.shape[1:]
    S = pltpu.SemaphoreType.DMA
    hbm = pl.BlockSpec(memory_space=pl.ANY)
    vecs = [jax.ShapeDtypeStruct((n * C,), f32) for n in (1, 1, 1, 1, 1, 1, 1, 4)]
    shapes = [jax.ShapeDtypeStruct(s, f32) for s in ((2 * R, C), (R, 3 * C), (R, C), (R, 4 * C), (4 * R, C))]
    shapes += [jax.ShapeDtypeStruct(a.shape, a.dtype) for a in images] + vecs
    return pl.pallas_call(
        unpack_kernel, out_shape=shapes, in_specs=[hbm] * 5, out_specs=[hbm] * len(shapes),
        scratch_shapes=[pltpu.VMEM((NB, R, C), bf16), pltpu.VMEM((NB, R, C), f32), pltpu.VMEM(sums.shape, f32),
                        pltpu.VMEM((3,) + images[0].shape, bf16), *[pltpu.VMEM(v.shape, f32) for v in vecs],
                        S((NB,)), S((NB,)), S((1,)), S((8,)), S((3,)), S((3,))],
        compiler_params=pltpu.CompilerParams(vmem_limit_bytes=63 * 2**20),
    )(F, sums, *images)


def pack(m, t, o, e, r):
    R, C = o.shape
    def cut(w):
        a, b = w.shape
        return w.reshape(a // R, R, b // C, C).transpose(0, 2, 1, 3).reshape(-1, R, C)
    return jnp.concatenate([cut(w) for w in (m, t, o, e, r)])


def against(left, right):
    return lax.dot_general(left, right, (((1,), (1,)), ((), ())), preferred_element_type=jnp.float32)


def weight_grad(left, right):
    return lax.dot_general(left, right, (((0,), (0,)), ((), ())), preferred_element_type=jnp.float32)


def norm_parts(v):
    c = v - jnp.mean(v, axis=-1, keepdims=True)
    inv = lax.rsqrt(jnp.mean(c * c, axis=-1, keepdims=True) + EPS)
    return c * inv, inv


def norm_back(e, xhat, inv, gain):
    t = e * gain
    return (t - jnp.mean(t, axis=-1, keepdims=True) - xhat * jnp.mean(t * xhat, axis=-1, keepdims=True)) * inv


def plain(hidden, skipped, row_mask, cotangent, merge_weight, merge_bias, first_gain, first_shift, triple_weight,
         output_weight, output_bias, second_gain, second_shift, expand_weight, expand_bias, reduce_weight, reduce_bias):
    length, D = hidden.shape[1:]
    hs = D // HEADS
    nz = lax.axis_size("seq")
    z = lax.axis_index("seq")
    c = lax.axis_index("dp") % 2
    weights = (merge_weight, triple_weight, output_weight, expand_weight, reduce_weight)
    G = lax.all_gather(pack(*weights), "seq")
    R = G.shape[2]
    merge_full = G[:, 0:2].reshape(2 * D, D)
    triple_full = G[:, 2:5].transpose(1, 0, 2, 3).reshape(3, D, D)
    output_full = G[:, 5].reshape(D, D)
    expand_full = G[:, 6:10].transpose(1, 0, 2, 3).reshape(4, D, D)
    reduce_full = G[:, 10:14].reshape(4 * D, D)
    gain_a, shift_a, gain_b, shift_b = (v.astype(f32) for v in (first_gain, first_shift, second_gain, second_shift))
    joined = jnp.concatenate([hidden[0], skipped[0]], axis=-1)
    merged = jnp.dot(joined, merge_full, preferred_element_type=f32) + merge_bias.astype(f32)
    xhat_a, inv_a = norm_parts(merged)
    normed = (xhat_a * gain_a + shift_a).astype(bf16)
    triple = jnp.einsum("ld,jde->jle", normed, triple_full, preferred_element_type=f32).astype(bf16)
    queries, key_heads, value_heads = (triple[j].reshape(length, HEADS, hs) for j in range(3))
    valid = lax.dynamic_index_in_dim(row_mask, z, 0, False)
    scores = jnp.einsum("qhd,khd->hqk", queries, key_heads, preferred_element_type=f32) * hs ** -0.5
    scores = jnp.where(valid[None, None, :] > 0, scores, NEGATIVE)
    weights_ = jnp.exp(scores - jnp.max(scores, axis=-1, keepdims=True))
    probs = weights_ / jnp.sum(weights_, axis=-1, keepdims=True)
    probs_low = probs.astype(bf16)
    attended = jnp.einsum("hqk,khd->qhd", probs_low, value_heads, preferred_element_type=f32).astype(bf16).reshape(length, D)
    middle = merged + jnp.dot(attended, output_full, preferred_element_type=f32) + output_bias.astype(f32)
    xhat_b, inv_b = norm_parts(middle)
    normed_two = (xhat_b * gain_b + shift_b).astype(bf16)
    expanded = jnp.einsum("ld,jde->jle", normed_two, expand_full, preferred_element_type=f32) + expand_bias.astype(f32).reshape(4, 1, D)
    activated, gelu_back = jax.vjp(functools.partial(jax.nn.gelu, approximate=False), expanded)
    activated = activated.astype(bf16).transpose(1, 0, 2).reshape(length, 4 * D)
    result = middle + jnp.dot(activated, reduce_full, preferred_element_type=f32) + reduce_bias.astype(f32)
    result = result.astype(bf16)
    upstream = cotangent[0]
    wide = upstream.astype(f32)
    activated_grad = jnp.einsum("le,jde->jld", upstream, reduce_full.reshape(4, D, D), preferred_element_type=f32)
    expanded_grad = gelu_back(activated_grad)[0].astype(bf16)
    e_two = jnp.einsum("jle,jde->ld", expanded_grad, expand_full, preferred_element_type=f32)
    middle_grad = wide + norm_back(e_two, xhat_b, inv_b, gain_b)
    branch_grad = middle_grad.astype(bf16)
    attended_grad = against(branch_grad, output_full).astype(bf16).reshape(length, HEADS, hs)
    prob_grad = jnp.einsum("qhd,khd->hqk", attended_grad, value_heads, preferred_element_type=f32)
    values_grad = jnp.einsum("hqk,qhd->khd", probs_low, attended_grad, preferred_element_type=f32)
    score_grad = (probs * (prob_grad - jnp.sum(probs * prob_grad, axis=-1, keepdims=True))).astype(bf16)
    queries_grad = jnp.einsum("hqk,khd->qhd", score_grad, key_heads, preferred_element_type=f32) * hs ** -0.5
    keys_grad = jnp.einsum("hqk,qhd->khd", score_grad, queries, preferred_element_type=f32) * hs ** -0.5
    triple_grad = jnp.stack([g.astype(bf16).reshape(length, D) for g in (queries_grad, keys_grad, values_grad)])
    e_one = jnp.einsum("jle,jde->ld", triple_grad, triple_full, preferred_element_type=f32)
    merged_grad = (middle_grad + norm_back(e_one, xhat_a, inv_a, gain_a)).astype(bf16)
    joined_grad = against(merged_grad, merge_full).astype(bf16)
    vectors = jnp.stack([
        jnp.sum(merged_grad.astype(f32), 0), jnp.sum(e_one * xhat_a, 0), jnp.sum(e_one, 0),
        jnp.sum(branch_grad.astype(f32), 0), jnp.sum(e_two * xhat_b, 0), jnp.sum(e_two, 0), jnp.sum(wide, 0),
    ])
    vectors = jnp.concatenate([vectors, jnp.sum(expanded_grad.astype(f32), 1), jnp.zeros((VR - 11, D), f32)])

    count = lax.axis_size("dp")
    def both(v):
        other = lax.ppermute(v, "dp", [(i, i + 1 - 2 * (i % 2)) for i in range(count)])
        return jnp.concatenate([v, other], axis=-2)
    joined2, normed2, triple2, attended2, branch2, normed_two2, expanded2, activated2, upstream2 = (
        both(v) for v in (joined, normed, triple_grad, attended, branch_grad, normed_two, expanded_grad, activated, upstream))
    def pick(v, axis, index):
        return lax.dynamic_index_in_dim(v, index, axis, False)
    def rows(left, right):
        return jnp.einsum("lsr,le->sre", left, right, preferred_element_type=f32).astype(bf16)
    def split(left):
        return left.reshape(left.shape[0], nz, -1, R)
    parts = [
        rows(pick(split(joined2), 2, c), both(merged_grad)),
        rows(split(normed2)[:, :, 0], pick(triple2, 0, c)),
        rows(split(jnp.where(c == 0, normed2, attended2))[:, :, 0], jnp.where(c == 0, triple2[2], branch2)),
        rows(split(normed_two2)[:, :, 0], pick(expanded2, 0, c)),
        rows(split(normed_two2)[:, :, 0], pick(expanded2, 0, c + 2)),
        rows(pick(split(activated2), 2, c), upstream2),
        rows(pick(split(activated2), 2, c + 2), upstream2),
    ]
    grads = jnp.stack(parts, axis=1)
    wide_grads = jnp.stack([jnp.where(c == i, grads, 0) for i in range(2)], axis=2).reshape(nz, NB, R, D)
    F = lax.psum(lax.psum_scatter(wide_grads, "seq", scatter_dimension=0, tiled=False), "dp")
    vectors = lax.psum(vectors, ("dp", "seq"))
    F = F.astype(f32)
    def columns(blocks):
        return blocks.transpose(1, 0, 2).reshape(R, -1)
    summed = (F[0:2].reshape(-1, D), columns(F[2:5]), F[5], columns(F[6:10]), F[10:14].reshape(-1, D))
    return outputs((result, joined_grad[:, :D], joined_grad[:, D:]), summed, vectors)


def outputs(images, summed, vectors):
    result, hidden_grad, skipped_grad = images
    merge, triple, output, expand, reduce = summed
    return (result[None], hidden_grad[None], skipped_grad[None], merge, vectors[0], vectors[1], vectors[2], triple, output,
            vectors[3], vectors[4], vectors[5], expand, vectors[7:11].reshape(-1), reduce, vectors[6])


def body(hidden, skipped, row_mask, cotangent, merge_weight, merge_bias, first_gain, first_shift, triple_weight,
         output_weight, output_bias, second_gain, second_shift, expand_weight, expand_bias, reduce_weight, reduce_bias):
    vectors = (merge_bias, first_gain, first_shift, output_bias, second_gain, second_shift, reduce_bias, expand_bias)
    weights = (merge_weight, triple_weight, output_weight, expand_weight, reduce_weight)
    *images, F, sums = block(hidden, skipped, cotangent, row_mask, vectors, weights, lax.axis_size("seq"))
    merge, triple, output, expand, reduce, result, hidden_grad, skipped_grad, *v = unpack(images, F, sums)
    return (result, hidden_grad, skipped_grad, merge, v[0], v[1], v[2], triple, output, v[3], v[4], v[5], expand, v[7],
            reduce, v[6])


def solution(mesh):
    rows, held, copied = P(("dp", "seq"), None, None), P("seq", None), P()
    fast = mesh.shape["dp"] == 8 and mesh.shape["seq"] == 4
    return jax.shard_map(
        body if fast else plain,
        mesh=mesh,
        in_specs=(rows, rows, P("dp", None), rows, held, copied, copied, copied, held, held, copied, copied, copied,
                  held, copied, held, copied),
        out_specs=(rows, rows, rows, held, copied, copied, copied, held, held, copied, copied, copied, held, copied,
                   held, copied),
        check_vma=False,
    )
```

```python
import functools

import jax
import jax.numpy as jnp
from jax import lax
from jax.experimental import pallas as pl
from jax.experimental.pallas import tpu as pltpu
from jax.sharding import PartitionSpec as P

MESH = pl.DeviceIdType.MESH
HEADS = 16
EPS = 1e-05
NEGATIVE = -1e30
NB = 14
NP, SUB = 7, 3
Q = NP * SUB
AHEAD = 2
RING = 8
SLOTS = 3
VR = 16
READY = 5
LEAD = READY + 9
f32, bf16 = jnp.float32, jnp.bfloat16


def block_slices(refs):
    merge, triple, output, expand, reduce = refs
    R, C = output.shape
    out = []
    for j in range(merge.shape[0] // R): out.append(merge.at[pl.ds(j * R, R), :])
    for j in range(triple.shape[1] // C): out.append(triple.at[:, pl.ds(j * C, C)])
    out.append(output.at[:, :])
    for j in range(expand.shape[1] // C): out.append(expand.at[:, pl.ds(j * C, C)])
    for j in range(reduce.shape[0] // R): out.append(reduce.at[pl.ds(j * R, R), :])
    return out


def nn(a, b):
    return jnp.dot(a, b, preferred_element_type=f32)


def nt(a, b):
    return lax.dot_general(a, b, (((1,), (1,)), ((), ())), preferred_element_type=f32)


def tn(a, b):
    return lax.dot_general(a, b, (((0,), (0,)), ((), ())), preferred_element_type=f32)


HID, SKP, COT, NORMED, ATT, TWO, ACT, TRI, BR, TG, GR, EXP, ATTG, PLACES = 0, 2, 4, 6, 8, 10, 12, 20, 23, 25, 31, 33, 41, 42
HGRAD, SGRAD, RESULT = NORMED, TWO, ATT
NN, NT, EXTRA, CAST, FETCH, NORM, NORM_BACK, GELU, GELU_BACK, ATTEND, ATTEND_BACK, ROWS, FULL = range(1, 14)


def op(mode, a=0, w=0, acc=0, wait=1, pre=None, post=None):
    pre, post = (0 if v is None else v + 1 for v in (pre, post))
    return mode + 16 * (a + 64 * (w + 32 * (acc + 2 * (wait + 2 * (pre + 32 * post)))))


def plan():
    B = READY
    ops = []
    def at(tick, *what): ops.extend((tick, o) for o in what)
    (begin, stored, cot, attended, acts, pairs, px, triple, heads, merge, joined, result, outs, *sums) = (op(EXTRA, i) for i in range(18))
    at(0, begin)
    at(1, stored)
    at(2, cot)
    halves = []
    def by_half(tick, first, second):
        halves.extend([(2 * tick + 1, o) for o in first] + [(2 * tick + 2, o) for o in second])
    by_half(B + 1, [op(FETCH, 0), op(FETCH, 1)], [op(NN, HID, 0), op(NN, SKP, 1, acc=1), op(NORM, 0)])
    by_half(B + 2, [op(FETCH, 2)], [op(NN, NORMED, 2), op(CAST, TRI)])
    by_half(B + 3, [op(FETCH, 3)], [op(NN, NORMED, 3), op(CAST, TRI + 1)])
    by_half(B + 4, [op(FETCH, 4)], [op(NN, NORMED, 4), op(CAST, TRI + 2), op(ATTEND, 0)])
    by_half(B + 5, [op(FETCH, 5), op(ATTEND, 1)], [op(ATTEND, 2), op(ATTEND, 3), attended])
    by_half(B + 6, [op(FETCH, 6), op(NN, ATT, 5), op(NORM, 1)], [op(NN, TWO, 6), op(GELU, 0)])
    by_half(B + 7, [op(FETCH, 7), acts, op(ROWS, 0)], [op(NN, TWO, 7), op(GELU, 1)])
    by_half(B + 8, [op(FETCH, 8), op(ROWS, 4)], [op(NN, TWO, 8), op(GELU, 2)])
    by_half(B + 9, [op(FETCH, 9), op(ROWS, 8)], [op(NN, TWO, 9), op(GELU, 3), op(ROWS, 12)])
    by_half(B + 13, [op(FETCH, 10), op(FETCH, 11), op(FETCH, 12)], [])
    for i in range(4):
        halves += [(2 * (B + 14) + i // 2, o) for o in (op(NT, COT, 10 + i, post=13 + i), op(GELU_BACK, i))]
    halves += [(2 * (B + 14) + 1, pairs), (2 * (B + 14) + 2, px), (2 * (B + 14) + 2, op(FULL, 0))]
    at(B + 11, op(ROWS, 1))
    for i in range(4):
        at(B + 15 + i // 2, op(NT, EXP + 2 * i, 14 + i, acc=int(i > 0), post=17 + i))
    at(B + 16, op(NORM_BACK, 1))
    at(B + 17, op(NT, BR, 18, post=21), op(CAST, ATTG), op(FULL, 1))
    at(B + 18, op(ATTEND_BACK, 0), op(ATTEND_BACK, 1))
    at(B + 19, op(ATTEND_BACK, 2), op(ATTEND_BACK, 3), triple)
    at(B + 20, heads, op(FULL, 2))
    at(B + 21, op(NT, TG, 19, post=22), op(NT, TG + 2, 20, acc=1, post=23))
    at(B + 22, op(NT, TG + 4, 21, acc=1, post=24), op(NORM_BACK, 0))
    at(B + 23, op(FULL, 3))
    at(B + 24, merge, op(ROWS, 2))
    at(B + 25, sums[0], op(NT, GR, 22, post=25), op(CAST, HGRAD))
    at(B + 26, sums[1], op(NT, GR, 23, post=26), op(CAST, SGRAD), joined)
    at(B + 27, sums[2], op(NN, ACT, 24, post=27), op(NN, ACT + 2, 25, acc=1))
    at(B + 28, sums[3], op(NN, ACT + 4, 26, acc=1), op(NN, ACT + 6, 27, acc=1), result)
    at(B + 29, outs)
    at(B + 32, sums[4])
    spread = []
    for tick in sorted({t for t, _ in ops}):
        mine = [o for t, o in ops if t == tick]
        spread += [(2 * tick + 1 + 2 * i // len(mine), o) for i, o in enumerate(mine)]
    return sorted(spread + halves, key=lambda pair: pair[0])


OPS = plan()
STARTS = [sum(t < half for t, _ in OPS) for half in range(2 * (LEAD + AHEAD + Q + 10))]
UNITS = [2, 6] + [4 * j for j in range(2, 10)] + [1 + 4 * s for s in range(4)] + [4 * j for j in (6, 7, 8, 9, 5, 2, 3, 4)] + [2, 6] + [1 + 4 * s for s in range(4)]


def lookup(values, i):
    total = jnp.int32(values[0])
    for k in range(1, len(values)):
        if values[k] != values[k - 1]:
            total = total + jnp.where(i >= k, values[k] - values[k - 1], 0)
    return total


def block_kernel(hid, skp, cot_in, mask_in, *refs, nz):
    (b0, b1, b2, b3, b4, b5, b6, b7, wm, wt, wo, we, wr,
     res, hgrad, sgrad, F, WV, G, D,
     W, X, PR, XH, MID, MG, E, INV, MASK, VEC, DB, MROWS, v0, v1, v2, v3, v4, v5, v6, v7,
     K, R1, R2, R3, O, VB,
     loc, loc2, zs, zr, xs, xr, ys, yr, cs, cr, fsem, insem, es, er, dsem, osem,
     ld, s1, r1, s2, r2, s3, r3, st, sf, rf, sc, rcv, vl, vs, vr) = refs
    dp = lax.axis_index("dp"); z = lax.axis_index("seq")
    c = dp % 2; x = (dp // 2) % 2; y = dp // 4
    xn = dp + 2 - 4 * x; yn = dp + 4 - 8 * y; cn = dp + 1 - 2 * c; co = 1 - c
    L, C = X.shape[1:]
    R = G.shape[2]
    scale = (C // HEADS) ** -0.5
    bar = pltpu.get_barrier_semaphore()
    for tgt in (xn, yn, cn):
        pl.semaphore_signal(bar, inc=1, device_id=(tgt, z), device_id_type=MESH)
    for d in range(1, nz):
        pl.semaphore_signal(bar, inc=1, device_id=(dp, (z + d) % nz), device_id_type=MESH)

    def rc(src, dst, ss, rs, dev):
        return pltpu.make_async_remote_copy(src_ref=src, dst_ref=dst, send_sem=ss, recv_sem=rs, device_id=dev, device_id_type=MESH)

    blocks = block_slices((wm, wt, wo, we, wr))
    room = SLOTS * 4
    def stage(j): return W.at[(j % room) // 4, j % 4]
    def load_in(j): return pltpu.make_async_copy(blocks[j], stage(j), loc.at[j])
    def load_out(j, slot): return pltpu.make_async_copy(slot, G.at[z, j], loc2.at[j])
    for j in range(min(room, NB)): load_in(j).start()
    inputs = [pltpu.make_async_copy(a, b, insem.at[i]) for i, (a, b) in enumerate(
        ((hid.at[0], X.at[HID]), (skp.at[0], X.at[SKP]), (cot_in.at[0], X.at[COT]), (mask_in, MROWS),
         (b0, v0), (b1, v1), (b2, v2), (b3, v3), (b4, v4), (b5, v5), (b6, v6), (b7, v7)))]
    for cp in inputs: cp.start()
    pl.semaphore_wait(bar, nz + 2)

    half = R // 2; third = half // 3
    base = half * c
    zp = ((x + y) % 2) * (2 - x)
    yp = 1 + y
    def reg(s, b, start, n):
        return G.at[s, b, pl.ds(pl.multiple_of(start, 16), n), :]
    def same(region, ss, rs, dev): return rc(region, region, ss, rs, dev)
    def zcopy(b, d, k):
        s = z - k if d == 0 else z + k
        return same(reg(s, b, base + third * zp, third), zs.at[b % RING, d, k], zr.at[b % RING, d, k], (dp, z + 1 if d == 0 else z - 1))
    def zsend_ok(d, k):
        return (z >= k) & (z < nz - 1) if d == 0 else (z + k <= nz - 1) & (z > 0)
    def zrecv_ok(d, k):
        return z >= k + 1 if d == 0 else z + 1 + k <= nz - 1
    def shard_in(d, k):
        return z - 1 - k if d == 0 else z + 1 + k
    def xcopy(b, s): return same(reg(s, b, base + third * zp, third), xs.at[b % 6, s], xr.at[b % 6, s], (xn, z))
    def ycopy(b, s): return same(reg(s, b, base + third * yp, third), ys.at[b % 6, s], yr.at[b % 6, s], (yn, z))
    def ccopy(b, s): return same(reg(s, b, base, half), cs.at[b % 6, s], cr.at[b % 6, s], (cn, z))
    def own(b):
        for d in (0, 1):
            @pl.when(zsend_ok(d, 0))
            def _(): zcopy(b, d, 0).start()
    def zarr(b, d, k):
        zcopy(b, d, k).wait_recv()
        if k + 1 < nz - 1:
            @pl.when(zsend_ok(d, k + 1))
            def _(): zcopy(b, d, k + 1).start()
        s = shard_in(d, k)
        xcopy(b, s).start()
        @pl.when((x + y) % 2 == 1)
        def _(): ycopy(b, s).start()
    def xarr(b, d, k):
        s = shard_in(d, k)
        xcopy(b, s).wait_recv()
        @pl.when((x + y) % 2 == 0)
        def _(): ycopy(b, s).start()
    def yarr(b, d, k):
        s = shard_in(d, k)
        ycopy(b, s).wait_recv()
        ccopy(b, s).start()
    def fin(b, d, k):
        s = shard_in(d, k)
        ccopy(b, s).wait()
        xcopy(b, s).wait_send()
        ycopy(b, s).wait_send()
    for j in range(AHEAD):
        for d in (0, 1):
            @pl.when(zsend_ok(d, 0))
            def _():
                rc(blocks[j].at[pl.ds(pl.multiple_of(base + third * zp, 16), third)], reg(z, j, base + third * zp, third),
                   zs.at[j, d, 0], zr.at[j, d, 0], (dp, z + 1 if d == 0 else z - 1)).start()
    for j in range(4):
        load_in(j).wait()
        load_out(j, stage(j)).start()
    for j in range(4): load_out(j, stage(j)).wait()
    FIRST = [(zarr, 0, 0), (zarr, 0, 1), (zarr, 0, 2), (None, 0, 0)]
    SECOND = [(xarr, 1, k) for k in range(3)] + [(yarr, 2, k) for k in range(3)] + [(fin, 3, k) for k in range(3)]
    def gather_half(t, todo):
        for fn, off, k in todo:
            if fn is None:
                @pl.when(t < NB - AHEAD)
                def _(): own(t + AHEAD)
                continue
            b = t - off - k
            @pl.when((b >= 0) & (b < NB))
            def _():
                for d in (0, 1):
                    @pl.when(zrecv_ok(d, k))
                    def _(): fn(b, d, k)
                    if fn is fin:
                        @pl.when(zsend_ok(d, k))
                        def _(): zcopy(b, d, k).wait_send()

    T = K.shape[2]
    def ring(q): return q % RING
    def typ(q, s): return (q + s) % 2
    def keep(q, s): return x + typ(q, s) * (y - x)
    def near(q, s): return xn + typ(q, s) * (yn - xn)
    def far(q, s): return yn + typ(q, s) * (xn - yn)
    def piece(q, h):
        return NP - 1 - q // SUB, pl.ds(pl.multiple_of(half * h + T * (q % SUB), 16), T)
    def load(q, s):
        p, rows = piece(q, keep(q, s))
        return pltpu.make_async_copy(D.at[s, p, rows], K.at[ring(q), s], ld.at[s, ring(q)])
    def first(q, s):
        p, rows = piece(q, 1 - keep(q, s))
        return rc(D.at[s, p, rows], R1.at[ring(q), s], s1.at[s, ring(q)], r1.at[s, ring(q)], (near(q, s), z))
    def up(q, s):
        return rc(K.at[ring(q), s], R2.at[ring(q), s], s2.at[s, ring(q)], r2.at[s, ring(q)], (dp, z + 1))
    def down(q, s):
        away = jnp.minimum(z - 1 - s, 1)
        slot = nz + away * (s - nz)
        return rc(K.at[ring(q), s], R2.at[ring(q), slot], s2.at[s, ring(q)], r2.at[slot, ring(q)], (dp, z - 1))
    def got(slot, q):
        return rc(K.at[ring(q), 0], R2.at[ring(q), slot], s2.at[0, ring(q)], r2.at[slot, ring(q)], (dp, z))
    def last(q):
        return rc(K.at[ring(q), z], R3.at[ring(q)], s3.at[ring(q)], r3.at[ring(q)], (far(q, z), z))
    def frow(q, h, cc):
        p, rows = piece(q, h)
        return F.at[2 * p + cc, rows]
    def keepf(q): return pltpu.make_async_copy(O.at[ring(q)], frow(q, keep(q, z), c), st.at[ring(q)])
    def spread(q): return rc(O.at[ring(q)], frow(q, keep(q, z), c), sf.at[ring(q)], rf.at[ring(q)], (near(q, z), z))
    def spread_in(q):
        r = frow(q, 1 - keep(q, z), c)
        return rc(r, r, sf.at[ring(q)], rf.at[ring(q)], (near(q, z), z))
    def cross(q): return rc(O.at[ring(q)], frow(q, keep(q, z), c), sc.at[0, ring(q)], rcv.at[0, ring(q)], (cn, z))
    def cross2(q):
        r = frow(q, 1 - keep(q, z), c)
        return rc(r, r, sc.at[1, ring(q)], rcv.at[1, ring(q)], (cn, z))
    def add(a, b): return (a.astype(f32) + b.astype(f32)).astype(bf16)
    def issue(q):
        for s in range(nz):
            first(q, s).start(); load(q, s).start()
    def start(q):
        for s in range(nz):
            load(q, s).wait(); first(q, s).wait_recv()
            K[ring(q), s] = add(K[ring(q), s], R1[ring(q), s])
        for s in range(nz):
            if s < nz - 1:
                @pl.when(z == nz - 1)
                def _(): down(q, s).start()
            if nz - 1 - s > 0:
                @pl.when(z == 0)
                def _(): up(q, nz - 1 - s).start()
    def hop(q, k):
        for s in reversed(range(nz)):
            if s > k:
                @pl.when(z == k)
                def _():
                    got(s, q).wait_recv()
                    K[ring(q), s] = add(K[ring(q), s], R2[ring(q), s])
                    up(q, s).start()
        for s in range(nz):
            if s < nz - 1 - k:
                @pl.when(z == nz - 1 - k)
                def _():
                    got(s, q).wait_recv()
                    K[ring(q), s] = add(K[ring(q), s], R2[ring(q), s])
                    down(q, s).start()
    def arrive(q):
        @pl.when(z > 0)
        def _():
            got(z, q).wait_recv()
            K[ring(q), z] = add(K[ring(q), z], R2[ring(q), z])
        @pl.when(z < nz - 1)
        def _():
            got(nz, q).wait_recv()
            K[ring(q), z] = add(K[ring(q), z], R2[ring(q), nz])
        last(q).start()
    def final(q):
        last(q).wait_recv()
        O[ring(q)] = add(K[ring(q), z], R3[ring(q)])
        keepf(q).start(); spread(q).start(); cross(q).start()
    def relay(q):
        spread_in(q).wait_recv()
        cross2(q).start()
        for s in range(nz):
            first(q, s).wait_send()
            if s > 0:
                @pl.when(z < s)
                def _(): up(q, s).wait_send()
            if s < nz - 1:
                @pl.when(z > s)
                def _(): down(q, s).wait_send()
        last(q).wait_send()
    def drain(q):
        keepf(q).wait(); spread(q).wait_send()
        cross(q).wait_send(); cross(q).wait_recv(); cross2(q).wait_send(); cross2(q).wait_recv()
    steps = [(0, start)] + [(k, functools.partial(hop, k=k)) for k in range(1, nz - 1)] + [
        (nz - 1, arrive), (nz, final), (nz + 1, relay), (nz + 3, drain)]
    def sum_half(t, todo):
        for off, fn in todo:
            q = t - AHEAD - off
            @pl.when((q >= 0) & (q < Q))
            def _(): fn(q)
    def sum_issue(t):
        @pl.when(((t % SUB == 0) & (t > 0) & (t < Q)) | (t == 1))
        def _():
            for cp in puts(NP - 1 - t // SUB): cp.wait()
        @pl.when(t == 1)
        def _(): issue(0)
        @pl.when((t > 0) & (t < Q))
        def _(): issue(t)

    devs = ((cn, z), (xn, z), (yn, z))
    def swap(i): return rc(VB.at[2 * i], VB.at[2 * i + 1], vs.at[i], vr.at[i], devs[i])
    def vstep(i):
        if i > 0:
            swap(i - 1).wait()
            VB[2 * i] = VB[2 * i - 2] + VB[2 * i - 1]
        if i < 3:
            swap(i).start()
    def line(d):
        return rc(VB.at[6], VB.at[6 + d], vs.at[2 + d], vr.at[2 + d], (dp, (z + d) % nz))
    def vline():
        vstep(3)
        for d in range(1, nz): line(d).start()
    def vend():
        for d in range(1, nz): line(d).wait()
        def plane(s): return VB[6 + (z - s + nz) % nz]
        total = plane(0)
        for s in range(1, nz): total = total + plane(s)
        VB[0] = total
        cp = pltpu.make_async_copy(VB.at[0], WV, vl.at[1])
        cp.start(); cp.wait()

    def pair(i, src, dst): return rc(src, dst, es.at[i], er.at[i], (cn, z))
    def both(i, a): return pair(i, X.at[a], X.at[a + 1])
    ex = {
        "hid": both(0, HID), "skp": both(1, SKP), "cot": both(2, COT), "normed": both(3, NORMED), "att": both(4, ATT), "two": both(5, TWO),
        "px0": both(10, EXP + 2 * co), "px1": both(11, EXP + 2 * co + 4), "br": both(12, BR),
        "qk": both(13, TG + 2 * co), "v": both(14, TG + 4), "gr": both(15, GR),
    }
    def arrives(i, a): return both(i, a).wait_recv()
    def send_act(i): return both(6 + i, ACT + 2 * i)
    def arrived(*names):
        for n in names: ex[n].wait()

    def fetch(n):
        code = lookup(UNITS, n)
        kind, arg = code % 4, code // 4
        for i in range(4):
            s = jnp.where(kind == 0, i, jnp.where(kind == 1, arg, 2 * arg + i // 2))
            j = jnp.where(kind == 0, arg, jnp.where(kind == 1, 10 + i, i % 2))
            pltpu.make_async_copy(G.at[s, j], W.at[n % SLOTS, i], fsem.at[n % SLOTS, i]).start()
    def fetched(n):
        for i in range(4):
            pltpu.make_async_copy(G.at[0, 0], W.at[n % SLOTS, i], fsem.at[n % SLOTS, i]).wait()
    def weight(n): return W[n % SLOTS].reshape(4 * R, C)
    def vec(i): return VEC[pl.ds(i, 1), :]
    def tally(i, v): VB[0, pl.ds(i, 1), :] = jnp.sum(v, axis=0, keepdims=True)

    def do_matmul(dot, a, n, acc, wait, pre, post):
        @pl.when(pre > 0)
        def _(): fetch(pre - 1)
        @pl.when(wait > 0)
        def _(): fetched(n)
        v = dot(X[a], weight(n))
        E[...] = jnp.where(acc > 0, E[...], 0.0) + v
        @pl.when(post > 0)
        def _(): fetch(post - 1)
    def do_cast(a):
        X[a] = E[...].astype(bf16)
    def do_norm(k):
        v = jnp.where(k > 0, MID[...], 0.0) + E[...] + vec(3 * k)
        MID[...] = v
        m = v - jnp.mean(v, axis=-1, keepdims=True)
        r = lax.rsqrt(jnp.mean(m * m, axis=-1, keepdims=True) + EPS)
        XH[k] = m * r
        INV[k] = jnp.broadcast_to(r, INV.shape[1:])
        a = NORMED + (TWO - NORMED) * k
        X[a] = (m * r * vec(3 * k + 1) + vec(3 * k + 2)).astype(bf16)
        both(3 + 2 * k, a).start()
    def do_norm_back(k):
        e = E[...]
        xhat = XH[k]
        tally(3 * k + 1, e * xhat); tally(3 * k + 2, e)
        t = e * vec(3 * k + 1)
        a = jnp.mean(t, axis=-1, keepdims=True)
        b = jnp.mean(t * xhat, axis=-1, keepdims=True)
        v = jnp.where(k > 0, X[COT].astype(f32), MG[...]) + (t - a - xhat * b) * INV[k, :, 0:1]
        MG[...] = v
        low = v.astype(bf16)
        a = GR + (BR - GR) * k
        X[a] = low
        tally(3 * k, low.astype(f32))
        both(15 - 3 * k, a).start()
    step = C // 3
    def part(n): return pl.ds(pl.multiple_of(step * n, 128), step)
    def do_gelu(i):
        def one(n, _):
            v = E[:, part(n)] + VEC[pl.ds(7 + i, 1), part(n)]
            cdf = 0.5 * (1.0 + lax.erf(v * (0.5 ** 0.5)))
            X[ACT + 2 * i, :, part(n)] = (v * cdf).astype(bf16)
            X[EXP + 2 * i, :, part(n)] = (cdf + v * jnp.exp(-0.5 * v * v) * 0.3989422804014327).astype(bf16)
            return 0
        lax.fori_loop(0, 3, one, 0)
        send_act(i).start()
    def do_gelu_back(i):
        def one(n, _):
            low = (E[:, part(n)] * X[EXP + 2 * i, :, part(n)].astype(f32)).astype(bf16)
            X[EXP + 2 * i, :, part(n)] = low
            VB[0, pl.ds(7 + i, 1), part(n)] = jnp.sum(low.astype(f32), axis=0, keepdims=True)
            return 0
        lax.fori_loop(0, 3, one, 0)
    hs = C // HEADS
    group = HEADS // 4
    def do_attend(i):
        for g in range(4):
            @pl.when(i == g)
            def _():
                for h in range(group * g, group * g + group):
                    sl = slice(hs * h, hs * h + hs)
                    scores = nt(X[TRI + 1, :, sl], X[TRI, :, sl]) * scale
                    scores = jnp.where(MASK[:, 0:1] > 0, scores, NEGATIVE)
                    e = jnp.exp(scores - jnp.max(scores, axis=0, keepdims=True))
                    p = (e * (1.0 / jnp.sum(e, axis=0, keepdims=True))).astype(bf16)
                    PR[h] = p
                    X[ATT, :, sl] = tn(p, X[TRI + 2, :, sl]).astype(bf16)
    def do_attend_back(i):
        for g in range(4):
            @pl.when(i == g)
            def _():
                for h in range(group * g, group * g + group):
                    sl = slice(hs * h, hs * h + hs)
                    q, k, v, d, p = X[TRI, :, sl], X[TRI + 1, :, sl], X[TRI + 2, :, sl], X[ATTG, :, sl], PR[h]
                    X[TG + 4, :, sl] = nn(p, d).astype(bf16)
                    pg = nt(v, d)
                    pf = p.astype(f32)
                    sg = (pf * (pg - jnp.sum(pf * pg, axis=0, keepdims=True))).astype(bf16)
                    X[TG, :, sl] = (tn(sg, k) * scale).astype(bf16)
                    X[TG + 2, :, sl] = (nn(sg, q) * scale).astype(bf16)
    def puts(p): return [pltpu.make_async_copy(DB.at[pl.ds(R * s, R)], D.at[s, p], dsem.at[s]) for s in range(4)]
    def put(p):
        for cp in puts(p): cp.start()
    def pair_of(a, cols=slice(None)): return X[pl.ds(a, 2), :, cols].reshape(2 * L, -1)
    def do_rows(a):
        kind = a % 4
        merge = kind // 2
        lo = a // 4
        hi = jnp.where(kind == 0, lo + 1, 4)
        @pl.when(kind == 0)
        def _(): send_act(lo).wait()
        right = COT + (GR - COT) * merge
        def one(s, _):
            left = ACT + 2 * s + merge * (HID + 2 * (s // 2) - ACT - 2 * s)
            cut = merge * (2 * (s % 2)) + (1 - merge) * 2 * (1 - kind) + c
            rows = pl.ds(pl.multiple_of(R * s, 16), R)
            for v in range(4):
                @pl.when(cut == v)
                def _():
                    DB[rows] = tn(pair_of(left, slice(R * v, R * v + R)), pair_of(right)).astype(bf16)
            pltpu.make_async_copy(DB.at[rows], D.at[s, 6 - kind - 4 * merge], dsem.at[s]).start()
            return 0
        lax.fori_loop(lo, hi, one, 0)
    def do_full(kind):
        left = jnp.where(kind < 2, TWO, jnp.where(kind == 2, NORMED + (ATT - NORMED) * c, NORMED))
        right = jnp.where(kind < 2, EXP + 2 * c + 4 * (1 - kind), jnp.where(kind == 2, TG + 4 + (BR - TG - 4) * c, TG + 2 * c))
        def one(n, _):
            DB[pl.ds(pl.multiple_of(step * n, 128), step)] = tn(pair_of(left, part(n)), pair_of(right)).astype(bf16)
            return 0
        lax.fori_loop(0, 3, one, 0)
        put(4 - kind)

    def x_begin():
        VB[0] = jnp.zeros_like(VB[0])
        for cp in inputs: cp.wait()
        for n in ("hid", "skp", "cot"): ex[n].start()
        valid = MROWS[pl.ds(z, 1), :].astype(f32)
        MASK[...] = jnp.broadcast_to(valid, (MASK.shape[1], L)).T
        for i, v in enumerate((v0, v1, v2, v3, v4, v5, v6)):
            VEC[i:i + 1, :] = v[...].astype(f32).reshape(1, C)
        for i in range(4):
            VEC[7 + i:8 + i, :] = v7[C * i:C * (i + 1)].astype(f32).reshape(1, C)
        for j in range(room, NB): load_in(j).start()
        for j in range(4, NB):
            load_in(j).wait()
            load_out(j, stage(j)).start()
    def x_stored():
        for j in range(4, NB): load_out(j, stage(j)).wait()
    def x_attended(): ex["att"].start()
    def x_acts():
        arrived("cot")
    def x_cot(): tally(6, X[COT].astype(f32))
    def x_pairs():
        ex["px0"].start(); ex["px1"].start()
    def out(i):
        return pltpu.make_async_copy(X.at[(RESULT, HGRAD, SGRAD)[i]], (res, hgrad, sgrad)[i].at[0], osem.at[i])
    def x_result():
        X[RESULT] = (MID[...] + E[...] + vec(6)).astype(bf16)
        out(0).start()
    def x_joined():
        out(1).start(); out(2).start()
    def x_outs():
        for i in range(3): out(i).wait()
    def x_px():
        arrived("two")
        for i in range(2):
            ex["px" + str(i)].wait_send(); arrives(10 + i, EXP + 2 * c + 4 * i)
    def x_triple():
        ex["qk"].start(); ex["v"].start()
    def x_heads():
        arrived("normed", "att", "br", "v")
        ex["qk"].wait_send(); arrives(13, TG + 2 * c)
    def x_merge(): arrived("hid", "skp", "gr")
    extras = [x_begin, x_stored, x_cot, x_attended, x_acts, x_pairs, x_px, x_triple, x_heads, x_merge, x_joined, x_result, x_outs,
              functools.partial(vstep, 0), functools.partial(vstep, 1), functools.partial(vstep, 2), vline, vend]
    def do_extra(i):
        for k, fn in enumerate(extras):
            @pl.when(i == k)
            def _(): fn()

    def run(n, _):
        code = lookup([op for _, op in OPS], n)
        mode, a, w = code % 16, code // 16 % 64, code // 1024 % 32
        acc, wait = code // 2 ** 15 % 2, code // 2 ** 16 % 2
        pre, post = code // 2 ** 17 % 32, code // 2 ** 22 % 32
        small = ((do_extra, EXTRA), (do_cast, CAST), (fetch, FETCH), (do_norm, NORM), (do_norm_back, NORM_BACK), (do_gelu, GELU),
                 (do_gelu_back, GELU_BACK), (do_attend, ATTEND), (do_attend_back, ATTEND_BACK), (do_rows, ROWS), (do_full, FULL))
        for dot, m in ((nn, NN), (nt, NT)):
            @pl.when(mode == m)
            def _(): do_matmul(dot, a, w, acc, wait, pre, post)
        for fn, m in small:
            @pl.when(mode == m)
            def _(): fn(a)
        return 0

    cut = nz - 1
    def tick(h, _):
        t = h // 2
        @pl.when((h % 2 == 0) & (t < NB + nz + 2))
        def _(): gather_half(t, FIRST)
        @pl.when((h % 2 == 1) & (t < NB + nz + 2))
        def _(): gather_half(t, SECOND)
        @pl.when((h % 2 == 0) & (t >= LEAD))
        def _(): sum_half(t - LEAD, steps[:cut])
        @pl.when((h % 2 == 1) & (t >= LEAD))
        def _():
            sum_half(t - LEAD, steps[cut:])
            sum_issue(t - LEAD)
        lax.fori_loop(lookup(STARTS, h), lookup(STARTS, h + 1), run, 0)
        return 0
    lax.fori_loop(0, 2 * (LEAD + AHEAD + Q + nz + 3), tick, 0)


def block(hidden, skipped, cotangent, mask, vectors, weights, nz):
    L, C = hidden.shape[1:]
    R = weights[2].shape[0]
    T = R // 2 // SUB
    S = pltpu.SemaphoreType.DMA
    V = pltpu.VMEM
    rows = jax.ShapeDtypeStruct((1, L, C), bf16)
    hbm = pl.BlockSpec(memory_space=pl.ANY)
    out_shape = (rows, rows, rows, jax.ShapeDtypeStruct((NB, R, C), bf16), jax.ShapeDtypeStruct((VR, C), f32),
                 jax.ShapeDtypeStruct((nz, NB, R, C), bf16), jax.ShapeDtypeStruct((nz, NP, R, C), bf16))
    scratch = [
        V((SLOTS, 4, R, C), bf16), V((PLACES, L, C), bf16), V((HEADS, L, L), bf16), V((2, L, C), f32), V((L, C), f32), V((L, C), f32),
        V((L, C), f32), V((2, L, 128), f32), V((L, 128), f32), V((VR, C), f32), V((4 * R, C), bf16),
        V(mask.shape, jnp.int32), *[V(v.shape, bf16) for v in vectors],
        V((RING, nz, T, C), bf16), V((RING, nz, T, C), bf16), V((RING, nz + 1, T, C), bf16), V((RING, T, C), bf16), V((RING, T, C), bf16),
        V((6 + nz, VR, C), f32),
        S((NB,)), S((NB,)), S((RING, 2, nz - 1)), S((RING, 2, nz - 1)), S((6, nz)), S((6, nz)), S((6, nz)), S((6, nz)), S((6, nz)), S((6, nz)),
        S((SLOTS, 4)), S((12,)), S((16,)), S((16,)), S((4,)), S((3,)),
        S((nz, RING)), S((nz, RING)), S((nz, RING)), S((nz, RING)), S((nz + 1, RING)), S((RING,)), S((RING,)), S((RING,)), S((RING,)), S((RING,)), S((2, RING)), S((2, RING)),
        S((2,)), S((2 + nz,)), S((2 + nz,)),
    ]
    return pl.pallas_call(
        functools.partial(block_kernel, nz=nz),
        out_shape=out_shape, in_specs=[hbm] * 17, out_specs=(hbm,) * 7, scratch_shapes=scratch,
        compiler_params=pltpu.CompilerParams(collective_id=0, has_side_effects=True, vmem_limit_bytes=63 * 2**20),
    )(hidden, skipped, cotangent, mask, *vectors, *weights)[:5]


def unpack_kernel(F, WV, i0, i1, i2, m, t, o, e, r, o0, o1, o2, *rest):
    vec_outs, (FB, OB, VB, IB), vbufs, (fin, fout, vin, vout, iin, iout) = rest[:8], rest[8:12], rest[12:20], rest[20:]
    R, C = FB.shape[1:]
    outs = block_slices((m, t, o, e, r))
    takes = [pltpu.make_async_copy(F.at[j], FB.at[j], fin.at[j]) for j in range(NB)]
    puts = [pltpu.make_async_copy(OB.at[j], outs[j], fout.at[j]) for j in range(NB)]
    sums = pltpu.make_async_copy(WV, VB, vin.at[0])
    images = [(pltpu.make_async_copy(a, IB.at[i], iin.at[i]), pltpu.make_async_copy(IB.at[i], b, iout.at[i]))
              for i, (a, b) in enumerate(((i0, o0), (i1, o1), (i2, o2)))]
    for cp in takes[:4]: cp.start()
    sums.start()
    for a, _ in images: a.start()
    for cp in takes[4:]: cp.start()
    for j in range(NB):
        takes[j].wait()
        def widen(i, _):
            part = pl.ds(pl.multiple_of(i * 32, 16), 32)
            OB[j, part] = FB[j, part].astype(f32)
            return 0
        lax.fori_loop(0, R // 32, widen, 0)
        puts[j].start()
        if j == 3:
            sums.wait()
            for i in range(7): vbufs[i][...] = VB[i:i + 1, :].reshape(C)
            for i in range(4): vbufs[7][C * i:C * (i + 1)] = VB[7 + i:8 + i, :].reshape(C)
            small = [pltpu.make_async_copy(a, b, vout.at[i]) for i, (a, b) in enumerate(zip(vbufs, vec_outs))]
            for cp in small: cp.start()
            for a, b in images:
                a.wait()
                b.start()
    for cp in puts: cp.wait()
    for cp in small: cp.wait()
    for _, b in images: b.wait()


def unpack(images, F, sums):
    R, C = F.shape[1:]
    S = pltpu.SemaphoreType.DMA
    hbm = pl.BlockSpec(memory_space=pl.ANY)
    vecs = [jax.ShapeDtypeStruct((n * C,), f32) for n in (1, 1, 1, 1, 1, 1, 1, 4)]
    shapes = [jax.ShapeDtypeStruct(s, f32) for s in ((2 * R, C), (R, 3 * C), (R, C), (R, 4 * C), (4 * R, C))]
    shapes += [jax.ShapeDtypeStruct(a.shape, a.dtype) for a in images] + vecs
    return pl.pallas_call(
        unpack_kernel, out_shape=shapes, in_specs=[hbm] * 5, out_specs=[hbm] * len(shapes),
        scratch_shapes=[pltpu.VMEM((NB, R, C), bf16), pltpu.VMEM((NB, R, C), f32), pltpu.VMEM(sums.shape, f32),
                        pltpu.VMEM((3,) + images[0].shape, bf16), *[pltpu.VMEM(v.shape, f32) for v in vecs],
                        S((NB,)), S((NB,)), S((1,)), S((8,)), S((3,)), S((3,))],
        compiler_params=pltpu.CompilerParams(vmem_limit_bytes=63 * 2**20),
    )(F, sums, *images)


def pack(m, t, o, e, r):
    R, C = o.shape
    def cut(w):
        a, b = w.shape
        return w.reshape(a // R, R, b // C, C).transpose(0, 2, 1, 3).reshape(-1, R, C)
    return jnp.concatenate([cut(w) for w in (m, t, o, e, r)])


def against(left, right):
    return lax.dot_general(left, right, (((1,), (1,)), ((), ())), preferred_element_type=jnp.float32)


def weight_grad(left, right):
    return lax.dot_general(left, right, (((0,), (0,)), ((), ())), preferred_element_type=jnp.float32)


def norm_parts(v):
    c = v - jnp.mean(v, axis=-1, keepdims=True)
    inv = lax.rsqrt(jnp.mean(c * c, axis=-1, keepdims=True) + EPS)
    return c * inv, inv


def norm_back(e, xhat, inv, gain):
    t = e * gain
    return (t - jnp.mean(t, axis=-1, keepdims=True) - xhat * jnp.mean(t * xhat, axis=-1, keepdims=True)) * inv


def plain(hidden, skipped, row_mask, cotangent, merge_weight, merge_bias, first_gain, first_shift, triple_weight,
         output_weight, output_bias, second_gain, second_shift, expand_weight, expand_bias, reduce_weight, reduce_bias):
    length, D = hidden.shape[1:]
    hs = D // HEADS
    nz = lax.axis_size("seq")
    z = lax.axis_index("seq")
    c = lax.axis_index("dp") % 2
    weights = (merge_weight, triple_weight, output_weight, expand_weight, reduce_weight)
    G = lax.all_gather(pack(*weights), "seq")
    R = G.shape[2]
    merge_full = G[:, 0:2].reshape(2 * D, D)
    triple_full = G[:, 2:5].transpose(1, 0, 2, 3).reshape(3, D, D)
    output_full = G[:, 5].reshape(D, D)
    expand_full = G[:, 6:10].transpose(1, 0, 2, 3).reshape(4, D, D)
    reduce_full = G[:, 10:14].reshape(4 * D, D)
    gain_a, shift_a, gain_b, shift_b = (v.astype(f32) for v in (first_gain, first_shift, second_gain, second_shift))
    joined = jnp.concatenate([hidden[0], skipped[0]], axis=-1)
    merged = jnp.dot(joined, merge_full, preferred_element_type=f32) + merge_bias.astype(f32)
    xhat_a, inv_a = norm_parts(merged)
    normed = (xhat_a * gain_a + shift_a).astype(bf16)
    triple = jnp.einsum("ld,jde->jle", normed, triple_full, preferred_element_type=f32).astype(bf16)
    queries, key_heads, value_heads = (triple[j].reshape(length, HEADS, hs) for j in range(3))
    valid = lax.dynamic_index_in_dim(row_mask, z, 0, False)
    scores = jnp.einsum("qhd,khd->hqk", queries, key_heads, preferred_element_type=f32) * hs ** -0.5
    scores = jnp.where(valid[None, None, :] > 0, scores, NEGATIVE)
    weights_ = jnp.exp(scores - jnp.max(scores, axis=-1, keepdims=True))
    probs = weights_ / jnp.sum(weights_, axis=-1, keepdims=True)
    probs_low = probs.astype(bf16)
    attended = jnp.einsum("hqk,khd->qhd", probs_low, value_heads, preferred_element_type=f32).astype(bf16).reshape(length, D)
    middle = merged + jnp.dot(attended, output_full, preferred_element_type=f32) + output_bias.astype(f32)
    xhat_b, inv_b = norm_parts(middle)
    normed_two = (xhat_b * gain_b + shift_b).astype(bf16)
    expanded = jnp.einsum("ld,jde->jle", normed_two, expand_full, preferred_element_type=f32) + expand_bias.astype(f32).reshape(4, 1, D)
    activated, gelu_back = jax.vjp(functools.partial(jax.nn.gelu, approximate=False), expanded)
    activated = activated.astype(bf16).transpose(1, 0, 2).reshape(length, 4 * D)
    result = middle + jnp.dot(activated, reduce_full, preferred_element_type=f32) + reduce_bias.astype(f32)
    result = result.astype(bf16)
    upstream = cotangent[0]
    wide = upstream.astype(f32)
    activated_grad = jnp.einsum("le,jde->jld", upstream, reduce_full.reshape(4, D, D), preferred_element_type=f32)
    expanded_grad = gelu_back(activated_grad)[0].astype(bf16)
    e_two = jnp.einsum("jle,jde->ld", expanded_grad, expand_full, preferred_element_type=f32)
    middle_grad = wide + norm_back(e_two, xhat_b, inv_b, gain_b)
    branch_grad = middle_grad.astype(bf16)
    attended_grad = against(branch_grad, output_full).astype(bf16).reshape(length, HEADS, hs)
    prob_grad = jnp.einsum("qhd,khd->hqk", attended_grad, value_heads, preferred_element_type=f32)
    values_grad = jnp.einsum("hqk,qhd->khd", probs_low, attended_grad, preferred_element_type=f32)
    score_grad = (probs * (prob_grad - jnp.sum(probs * prob_grad, axis=-1, keepdims=True))).astype(bf16)
    queries_grad = jnp.einsum("hqk,khd->qhd", score_grad, key_heads, preferred_element_type=f32) * hs ** -0.5
    keys_grad = jnp.einsum("hqk,qhd->khd", score_grad, queries, preferred_element_type=f32) * hs ** -0.5
    triple_grad = jnp.stack([g.astype(bf16).reshape(length, D) for g in (queries_grad, keys_grad, values_grad)])
    e_one = jnp.einsum("jle,jde->ld", triple_grad, triple_full, preferred_element_type=f32)
    merged_grad = (middle_grad + norm_back(e_one, xhat_a, inv_a, gain_a)).astype(bf16)
    joined_grad = against(merged_grad, merge_full).astype(bf16)
    vectors = jnp.stack([
        jnp.sum(merged_grad.astype(f32), 0), jnp.sum(e_one * xhat_a, 0), jnp.sum(e_one, 0),
        jnp.sum(branch_grad.astype(f32), 0), jnp.sum(e_two * xhat_b, 0), jnp.sum(e_two, 0), jnp.sum(wide, 0),
    ])
    vectors = jnp.concatenate([vectors, jnp.sum(expanded_grad.astype(f32), 1), jnp.zeros((VR - 11, D), f32)])

    count = lax.axis_size("dp")
    def both(v):
        other = lax.ppermute(v, "dp", [(i, i + 1 - 2 * (i % 2)) for i in range(count)])
        return jnp.concatenate([v, other], axis=-2)
    joined2, normed2, triple2, attended2, branch2, normed_two2, expanded2, activated2, upstream2 = (
        both(v) for v in (joined, normed, triple_grad, attended, branch_grad, normed_two, expanded_grad, activated, upstream))
    def pick(v, axis, index):
        return lax.dynamic_index_in_dim(v, index, axis, False)
    def rows(left, right):
        return jnp.einsum("lsr,le->sre", left, right, preferred_element_type=f32).astype(bf16)
    def split(left):
        return left.reshape(left.shape[0], nz, -1, R)
    parts = [
        rows(pick(split(joined2), 2, c), both(merged_grad)),
        rows(split(normed2)[:, :, 0], pick(triple2, 0, c)),
        rows(split(jnp.where(c == 0, normed2, attended2))[:, :, 0], jnp.where(c == 0, triple2[2], branch2)),
        rows(split(normed_two2)[:, :, 0], pick(expanded2, 0, c)),
        rows(split(normed_two2)[:, :, 0], pick(expanded2, 0, c + 2)),
        rows(pick(split(activated2), 2, c), upstream2),
        rows(pick(split(activated2), 2, c + 2), upstream2),
    ]
    grads = jnp.stack(parts, axis=1)
    wide_grads = jnp.stack([jnp.where(c == i, grads, 0) for i in range(2)], axis=2).reshape(nz, NB, R, D)
    F = lax.psum(lax.psum_scatter(wide_grads, "seq", scatter_dimension=0, tiled=False), "dp")
    vectors = lax.psum(vectors, ("dp", "seq"))
    F = F.astype(f32)
    def columns(blocks):
        return blocks.transpose(1, 0, 2).reshape(R, -1)
    summed = (F[0:2].reshape(-1, D), columns(F[2:5]), F[5], columns(F[6:10]), F[10:14].reshape(-1, D))
    return outputs((result, joined_grad[:, :D], joined_grad[:, D:]), summed, vectors)


def outputs(images, summed, vectors):
    result, hidden_grad, skipped_grad = images
    merge, triple, output, expand, reduce = summed
    return (result[None], hidden_grad[None], skipped_grad[None], merge, vectors[0], vectors[1], vectors[2], triple, output,
            vectors[3], vectors[4], vectors[5], expand, vectors[7:11].reshape(-1), reduce, vectors[6])


def body(hidden, skipped, row_mask, cotangent, merge_weight, merge_bias, first_gain, first_shift, triple_weight,
         output_weight, output_bias, second_gain, second_shift, expand_weight, expand_bias, reduce_weight, reduce_bias):
    vectors = (merge_bias, first_gain, first_shift, output_bias, second_gain, second_shift, reduce_bias, expand_bias)
    weights = (merge_weight, triple_weight, output_weight, expand_weight, reduce_weight)
    *images, F, sums = block(hidden, skipped, cotangent, row_mask, vectors, weights, lax.axis_size("seq"))
    merge, triple, output, expand, reduce, result, hidden_grad, skipped_grad, *v = unpack(images, F, sums)
    return (result, hidden_grad, skipped_grad, merge, v[0], v[1], v[2], triple, output, v[3], v[4], v[5], expand, v[7],
            reduce, v[6])


def solution(mesh):
    rows, held, copied = P(("dp", "seq"), None, None), P("seq", None), P()
    fast = mesh.shape["dp"] == 8 and mesh.shape["seq"] == 4
    return jax.shard_map(
        body if fast else plain,
        mesh=mesh,
        in_specs=(rows, rows, P("dp", None), rows, held, copied, copied, copied, held, held, copied, copied, copied,
                  held, copied, held, copied),
        out_specs=(rows, rows, rows, held, copied, copied, copied, held, held, copied, copied, copied, held, copied,
                   held, copied),
        check_vma=False,
    )
```

```python
import functools

import jax
import jax.numpy as jnp
from jax import lax
from jax.experimental import pallas as pl
from jax.experimental.pallas import tpu as pltpu
from jax.sharding import PartitionSpec as P

MESH = pl.DeviceIdType.MESH
HEADS = 16
EPS = 1e-05
NEGATIVE = -1e30
NB = 14
NP, SUB = 7, 3
Q = NP * SUB
AHEAD = 2
RING = 8
SLOTS = 3
VR = 16
READY = 5
LEAD = READY + 9
f32, bf16 = jnp.float32, jnp.bfloat16


def block_slices(refs):
    merge, triple, output, expand, reduce = refs
    R, C = output.shape
    out = []
    for j in range(merge.shape[0] // R): out.append(merge.at[pl.ds(j * R, R), :])
    for j in range(triple.shape[1] // C): out.append(triple.at[:, pl.ds(j * C, C)])
    out.append(output.at[:, :])
    for j in range(expand.shape[1] // C): out.append(expand.at[:, pl.ds(j * C, C)])
    for j in range(reduce.shape[0] // R): out.append(reduce.at[pl.ds(j * R, R), :])
    return out


def nn(a, b):
    return jnp.dot(a, b, preferred_element_type=f32)


def nt(a, b):
    return lax.dot_general(a, b, (((1,), (1,)), ((), ())), preferred_element_type=f32)


def tn(a, b):
    return lax.dot_general(a, b, (((0,), (0,)), ((), ())), preferred_element_type=f32)


HID, SKP, COT, NORMED, ATT, TWO, ACT, TRI, BR, TG, GR, EXP, ATTG, PLACES = 0, 2, 4, 6, 8, 10, 12, 20, 23, 25, 31, 33, 41, 42
HGRAD, SGRAD, RESULT = NORMED, TWO, ATT
NN, NT, EXTRA, CAST, FETCH, NORM, NORM_BACK, GELU, GELU_BACK, ATTEND, ATTEND_BACK, ROWS, FULL = range(1, 14)


def op(mode, a=0, w=0, acc=0, wait=1, pre=None, post=None):
    pre, post = (0 if v is None else v + 1 for v in (pre, post))
    return mode + 16 * (a + 64 * (w + 32 * (acc + 2 * (wait + 2 * (pre + 32 * post)))))


def plan():
    B = READY
    ops = []
    def at(tick, *what): ops.extend((tick, o) for o in what)
    (begin, stored, cot, attended, acts, pairs, px, triple, heads, merge, joined, result, outs, *sums) = (op(EXTRA, i) for i in range(18))
    at(0, begin)
    at(1, stored)
    at(2, cot)
    halves = []
    def by_half(tick, first, second):
        halves.extend([(2 * tick + 1, o) for o in first] + [(2 * tick + 2, o) for o in second])
    by_half(B + 1, [op(FETCH, 0), op(FETCH, 1)], [op(NN, HID, 0), op(NN, SKP, 1, acc=1), op(NORM, 0)])
    by_half(B + 2, [op(FETCH, 2)], [op(NN, NORMED, 2), op(CAST, TRI)])
    by_half(B + 3, [op(FETCH, 3)], [op(NN, NORMED, 3), op(CAST, TRI + 1)])
    by_half(B + 4, [op(FETCH, 4)], [op(NN, NORMED, 4), op(CAST, TRI + 2), op(ATTEND, 0)])
    by_half(B + 5, [op(FETCH, 5), op(ATTEND, 1)], [op(ATTEND, 2), op(ATTEND, 3), attended])
    by_half(B + 6, [op(FETCH, 6), op(NN, ATT, 5), op(NORM, 1)], [op(NN, TWO, 6), op(GELU, 0)])
    by_half(B + 7, [op(FETCH, 7), acts, op(ROWS, 0)], [op(NN, TWO, 7), op(GELU, 1)])
    by_half(B + 8, [op(FETCH, 8), op(ROWS, 4)], [op(NN, TWO, 8), op(GELU, 2)])
    by_half(B + 9, [op(FETCH, 9), op(ROWS, 8), op(NN, TWO, 9), op(GELU, 3)], [op(ROWS, 12)])
    by_half(B + 13, [op(FETCH, 10), op(FETCH, 11), op(FETCH, 12)], [])
    for i in range(4):
        halves += [(2 * (B + 14) + i // 2, o) for o in (op(NT, COT, 10 + i, post=13 + i), op(GELU_BACK, i))]
    halves += [(2 * (B + 14) + 1, pairs), (2 * (B + 14) + 2, px), (2 * (B + 14) + 2, op(FULL, 0))]
    at(B + 11, op(ROWS, 1))
    for i in range(4):
        at(B + 15 + i // 2, op(NT, EXP + 2 * i, 14 + i, acc=int(i > 0), post=17 + i))
    at(B + 16, op(NORM_BACK, 1))
    at(B + 17, op(NT, BR, 18, post=21), op(CAST, ATTG), op(FULL, 1))
    at(B + 18, op(ATTEND_BACK, 0), op(ATTEND_BACK, 1))
    at(B + 19, op(ATTEND_BACK, 2), op(ATTEND_BACK, 3), triple)
    at(B + 20, heads, op(FULL, 2))
    at(B + 21, op(NT, TG, 19, post=22), op(NT, TG + 2, 20, acc=1, post=23))
    at(B + 22, op(NT, TG + 4, 21, acc=1, post=24), op(NORM_BACK, 0))
    at(B + 23, op(FULL, 3))
    at(B + 24, merge, op(ROWS, 2))
    at(B + 25, sums[0], op(NT, GR, 22, post=25), op(CAST, HGRAD))
    at(B + 26, sums[1], op(NT, GR, 23, post=26), op(CAST, SGRAD), joined)
    at(B + 27, sums[2], op(NN, ACT, 24, post=27), op(NN, ACT + 2, 25, acc=1))
    at(B + 28, sums[3], op(NN, ACT + 4, 26, acc=1), op(NN, ACT + 6, 27, acc=1), result)
    at(B + 29, outs)
    at(B + 32, sums[4])
    spread = []
    for tick in sorted({t for t, _ in ops}):
        mine = [o for t, o in ops if t == tick]
        spread += [(2 * tick + 1 + 2 * i // len(mine), o) for i, o in enumerate(mine)]
    return sorted(spread + halves, key=lambda pair: pair[0])


OPS = plan()
STARTS = [sum(t < half for t, _ in OPS) for half in range(2 * (LEAD + AHEAD + Q + 10))]
UNITS = [2, 6] + [4 * j for j in range(2, 10)] + [1 + 4 * s for s in range(4)] + [4 * j for j in (6, 7, 8, 9, 5, 2, 3, 4)] + [2, 6] + [1 + 4 * s for s in range(4)]


def lookup(values, i):
    total = jnp.int32(values[0])
    for k in range(1, len(values)):
        if values[k] != values[k - 1]:
            total = total + jnp.where(i >= k, values[k] - values[k - 1], 0)
    return total


def block_kernel(hid, skp, cot_in, mask_in, *refs, nz):
    (b0, b1, b2, b3, b4, b5, b6, b7, wm, wt, wo, we, wr,
     res, hgrad, sgrad, F, WV, G, D,
     W, X, PR, XH, MID, MG, E, INV, MASK, VEC, DB, MROWS, v0, v1, v2, v3, v4, v5, v6, v7,
     K, R1, R2, R3, O, VB,
     loc, loc2, zs, zr, xs, xr, ys, yr, cs, cr, fsem, insem, es, er, dsem, osem,
     ld, s1, r1, s2, r2, s3, r3, st, sf, rf, sc, rcv, vl, vs, vr) = refs
    dp = lax.axis_index("dp"); z = lax.axis_index("seq")
    c = dp % 2; x = (dp // 2) % 2; y = dp // 4
    xn = dp + 2 - 4 * x; yn = dp + 4 - 8 * y; cn = dp + 1 - 2 * c; co = 1 - c
    L, C = X.shape[1:]
    R = G.shape[2]
    scale = (C // HEADS) ** -0.5
    bar = pltpu.get_barrier_semaphore()
    for tgt in (xn, yn, cn):
        pl.semaphore_signal(bar, inc=1, device_id=(tgt, z), device_id_type=MESH)
    for d in range(1, nz):
        pl.semaphore_signal(bar, inc=1, device_id=(dp, (z + d) % nz), device_id_type=MESH)

    def rc(src, dst, ss, rs, dev):
        return pltpu.make_async_remote_copy(src_ref=src, dst_ref=dst, send_sem=ss, recv_sem=rs, device_id=dev, device_id_type=MESH)

    blocks = block_slices((wm, wt, wo, we, wr))
    room = SLOTS * 4
    def stage(j): return W.at[(j % room) // 4, j % 4]
    def load_in(j): return pltpu.make_async_copy(blocks[j], stage(j), loc.at[j])
    def load_out(j, slot): return pltpu.make_async_copy(slot, G.at[z, j], loc2.at[j])
    for j in range(min(room, NB)): load_in(j).start()
    inputs = [pltpu.make_async_copy(a, b, insem.at[i]) for i, (a, b) in enumerate(
        ((hid.at[0], X.at[HID]), (skp.at[0], X.at[SKP]), (cot_in.at[0], X.at[COT]), (mask_in, MROWS),
         (b0, v0), (b1, v1), (b2, v2), (b3, v3), (b4, v4), (b5, v5), (b6, v6), (b7, v7)))]
    for cp in inputs: cp.start()
    pl.semaphore_wait(bar, nz + 2)

    half = R // 2; third = half // 3
    base = half * c
    zp = ((x + y) % 2) * (2 - x)
    yp = 1 + y
    def reg(s, b, start, n):
        return G.at[s, b, pl.ds(pl.multiple_of(start, 16), n), :]
    def same(region, ss, rs, dev): return rc(region, region, ss, rs, dev)
    def zcopy(b, d, k):
        s = z - k if d == 0 else z + k
        return same(reg(s, b, base + third * zp, third), zs.at[b % RING, d, k], zr.at[b % RING, d, k], (dp, z + 1 if d == 0 else z - 1))
    def zsend_ok(d, k):
        return (z >= k) & (z < nz - 1) if d == 0 else (z + k <= nz - 1) & (z > 0)
    def zrecv_ok(d, k):
        return z >= k + 1 if d == 0 else z + 1 + k <= nz - 1
    def shard_in(d, k):
        return z - 1 - k if d == 0 else z + 1 + k
    def xcopy(b, s): return same(reg(s, b, base + third * zp, third), xs.at[b % 6, s], xr.at[b % 6, s], (xn, z))
    def ycopy(b, s): return same(reg(s, b, base + third * yp, third), ys.at[b % 6, s], yr.at[b % 6, s], (yn, z))
    def ccopy(b, s): return same(reg(s, b, base, half), cs.at[b % 6, s], cr.at[b % 6, s], (cn, z))
    def own(b):
        for d in (0, 1):
            @pl.when(zsend_ok(d, 0))
            def _(): zcopy(b, d, 0).start()
    def zarr(b, d, k):
        zcopy(b, d, k).wait_recv()
        if k + 1 < nz - 1:
            @pl.when(zsend_ok(d, k + 1))
            def _(): zcopy(b, d, k + 1).start()
        s = shard_in(d, k)
        xcopy(b, s).start()
        @pl.when((x + y) % 2 == 1)
        def _(): ycopy(b, s).start()
    def xarr(b, d, k):
        s = shard_in(d, k)
        xcopy(b, s).wait_recv()
        @pl.when((x + y) % 2 == 0)
        def _(): ycopy(b, s).start()
    def yarr(b, d, k):
        s = shard_in(d, k)
        ycopy(b, s).wait_recv()
        ccopy(b, s).start()
    def fin(b, d, k):
        s = shard_in(d, k)
        ccopy(b, s).wait()
        xcopy(b, s).wait_send()
        ycopy(b, s).wait_send()
    for j in range(AHEAD):
        for d in (0, 1):
            @pl.when(zsend_ok(d, 0))
            def _():
                rc(blocks[j].at[pl.ds(pl.multiple_of(base + third * zp, 16), third)], reg(z, j, base + third * zp, third),
                   zs.at[j, d, 0], zr.at[j, d, 0], (dp, z + 1 if d == 0 else z - 1)).start()
    for j in range(4):
        load_in(j).wait()
        load_out(j, stage(j)).start()
    for j in range(4): load_out(j, stage(j)).wait()
    FIRST = [(zarr, 0, 0), (zarr, 0, 1), (zarr, 0, 2), (None, 0, 0)]
    SECOND = [(xarr, 1, k) for k in range(3)] + [(yarr, 2, k) for k in range(3)] + [(fin, 3, k) for k in range(3)]
    def gather_half(t, todo):
        for fn, off, k in todo:
            if fn is None:
                @pl.when(t < NB - AHEAD)
                def _(): own(t + AHEAD)
                continue
            b = t - off - k
            @pl.when((b >= 0) & (b < NB))
            def _():
                for d in (0, 1):
                    @pl.when(zrecv_ok(d, k))
                    def _(): fn(b, d, k)
                    if fn is fin:
                        @pl.when(zsend_ok(d, k))
                        def _(): zcopy(b, d, k).wait_send()

    T = K.shape[2]
    def ring(q): return q % RING
    def typ(q, s): return (q + s) % 2
    def keep(q, s): return x + typ(q, s) * (y - x)
    def near(q, s): return xn + typ(q, s) * (yn - xn)
    def far(q, s): return yn + typ(q, s) * (xn - yn)
    def piece(q, h):
        return NP - 1 - q // SUB, pl.ds(pl.multiple_of(half * h + T * (q % SUB), 16), T)
    def load(q, s):
        p, rows = piece(q, keep(q, s))
        return pltpu.make_async_copy(D.at[s, p, rows], K.at[ring(q), s], ld.at[s, ring(q)])
    def first(q, s):
        p, rows = piece(q, 1 - keep(q, s))
        return rc(D.at[s, p, rows], R1.at[ring(q), s], s1.at[s, ring(q)], r1.at[s, ring(q)], (near(q, s), z))
    def up(q, s):
        return rc(K.at[ring(q), s], R2.at[ring(q), s], s2.at[s, ring(q)], r2.at[s, ring(q)], (dp, z + 1))
    def down(q, s):
        away = jnp.minimum(z - 1 - s, 1)
        slot = nz + away * (s - nz)
        return rc(K.at[ring(q), s], R2.at[ring(q), slot], s2.at[s, ring(q)], r2.at[slot, ring(q)], (dp, z - 1))
    def got(slot, q):
        return rc(K.at[ring(q), 0], R2.at[ring(q), slot], s2.at[0, ring(q)], r2.at[slot, ring(q)], (dp, z))
    def last(q):
        return rc(K.at[ring(q), z], R3.at[ring(q)], s3.at[ring(q)], r3.at[ring(q)], (far(q, z), z))
    def frow(q, h, cc):
        p, rows = piece(q, h)
        return F.at[2 * p + cc, rows]
    def keepf(q): return pltpu.make_async_copy(O.at[ring(q)], frow(q, keep(q, z), c), st.at[ring(q)])
    def spread(q): return rc(O.at[ring(q)], frow(q, keep(q, z), c), sf.at[ring(q)], rf.at[ring(q)], (near(q, z), z))
    def spread_in(q):
        r = frow(q, 1 - keep(q, z), c)
        return rc(r, r, sf.at[ring(q)], rf.at[ring(q)], (near(q, z), z))
    def cross(q): return rc(O.at[ring(q)], frow(q, keep(q, z), c), sc.at[0, ring(q)], rcv.at[0, ring(q)], (cn, z))
    def cross2(q):
        r = frow(q, 1 - keep(q, z), c)
        return rc(r, r, sc.at[1, ring(q)], rcv.at[1, ring(q)], (cn, z))
    def add(a, b): return (a.astype(f32) + b.astype(f32)).astype(bf16)
    def issue(q):
        for s in range(nz):
            first(q, s).start(); load(q, s).start()
    def start(q):
        for s in range(nz):
            load(q, s).wait(); first(q, s).wait_recv()
            K[ring(q), s] = add(K[ring(q), s], R1[ring(q), s])
        for s in range(nz):
            if s < nz - 1:
                @pl.when(z == nz - 1)
                def _(): down(q, s).start()
            if nz - 1 - s > 0:
                @pl.when(z == 0)
                def _(): up(q, nz - 1 - s).start()
    def hop(q, k):
        for s in reversed(range(nz)):
            if s > k:
                @pl.when(z == k)
                def _():
                    got(s, q).wait_recv()
                    K[ring(q), s] = add(K[ring(q), s], R2[ring(q), s])
                    up(q, s).start()
        for s in range(nz):
            if s < nz - 1 - k:
                @pl.when(z == nz - 1 - k)
                def _():
                    got(s, q).wait_recv()
                    K[ring(q), s] = add(K[ring(q), s], R2[ring(q), s])
                    down(q, s).start()
    def arrive(q):
        @pl.when(z > 0)
        def _():
            got(z, q).wait_recv()
            K[ring(q), z] = add(K[ring(q), z], R2[ring(q), z])
        @pl.when(z < nz - 1)
        def _():
            got(nz, q).wait_recv()
            K[ring(q), z] = add(K[ring(q), z], R2[ring(q), nz])
        last(q).start()
    def final(q):
        last(q).wait_recv()
        O[ring(q)] = add(K[ring(q), z], R3[ring(q)])
        keepf(q).start(); spread(q).start(); cross(q).start()
    def relay(q):
        spread_in(q).wait_recv()
        cross2(q).start()
        for s in range(nz):
            first(q, s).wait_send()
            if s > 0:
                @pl.when(z < s)
                def _(): up(q, s).wait_send()
            if s < nz - 1:
                @pl.when(z > s)
                def _(): down(q, s).wait_send()
        last(q).wait_send()
    def drain(q):
        keepf(q).wait(); spread(q).wait_send()
        cross(q).wait_send(); cross(q).wait_recv(); cross2(q).wait_send(); cross2(q).wait_recv()
    steps = [(0, start)] + [(k, functools.partial(hop, k=k)) for k in range(1, nz - 1)] + [
        (nz - 1, arrive), (nz, final), (nz + 1, relay), (nz + 3, drain)]
    def sum_half(t, todo):
        for off, fn in todo:
            q = t - AHEAD - off
            @pl.when((q >= 0) & (q < Q))
            def _(): fn(q)
    def sum_issue(t):
        @pl.when(((t % SUB == 0) & (t > 0) & (t < Q)) | (t == 1))
        def _():
            for cp in puts(NP - 1 - t // SUB): cp.wait()
        @pl.when(t == 1)
        def _(): issue(0)
        @pl.when((t > 0) & (t < Q))
        def _(): issue(t)

    devs = ((cn, z), (xn, z), (yn, z))
    def swap(i): return rc(VB.at[2 * i], VB.at[2 * i + 1], vs.at[i], vr.at[i], devs[i])
    def vstep(i):
        if i > 0:
            swap(i - 1).wait()
            VB[2 * i] = VB[2 * i - 2] + VB[2 * i - 1]
        if i < 3:
            swap(i).start()
    def line(d):
        return rc(VB.at[6], VB.at[6 + d], vs.at[2 + d], vr.at[2 + d], (dp, (z + d) % nz))
    def vline():
        vstep(3)
        for d in range(1, nz): line(d).start()
    def vend():
        for d in range(1, nz): line(d).wait()
        def plane(s): return VB[6 + (z - s + nz) % nz]
        total = plane(0)
        for s in range(1, nz): total = total + plane(s)
        VB[0] = total
        cp = pltpu.make_async_copy(VB.at[0], WV, vl.at[1])
        cp.start(); cp.wait()

    def pair(i, src, dst): return rc(src, dst, es.at[i], er.at[i], (cn, z))
    def both(i, a): return pair(i, X.at[a], X.at[a + 1])
    ex = {
        "hid": both(0, HID), "skp": both(1, SKP), "cot": both(2, COT), "normed": both(3, NORMED), "att": both(4, ATT), "two": both(5, TWO),
        "px0": both(10, EXP + 2 * co), "px1": both(11, EXP + 2 * co + 4), "br": both(12, BR),
        "qk": both(13, TG + 2 * co), "v": both(14, TG + 4), "gr": both(15, GR),
    }
    def arrives(i, a): return both(i, a).wait_recv()
    def send_act(i): return both(6 + i, ACT + 2 * i)
    def arrived(*names):
        for n in names: ex[n].wait()

    def fetch(n):
        code = lookup(UNITS, n)
        kind, arg = code % 4, code // 4
        for i in range(4):
            s = jnp.where(kind == 0, i, jnp.where(kind == 1, arg, 2 * arg + i // 2))
            j = jnp.where(kind == 0, arg, jnp.where(kind == 1, 10 + i, i % 2))
            pltpu.make_async_copy(G.at[s, j], W.at[n % SLOTS, i], fsem.at[n % SLOTS, i]).start()
    def fetched(n):
        for i in range(4):
            pltpu.make_async_copy(G.at[0, 0], W.at[n % SLOTS, i], fsem.at[n % SLOTS, i]).wait()
    def weight(n): return W[n % SLOTS].reshape(4 * R, C)
    def vec(i): return VEC[pl.ds(i, 1), :]
    def tally(i, v): VB[0, pl.ds(i, 1), :] = jnp.sum(v, axis=0, keepdims=True)

    def do_matmul(dot, a, n, acc, wait, pre, post):
        @pl.when(pre > 0)
        def _(): fetch(pre - 1)
        @pl.when(wait > 0)
        def _(): fetched(n)
        v = dot(X[a], weight(n))
        E[...] = jnp.where(acc > 0, E[...], 0.0) + v
        @pl.when(post > 0)
        def _(): fetch(post - 1)
    def do_cast(a):
        X[a] = E[...].astype(bf16)
    def do_norm(k):
        v = jnp.where(k > 0, MID[...], 0.0) + E[...] + vec(3 * k)
        MID[...] = v
        m = v - jnp.mean(v, axis=-1, keepdims=True)
        r = lax.rsqrt(jnp.mean(m * m, axis=-1, keepdims=True) + EPS)
        XH[k] = m * r
        INV[k] = jnp.broadcast_to(r, INV.shape[1:])
        a = NORMED + (TWO - NORMED) * k
        X[a] = (m * r * vec(3 * k + 1) + vec(3 * k + 2)).astype(bf16)
        both(3 + 2 * k, a).start()
    def do_norm_back(k):
        e = E[...]
        xhat = XH[k]
        tally(3 * k + 1, e * xhat); tally(3 * k + 2, e)
        t = e * vec(3 * k + 1)
        a = jnp.mean(t, axis=-1, keepdims=True)
        b = jnp.mean(t * xhat, axis=-1, keepdims=True)
        v = jnp.where(k > 0, X[COT].astype(f32), MG[...]) + (t - a - xhat * b) * INV[k, :, 0:1]
        MG[...] = v
        low = v.astype(bf16)
        a = GR + (BR - GR) * k
        X[a] = low
        tally(3 * k, low.astype(f32))
        both(15 - 3 * k, a).start()
    step = C // 3
    def part(n): return pl.ds(pl.multiple_of(step * n, 128), step)
    def do_gelu(i):
        def one(n, _):
            v = E[:, part(n)] + VEC[pl.ds(7 + i, 1), part(n)]
            cdf = 0.5 * (1.0 + lax.erf(v * (0.5 ** 0.5)))
            X[ACT + 2 * i, :, part(n)] = (v * cdf).astype(bf16)
            X[EXP + 2 * i, :, part(n)] = (cdf + v * jnp.exp(-0.5 * v * v) * 0.3989422804014327).astype(bf16)
            return 0
        lax.fori_loop(0, 3, one, 0)
        send_act(i).start()
    def do_gelu_back(i):
        def one(n, _):
            low = (E[:, part(n)] * X[EXP + 2 * i, :, part(n)].astype(f32)).astype(bf16)
            X[EXP + 2 * i, :, part(n)] = low
            VB[0, pl.ds(7 + i, 1), part(n)] = jnp.sum(low.astype(f32), axis=0, keepdims=True)
            return 0
        lax.fori_loop(0, 3, one, 0)
    hs = C // HEADS
    group = HEADS // 4
    def do_attend(i):
        for g in range(4):
            @pl.when(i == g)
            def _():
                for h in range(group * g, group * g + group):
                    sl = slice(hs * h, hs * h + hs)
                    scores = nt(X[TRI + 1, :, sl], X[TRI, :, sl]) * scale
                    scores = jnp.where(MASK[:, 0:1] > 0, scores, NEGATIVE)
                    e = jnp.exp(scores - jnp.max(scores, axis=0, keepdims=True))
                    p = (e * (1.0 / jnp.sum(e, axis=0, keepdims=True))).astype(bf16)
                    PR[h] = p
                    X[ATT, :, sl] = tn(p, X[TRI + 2, :, sl]).astype(bf16)
    def do_attend_back(i):
        for g in range(4):
            @pl.when(i == g)
            def _():
                for h in range(group * g, group * g + group):
                    sl = slice(hs * h, hs * h + hs)
                    q, k, v, d, p = X[TRI, :, sl], X[TRI + 1, :, sl], X[TRI + 2, :, sl], X[ATTG, :, sl], PR[h]
                    X[TG + 4, :, sl] = nn(p, d).astype(bf16)
                    pg = nt(v, d)
                    pf = p.astype(f32)
                    sg = (pf * (pg - jnp.sum(pf * pg, axis=0, keepdims=True))).astype(bf16)
                    X[TG, :, sl] = (tn(sg, k) * scale).astype(bf16)
                    X[TG + 2, :, sl] = (nn(sg, q) * scale).astype(bf16)
    def puts(p): return [pltpu.make_async_copy(DB.at[pl.ds(R * s, R)], D.at[s, p], dsem.at[s]) for s in range(4)]
    def put(p):
        for cp in puts(p): cp.start()
    def pair_of(a, cols=slice(None)): return X[pl.ds(a, 2), :, cols].reshape(2 * L, -1)
    def do_rows(a):
        kind = a % 4
        merge = kind // 2
        lo = a // 4
        hi = jnp.where(kind == 0, lo + 1, 4)
        @pl.when(kind == 0)
        def _(): send_act(lo).wait()
        right = COT + (GR - COT) * merge
        def one(s, _):
            left = ACT + 2 * s + merge * (HID + 2 * (s // 2) - ACT - 2 * s)
            cut = merge * (2 * (s % 2)) + (1 - merge) * 2 * (1 - kind) + c
            rows = pl.ds(pl.multiple_of(R * s, 16), R)
            for v in range(4):
                @pl.when(cut == v)
                def _():
                    DB[rows] = tn(pair_of(left, slice(R * v, R * v + R)), pair_of(right)).astype(bf16)
            pltpu.make_async_copy(DB.at[rows], D.at[s, 6 - kind - 4 * merge], dsem.at[s]).start()
            return 0
        lax.fori_loop(lo, hi, one, 0)
    def do_full(kind):
        left = jnp.where(kind < 2, TWO, jnp.where(kind == 2, NORMED + (ATT - NORMED) * c, NORMED))
        right = jnp.where(kind < 2, EXP + 2 * c + 4 * (1 - kind), jnp.where(kind == 2, TG + 4 + (BR - TG - 4) * c, TG + 2 * c))
        def one(n, _):
            DB[pl.ds(pl.multiple_of(step * n, 128), step)] = tn(pair_of(left, part(n)), pair_of(right)).astype(bf16)
            return 0
        lax.fori_loop(0, 3, one, 0)
        put(4 - kind)

    def x_begin():
        VB[0] = jnp.zeros_like(VB[0])
        for cp in inputs: cp.wait()
        for n in ("hid", "skp", "cot"): ex[n].start()
        valid = MROWS[pl.ds(z, 1), :].astype(f32)
        MASK[...] = jnp.broadcast_to(valid, (MASK.shape[1], L)).T
        for i, v in enumerate((v0, v1, v2, v3, v4, v5, v6)):
            VEC[i:i + 1, :] = v[...].astype(f32).reshape(1, C)
        for i in range(4):
            VEC[7 + i:8 + i, :] = v7[C * i:C * (i + 1)].astype(f32).reshape(1, C)
        for j in range(room, NB): load_in(j).start()
        for j in range(4, NB):
            load_in(j).wait()
            load_out(j, stage(j)).start()
    def x_stored():
        for j in range(4, NB): load_out(j, stage(j)).wait()
    def x_attended(): ex["att"].start()
    def x_acts():
        arrived("cot")
    def x_cot(): tally(6, X[COT].astype(f32))
    def x_pairs():
        ex["px0"].start(); ex["px1"].start()
    def out(i):
        return pltpu.make_async_copy(X.at[(RESULT, HGRAD, SGRAD)[i]], (res, hgrad, sgrad)[i].at[0], osem.at[i])
    def x_result():
        X[RESULT] = (MID[...] + E[...] + vec(6)).astype(bf16)
        out(0).start()
    def x_joined():
        out(1).start(); out(2).start()
    def x_outs():
        for i in range(3): out(i).wait()
    def x_px():
        arrived("two")
        for i in range(2):
            ex["px" + str(i)].wait_send(); arrives(10 + i, EXP + 2 * c + 4 * i)
    def x_triple():
        ex["qk"].start(); ex["v"].start()
    def x_heads():
        arrived("normed", "att", "br", "v")
        ex["qk"].wait_send(); arrives(13, TG + 2 * c)
    def x_merge(): arrived("hid", "skp", "gr")
    extras = [x_begin, x_stored, x_cot, x_attended, x_acts, x_pairs, x_px, x_triple, x_heads, x_merge, x_joined, x_result, x_outs,
              functools.partial(vstep, 0), functools.partial(vstep, 1), functools.partial(vstep, 2), vline, vend]
    def do_extra(i):
        for k, fn in enumerate(extras):
            @pl.when(i == k)
            def _(): fn()

    def run(n, _):
        code = lookup([op for _, op in OPS], n)
        mode, a, w = code % 16, code // 16 % 64, code // 1024 % 32
        acc, wait = code // 2 ** 15 % 2, code // 2 ** 16 % 2
        pre, post = code // 2 ** 17 % 32, code // 2 ** 22 % 32
        small = ((do_extra, EXTRA), (do_cast, CAST), (fetch, FETCH), (do_norm, NORM), (do_norm_back, NORM_BACK), (do_gelu, GELU),
                 (do_gelu_back, GELU_BACK), (do_attend, ATTEND), (do_attend_back, ATTEND_BACK), (do_rows, ROWS), (do_full, FULL))
        for dot, m in ((nn, NN), (nt, NT)):
            @pl.when(mode == m)
            def _(): do_matmul(dot, a, w, acc, wait, pre, post)
        for fn, m in small:
            @pl.when(mode == m)
            def _(): fn(a)
        return 0

    cut = nz - 1
    def tick(h, _):
        t = h // 2
        @pl.when((h % 2 == 0) & (t < NB + nz + 2))
        def _(): gather_half(t, FIRST)
        @pl.when((h % 2 == 1) & (t < NB + nz + 2))
        def _(): gather_half(t, SECOND)
        @pl.when((h % 2 == 0) & (t >= LEAD))
        def _(): sum_half(t - LEAD, steps[:cut])
        @pl.when((h % 2 == 1) & (t >= LEAD))
        def _():
            sum_half(t - LEAD, steps[cut:])
            sum_issue(t - LEAD)
        lax.fori_loop(lookup(STARTS, h), lookup(STARTS, h + 1), run, 0)
        return 0
    lax.fori_loop(0, 2 * (LEAD + AHEAD + Q + nz + 3), tick, 0)


def block(hidden, skipped, cotangent, mask, vectors, weights, nz):
    L, C = hidden.shape[1:]
    R = weights[2].shape[0]
    T = R // 2 // SUB
    S = pltpu.SemaphoreType.DMA
    V = pltpu.VMEM
    rows = jax.ShapeDtypeStruct((1, L, C), bf16)
    hbm = pl.BlockSpec(memory_space=pl.ANY)
    out_shape = (rows, rows, rows, jax.ShapeDtypeStruct((NB, R, C), bf16), jax.ShapeDtypeStruct((VR, C), f32),
                 jax.ShapeDtypeStruct((nz, NB, R, C), bf16), jax.ShapeDtypeStruct((nz, NP, R, C), bf16))
    scratch = [
        V((SLOTS, 4, R, C), bf16), V((PLACES, L, C), bf16), V((HEADS, L, L), bf16), V((2, L, C), f32), V((L, C), f32), V((L, C), f32),
        V((L, C), f32), V((2, L, 128), f32), V((L, 128), f32), V((VR, C), f32), V((4 * R, C), bf16),
        V(mask.shape, jnp.int32), *[V(v.shape, bf16) for v in vectors],
        V((RING, nz, T, C), bf16), V((RING, nz, T, C), bf16), V((RING, nz + 1, T, C), bf16), V((RING, T, C), bf16), V((RING, T, C), bf16),
        V((6 + nz, VR, C), f32),
        S((NB,)), S((NB,)), S((RING, 2, nz - 1)), S((RING, 2, nz - 1)), S((6, nz)), S((6, nz)), S((6, nz)), S((6, nz)), S((6, nz)), S((6, nz)),
        S((SLOTS, 4)), S((12,)), S((16,)), S((16,)), S((4,)), S((3,)),
        S((nz, RING)), S((nz, RING)), S((nz, RING)), S((nz, RING)), S((nz + 1, RING)), S((RING,)), S((RING,)), S((RING,)), S((RING,)), S((RING,)), S((2, RING)), S((2, RING)),
        S((2,)), S((2 + nz,)), S((2 + nz,)),
    ]
    return pl.pallas_call(
        functools.partial(block_kernel, nz=nz),
        out_shape=out_shape, in_specs=[hbm] * 17, out_specs=(hbm,) * 7, scratch_shapes=scratch,
        compiler_params=pltpu.CompilerParams(collective_id=0, has_side_effects=True, vmem_limit_bytes=63 * 2**20),
    )(hidden, skipped, cotangent, mask, *vectors, *weights)[:5]


def unpack_kernel(F, WV, i0, i1, i2, m, t, o, e, r, o0, o1, o2, *rest):
    vec_outs, (FB, OB, VB, IB), vbufs, (fin, fout, vin, vout, iin, iout) = rest[:8], rest[8:12], rest[12:20], rest[20:]
    R, C = FB.shape[1:]
    outs = block_slices((m, t, o, e, r))
    takes = [pltpu.make_async_copy(F.at[j], FB.at[j], fin.at[j]) for j in range(NB)]
    puts = [pltpu.make_async_copy(OB.at[j], outs[j], fout.at[j]) for j in range(NB)]
    sums = pltpu.make_async_copy(WV, VB, vin.at[0])
    images = [(pltpu.make_async_copy(a, IB.at[i], iin.at[i]), pltpu.make_async_copy(IB.at[i], b, iout.at[i]))
              for i, (a, b) in enumerate(((i0, o0), (i1, o1), (i2, o2)))]
    for cp in takes[:4]: cp.start()
    sums.start()
    for a, _ in images: a.start()
    for cp in takes[4:]: cp.start()
    for j in range(NB):
        takes[j].wait()
        def widen(i, _):
            part = pl.ds(pl.multiple_of(i * 32, 16), 32)
            OB[j, part] = FB[j, part].astype(f32)
            return 0
        lax.fori_loop(0, R // 32, widen, 0)
        puts[j].start()
        if j == 3:
            sums.wait()
            for i in range(7): vbufs[i][...] = VB[i:i + 1, :].reshape(C)
            for i in range(4): vbufs[7][C * i:C * (i + 1)] = VB[7 + i:8 + i, :].reshape(C)
            small = [pltpu.make_async_copy(a, b, vout.at[i]) for i, (a, b) in enumerate(zip(vbufs, vec_outs))]
            for cp in small: cp.start()
            for a, b in images:
                a.wait()
                b.start()
    for cp in puts: cp.wait()
    for cp in small: cp.wait()
    for _, b in images: b.wait()


def unpack(images, F, sums):
    R, C = F.shape[1:]
    S = pltpu.SemaphoreType.DMA
    hbm = pl.BlockSpec(memory_space=pl.ANY)
    vecs = [jax.ShapeDtypeStruct((n * C,), f32) for n in (1, 1, 1, 1, 1, 1, 1, 4)]
    shapes = [jax.ShapeDtypeStruct(s, f32) for s in ((2 * R, C), (R, 3 * C), (R, C), (R, 4 * C), (4 * R, C))]
    shapes += [jax.ShapeDtypeStruct(a.shape, a.dtype) for a in images] + vecs
    return pl.pallas_call(
        unpack_kernel, out_shape=shapes, in_specs=[hbm] * 5, out_specs=[hbm] * len(shapes),
        scratch_shapes=[pltpu.VMEM((NB, R, C), bf16), pltpu.VMEM((NB, R, C), f32), pltpu.VMEM(sums.shape, f32),
                        pltpu.VMEM((3,) + images[0].shape, bf16), *[pltpu.VMEM(v.shape, f32) for v in vecs],
                        S((NB,)), S((NB,)), S((1,)), S((8,)), S((3,)), S((3,))],
        compiler_params=pltpu.CompilerParams(vmem_limit_bytes=63 * 2**20),
    )(F, sums, *images)


def pack(m, t, o, e, r):
    R, C = o.shape
    def cut(w):
        a, b = w.shape
        return w.reshape(a // R, R, b // C, C).transpose(0, 2, 1, 3).reshape(-1, R, C)
    return jnp.concatenate([cut(w) for w in (m, t, o, e, r)])


def against(left, right):
    return lax.dot_general(left, right, (((1,), (1,)), ((), ())), preferred_element_type=jnp.float32)


def weight_grad(left, right):
    return lax.dot_general(left, right, (((0,), (0,)), ((), ())), preferred_element_type=jnp.float32)


def norm_parts(v):
    c = v - jnp.mean(v, axis=-1, keepdims=True)
    inv = lax.rsqrt(jnp.mean(c * c, axis=-1, keepdims=True) + EPS)
    return c * inv, inv


def norm_back(e, xhat, inv, gain):
    t = e * gain
    return (t - jnp.mean(t, axis=-1, keepdims=True) - xhat * jnp.mean(t * xhat, axis=-1, keepdims=True)) * inv


def plain(hidden, skipped, row_mask, cotangent, merge_weight, merge_bias, first_gain, first_shift, triple_weight,
         output_weight, output_bias, second_gain, second_shift, expand_weight, expand_bias, reduce_weight, reduce_bias):
    length, D = hidden.shape[1:]
    hs = D // HEADS
    nz = lax.axis_size("seq")
    z = lax.axis_index("seq")
    c = lax.axis_index("dp") % 2
    weights = (merge_weight, triple_weight, output_weight, expand_weight, reduce_weight)
    G = lax.all_gather(pack(*weights), "seq")
    R = G.shape[2]
    merge_full = G[:, 0:2].reshape(2 * D, D)
    triple_full = G[:, 2:5].transpose(1, 0, 2, 3).reshape(3, D, D)
    output_full = G[:, 5].reshape(D, D)
    expand_full = G[:, 6:10].transpose(1, 0, 2, 3).reshape(4, D, D)
    reduce_full = G[:, 10:14].reshape(4 * D, D)
    gain_a, shift_a, gain_b, shift_b = (v.astype(f32) for v in (first_gain, first_shift, second_gain, second_shift))
    joined = jnp.concatenate([hidden[0], skipped[0]], axis=-1)
    merged = jnp.dot(joined, merge_full, preferred_element_type=f32) + merge_bias.astype(f32)
    xhat_a, inv_a = norm_parts(merged)
    normed = (xhat_a * gain_a + shift_a).astype(bf16)
    triple = jnp.einsum("ld,jde->jle", normed, triple_full, preferred_element_type=f32).astype(bf16)
    queries, key_heads, value_heads = (triple[j].reshape(length, HEADS, hs) for j in range(3))
    valid = lax.dynamic_index_in_dim(row_mask, z, 0, False)
    scores = jnp.einsum("qhd,khd->hqk", queries, key_heads, preferred_element_type=f32) * hs ** -0.5
    scores = jnp.where(valid[None, None, :] > 0, scores, NEGATIVE)
    weights_ = jnp.exp(scores - jnp.max(scores, axis=-1, keepdims=True))
    probs = weights_ / jnp.sum(weights_, axis=-1, keepdims=True)
    probs_low = probs.astype(bf16)
    attended = jnp.einsum("hqk,khd->qhd", probs_low, value_heads, preferred_element_type=f32).astype(bf16).reshape(length, D)
    middle = merged + jnp.dot(attended, output_full, preferred_element_type=f32) + output_bias.astype(f32)
    xhat_b, inv_b = norm_parts(middle)
    normed_two = (xhat_b * gain_b + shift_b).astype(bf16)
    expanded = jnp.einsum("ld,jde->jle", normed_two, expand_full, preferred_element_type=f32) + expand_bias.astype(f32).reshape(4, 1, D)
    activated, gelu_back = jax.vjp(functools.partial(jax.nn.gelu, approximate=False), expanded)
    activated = activated.astype(bf16).transpose(1, 0, 2).reshape(length, 4 * D)
    result = middle + jnp.dot(activated, reduce_full, preferred_element_type=f32) + reduce_bias.astype(f32)
    result = result.astype(bf16)
    upstream = cotangent[0]
    wide = upstream.astype(f32)
    activated_grad = jnp.einsum("le,jde->jld", upstream, reduce_full.reshape(4, D, D), preferred_element_type=f32)
    expanded_grad = gelu_back(activated_grad)[0].astype(bf16)
    e_two = jnp.einsum("jle,jde->ld", expanded_grad, expand_full, preferred_element_type=f32)
    middle_grad = wide + norm_back(e_two, xhat_b, inv_b, gain_b)
    branch_grad = middle_grad.astype(bf16)
    attended_grad = against(branch_grad, output_full).astype(bf16).reshape(length, HEADS, hs)
    prob_grad = jnp.einsum("qhd,khd->hqk", attended_grad, value_heads, preferred_element_type=f32)
    values_grad = jnp.einsum("hqk,qhd->khd", probs_low, attended_grad, preferred_element_type=f32)
    score_grad = (probs * (prob_grad - jnp.sum(probs * prob_grad, axis=-1, keepdims=True))).astype(bf16)
    queries_grad = jnp.einsum("hqk,khd->qhd", score_grad, key_heads, preferred_element_type=f32) * hs ** -0.5
    keys_grad = jnp.einsum("hqk,qhd->khd", score_grad, queries, preferred_element_type=f32) * hs ** -0.5
    triple_grad = jnp.stack([g.astype(bf16).reshape(length, D) for g in (queries_grad, keys_grad, values_grad)])
    e_one = jnp.einsum("jle,jde->ld", triple_grad, triple_full, preferred_element_type=f32)
    merged_grad = (middle_grad + norm_back(e_one, xhat_a, inv_a, gain_a)).astype(bf16)
    joined_grad = against(merged_grad, merge_full).astype(bf16)
    vectors = jnp.stack([
        jnp.sum(merged_grad.astype(f32), 0), jnp.sum(e_one * xhat_a, 0), jnp.sum(e_one, 0),
        jnp.sum(branch_grad.astype(f32), 0), jnp.sum(e_two * xhat_b, 0), jnp.sum(e_two, 0), jnp.sum(wide, 0),
    ])
    vectors = jnp.concatenate([vectors, jnp.sum(expanded_grad.astype(f32), 1), jnp.zeros((VR - 11, D), f32)])

    count = lax.axis_size("dp")
    def both(v):
        other = lax.ppermute(v, "dp", [(i, i + 1 - 2 * (i % 2)) for i in range(count)])
        return jnp.concatenate([v, other], axis=-2)
    joined2, normed2, triple2, attended2, branch2, normed_two2, expanded2, activated2, upstream2 = (
        both(v) for v in (joined, normed, triple_grad, attended, branch_grad, normed_two, expanded_grad, activated, upstream))
    def pick(v, axis, index):
        return lax.dynamic_index_in_dim(v, index, axis, False)
    def rows(left, right):
        return jnp.einsum("lsr,le->sre", left, right, preferred_element_type=f32).astype(bf16)
    def split(left):
        return left.reshape(left.shape[0], nz, -1, R)
    parts = [
        rows(pick(split(joined2), 2, c), both(merged_grad)),
        rows(split(normed2)[:, :, 0], pick(triple2, 0, c)),
        rows(split(jnp.where(c == 0, normed2, attended2))[:, :, 0], jnp.where(c == 0, triple2[2], branch2)),
        rows(split(normed_two2)[:, :, 0], pick(expanded2, 0, c)),
        rows(split(normed_two2)[:, :, 0], pick(expanded2, 0, c + 2)),
        rows(pick(split(activated2), 2, c), upstream2),
        rows(pick(split(activated2), 2, c + 2), upstream2),
    ]
    grads = jnp.stack(parts, axis=1)
    wide_grads = jnp.stack([jnp.where(c == i, grads, 0) for i in range(2)], axis=2).reshape(nz, NB, R, D)
    F = lax.psum(lax.psum_scatter(wide_grads, "seq", scatter_dimension=0, tiled=False), "dp")
    vectors = lax.psum(vectors, ("dp", "seq"))
    F = F.astype(f32)
    def columns(blocks):
        return blocks.transpose(1, 0, 2).reshape(R, -1)
    summed = (F[0:2].reshape(-1, D), columns(F[2:5]), F[5], columns(F[6:10]), F[10:14].reshape(-1, D))
    return outputs((result, joined_grad[:, :D], joined_grad[:, D:]), summed, vectors)


def outputs(images, summed, vectors):
    result, hidden_grad, skipped_grad = images
    merge, triple, output, expand, reduce = summed
    return (result[None], hidden_grad[None], skipped_grad[None], merge, vectors[0], vectors[1], vectors[2], triple, output,
            vectors[3], vectors[4], vectors[5], expand, vectors[7:11].reshape(-1), reduce, vectors[6])


def body(hidden, skipped, row_mask, cotangent, merge_weight, merge_bias, first_gain, first_shift, triple_weight,
         output_weight, output_bias, second_gain, second_shift, expand_weight, expand_bias, reduce_weight, reduce_bias):
    vectors = (merge_bias, first_gain, first_shift, output_bias, second_gain, second_shift, reduce_bias, expand_bias)
    weights = (merge_weight, triple_weight, output_weight, expand_weight, reduce_weight)
    *images, F, sums = block(hidden, skipped, cotangent, row_mask, vectors, weights, lax.axis_size("seq"))
    merge, triple, output, expand, reduce, result, hidden_grad, skipped_grad, *v = unpack(images, F, sums)
    return (result, hidden_grad, skipped_grad, merge, v[0], v[1], v[2], triple, output, v[3], v[4], v[5], expand, v[7],
            reduce, v[6])


def solution(mesh):
    rows, held, copied = P(("dp", "seq"), None, None), P("seq", None), P()
    fast = mesh.shape["dp"] == 8 and mesh.shape["seq"] == 4
    return jax.shard_map(
        body if fast else plain,
        mesh=mesh,
        in_specs=(rows, rows, P("dp", None), rows, held, copied, copied, copied, held, held, copied, copied, copied,
                  held, copied, held, copied),
        out_specs=(rows, rows, rows, held, copied, copied, copied, held, held, copied, copied, copied, held, copied,
                   held, copied),
        check_vma=False,
    )
```
